32 devices in a mesh: dp: 8 (over z, x), seq: 4 (over y, core).
Axes of the slice: x: 2, y: 2, z: 4, core: 2. Of those that a mesh axis runs over, the one named last changes fastest.
Arguments:
- block_in: bfloat16 [16, 768, 768], P('dp', 'seq'), may hold values from -6 to 6
- cotangent: bfloat16 [16, 768, 768], P('dp', 'seq'), may hold values from -6 to 6
- labels: int32 [16], P('dp'), may hold values 0 or 1
- master: float32 [2, 768, 9216], P(None, 'dp', 'seq'), may hold values from -8 to 8
- small_params: float32 [2, 9984], replicated, may hold values from -2 to 3
- row_state: float32 [2, 4, 768], P(None, None, 'dp')
- col_state: float32 [2, 9216], P(None, 'seq')
- small_state: float32 [2, 9984], replicated
Outputs:
- block_out: bfloat16 [16, 768, 768], P('dp', 'seq')
- input_grad: float32 [16, 768, 768], P('dp', 'seq')
- example_norms: float32 [16], P('dp')
- influence: float32 [16], P('dp')
- weight_grads: float32 [2, 768, 9216], P(None, 'dp', 'seq')
- fresh_row_moments: float32 [2, 4, 768], P(None, None, 'dp')
- col_stats: float32 [2, 9216], P(None, 'seq')
- new_master: float32 [2, 768, 9216], P(None, 'dp', 'seq')
- new_low: bfloat16 [2, 768, 9216], P(None, 'dp', 'seq')
- small_grads: float32 [2, 9984], replicated
- small_moments: float32 [2, 9984], replicated
- small_new: float32 [2, 9984], replicated
The draws below stay inside these ranges and needn't reach their ends.
All inputs are finite; a program needn't handle non-finite values. No bound on the sum of `labels` on one device may be relied on, other than what follows from the above.
Results may differ from the reference program's by a relative error of at most 0.022.
Values may be sent and summed in bfloat16 or wider, within the bound.
No kernel may reach another device: no remote copies, remote signals or barrier semaphores. Data moves between devices by JAX's collectives and lax.ppermute only.
A program may use at most 256 MiB of HBM per device.

```python
from functools import partial
import jax
import jax.numpy as jnp
from jax import lax

D = 768
HEADS = 12
FF = 3072
L = 768
LAYERS = 2
HEAD_DIM = 64
ROT = 16
SEQS = 16
PACK = 9216
GROUPS = 4
SLOT = 2304
SMALL = 9984


def column_kinds():
    column = jnp.arange(PACK)
    offset = column % SLOT
    group_index = column // SLOT
    cut_one = 3 * D // GROUPS
    cut_two = 4 * D // GROUPS
    cut_three = (4 * D + FF) // GROUPS
    head_part = (group_index * cut_one + offset) % (3 * HEAD_DIM) // HEAD_DIM
    inner_kind = jnp.where(head_part == 2, 1, 0)
    return jnp.where(offset < cut_one, inner_kind, jnp.where(offset < cut_two, 2, jnp.where(offset < cut_three, 3, 4)))


def draw_master(key, part):
    key = jax.random.fold_in(key, 11)
    spread_table = jnp.array([1.26 * D ** (-0.5), 6.1 * D ** (-0.5), 1.3 * D ** (-0.5), 0.7 * D ** (-0.5), FF ** (-0.5)], jnp.float32)
    spread = jnp.take(spread_table, column_kinds())
    row_place = jnp.arange(D).astype(jnp.float32) / max(D - 1, 1)
    sample = jax.random.truncated_normal(key, -4.0, 4.0, (LAYERS, D, PACK), jnp.float32)
    rising = 0.5 + row_place
    return sample * spread[None, None, :] * rising[None, :, None]


def draw_small_params(key, part):
    key = jax.random.fold_in(key, 12)
    gain_key, bias_key = jax.random.split(key)
    position = jnp.arange(SMALL)
    first_mask = position < D
    second_mask = (position >= 2 * D) & (position < 3 * D)
    unit = jax.random.uniform(gain_key, (LAYERS, SMALL), jnp.float32, 0.0, 1.0)
    first_gain = 0.5 + 0.6 * unit
    second_gain = 1.5 + 1.5 * unit
    bias_part = 0.3 * jax.random.truncated_normal(bias_key, -4.0, 4.0, (LAYERS, SMALL), jnp.float32)
    return jnp.where(first_mask[None, :], first_gain, jnp.where(second_mask[None, :], second_gain, bias_part))


def draw_row_state(key, part):
    key = jax.random.fold_in(key, 21)
    levels = jnp.array([1.4, 1.2, 1.6, 2.2], jnp.float32) * (0.75 * SEQS * L)
    row_index = jnp.arange(D).astype(jnp.float32)
    falling = 3.0 - 2.0 * row_index / max(D - 1, 1)
    factor = jnp.exp(jax.random.uniform(key, (LAYERS, 4, D), jnp.float32, -0.6931, 0.6931))
    return levels[None, :, None] * falling[None, None, :] * factor


def draw_col_state(key, part):
    key = jax.random.fold_in(key, 22)
    coeff_table = jnp.array([2.0, 0.06, 1.2, 1.6, 2.2], jnp.float32)
    coeffs = jnp.take(coeff_table, column_kinds())
    column = jnp.arange(PACK)
    falling = 3.0 - 2.0 * column.astype(jnp.float32) / (PACK - 1)
    factor = jnp.exp(jax.random.uniform(key, (LAYERS, PACK), jnp.float32, -0.6931, 0.6931))
    return 0.75 * SEQS * L * coeffs[None, :] * falling[None, :] * factor


def draw_small_state(key, part):
    key = jax.random.fold_in(key, 23)
    factor = jnp.exp(jax.random.uniform(key, (LAYERS, SMALL), jnp.float32, -0.6931, 0.6931))
    return 1.5 * SEQS * L * factor


def plant(values, rng, low, high):
    dims = values.shape
    place = [jax.random.randint(jax.random.fold_in(rng, axis), (), 0, dims[axis]) for axis in range(len(dims))]
    values = values.at[tuple(place)].set(low)
    longest = dims.index(max(dims))
    place[longest] = (place[longest] + 1) % dims[longest]
    return values.at[tuple(place)].set(high)


def block_levels(own_key, shape, cuts, smallest, top_value):
    gain, own = 1.0, jax.random.fold_in(own_key, 6)
    for dim, blocks in cuts:
        heights = jnp.exp(jax.random.uniform(jax.random.fold_in(own, dim), (blocks,), jnp.float32, smallest / len(cuts), top_value / len(cuts)))
        gain = gain * jnp.repeat(heights, shape[dim] // blocks).reshape([-1 if axis == dim else 1 for axis in range(len(shape))])
    return gain


def gaussian(stream_key, extent, width, most, cuts=(), kind=jnp.bfloat16):
    values = jax.random.normal(stream_key, extent, jnp.float32) * width
    if len(cuts) > 0:
        values = block_levels(stream_key, extent, cuts, -0.22, 0.18) * values
    return jnp.clip(values, min=-most, max=most).astype(kind)


def setup_inputs(seed: int = 0) -> dict:
    arg_keys = jax.random.split(jax.random.key(seed), 9)
    return {
        "block_in": gaussian(arg_keys[0], (SEQS, L, D), 1.0, 6.0, ((0, 8), (1, 4))),
        "cotangent": gaussian(arg_keys[1], (SEQS, L, D), 1.0, 6.0, ((0, 8), (1, 4))),
        "labels": plant((jax.random.randint(arg_keys[2], (SEQS,), 0, 4) < 1).astype(jnp.int32), jax.random.fold_in(arg_keys[2], 1), 0, 1),
        "master": draw_master(jax.random.fold_in(arg_keys[8], 71), 0),
        "small_params": draw_small_params(jax.random.fold_in(arg_keys[8], 71), 0),
        "row_state": draw_row_state(jax.random.fold_in(arg_keys[8], 71), 0),
        "col_state": draw_col_state(jax.random.fold_in(arg_keys[8], 71), 0),
        "small_state": draw_small_state(jax.random.fold_in(arg_keys[8], 71), 0),
    }


EPS_NORM = 1e-05
EPS_SQUARE = 1e-30
RATE = 0.5
DECAY = 0.5
NEG_LARGE = -1e+30
HIGH_ACCURACY = lax.Precision.HIGHEST

@jax.custom_vjp
def low(v):
    return lax.optimization_barrier(v.astype(jnp.bfloat16)).astype(jnp.float32)

@jax.custom_vjp
def low_back(v):
    return v

def low_keep(v):
    return (low(v), None)

def low_pass(kept, grad):
    return (grad,)

def back_keep(v):
    return (v, None)

def back_low(kept, grad):
    return (low(grad),)
low.defvjp(low_keep, low_pass)
low_back.defvjp(back_keep, back_low)

def matmul(left_side, right_side):
    return jnp.dot(left_side, right_side, precision=HIGH_ACCURACY)

def layer_norm(inputs, gain_vec, shift_vec):
    centred = inputs - lax.optimization_barrier(jnp.mean(inputs, axis=-1, keepdims=True))
    variance = lax.optimization_barrier(jnp.mean(centred * centred, axis=-1, keepdims=True))
    return centred * lax.rsqrt(variance + EPS_NORM) * gain_vec + shift_vec

def unpack(vector):
    return jnp.split(vector, [D, 2 * D, 3 * D, 4 * D, 7 * D, 8 * D, 8 * D + FF], axis=-1)

def group_cuts():
    return [3 * D // GROUPS, 4 * D // GROUPS, (4 * D + FF) // GROUPS]

def split_weight(packed):
    grouped = packed.reshape(D, GROUPS, SLOT)
    pieces = jnp.split(grouped, group_cuts(), axis=2)
    return [piece.reshape(D, -1) for piece in pieces]

def rotary_tables(positions):
    halfway = ROT // 2
    frequency = 10000.0 ** (-2.0 * jnp.arange(halfway, dtype=jnp.float32) / ROT)
    angles = positions.astype(jnp.float32)[:, None] * frequency[None, :]
    angles = jnp.concatenate([angles, angles], axis=-1)
    return (jnp.cos(angles), jnp.sin(angles))

def rotate(values, cosine_table, sine_table):
    turned = values[..., :ROT]
    passed = values[..., ROT:]
    front_half = turned[..., :ROT // 2]
    back_half = turned[..., ROT // 2:]
    swapped = jnp.concatenate([-back_half, front_half], axis=-1)
    turned = turned * cosine_table[:, None, :] + swapped * sine_table[:, None, :]
    return jnp.concatenate([turned, passed], axis=-1)

def layer(inputs, weight, small_layer, cosine_table, sine_table, causal):
    gain_one, shift_one, gain_two, shift_two, bias_qkv, bias_out, bias_up, bias_down = unpack(small_layer)
    w_qkv, w_out, w_up, w_down = split_weight(weight)
    length = inputs.shape[0]
    normed_one = low(layer_norm(inputs, gain_one, shift_one))
    normed_two = low(layer_norm(inputs, gain_two, shift_two))
    joined_proj = low_back(matmul(normed_one, w_qkv) + bias_qkv)
    shaped = joined_proj.reshape(length, HEADS, 3, HEAD_DIM)
    queries = low(rotate(shaped[:, :, 0], cosine_table, sine_table))
    keys_rot = low(rotate(shaped[:, :, 1], cosine_table, sine_table))
    values = low(shaped[:, :, 2])
    scores = low_back(jnp.einsum('qhd,khd->hqk', queries, keys_rot, precision=HIGH_ACCURACY) * HEAD_DIM ** (-0.5))
    scores = jnp.where(causal[None], scores, NEG_LARGE)
    largest = lax.optimization_barrier(jnp.max(scores, axis=-1, keepdims=True))
    exponent = jnp.exp(scores - largest)
    attention = low(exponent / lax.optimization_barrier(jnp.sum(exponent, axis=-1, keepdims=True)))
    mixed_heads = jnp.einsum('hqk,khd->qhd', attention, values, precision=HIGH_ACCURACY).reshape(length, D)
    attended = low(low_back(mixed_heads))
    branch_attn = low_back(matmul(attended, w_out) + bias_out)
    hidden_pre = low_back(matmul(normed_two, w_up) + bias_up)
    hidden = low(jax.nn.gelu(hidden_pre, approximate=False))
    branch_mlp = low_back(matmul(hidden, w_down.T) + bias_down)
    return inputs + branch_attn + branch_mlp

def sequence_pass(weight_train, weight_query, small_params, carried):
    inputs, delta_seq, label_seq = carried
    positions = jnp.arange(L)
    cosine_table, sine_table = rotary_tables(positions)
    causal = positions[None, :] <= positions[:, None]
    weight = low(jnp.where(label_seq > 0, weight_query, weight_train))
    stream = inputs
    for layer_index in range(LAYERS):
        stream = layer(stream, weight[layer_index], small_params[layer_index] + delta_seq[layer_index], cosine_table, sine_table, causal)
    return stream

def reference(block_in, cotangent, labels, master, small_params, row_state, col_state, small_state):
    inputs = block_in.astype(jnp.float32)
    deltas = jnp.zeros((SEQS, LAYERS, SMALL), jnp.float32)

    def forward(weight_train, weight_query, delta_all, inputs_all):
        step_fn = jax.checkpoint(partial(sequence_pass, weight_train, weight_query, small_params))
        return lax.map(step_fn, (inputs_all, delta_all, labels))
    outputs, pullback = jax.vjp(forward, master, master, deltas, inputs)
    grad_train, grad_query, example_grads, input_grad = pullback(cotangent.astype(jnp.float32))
    train_flag = (labels == 0).astype(jnp.float32)
    query_flag = 1.0 - train_flag
    flat_grads = example_grads.reshape(SEQS, LAYERS * SMALL)
    small_flat = jnp.dot(train_flag, flat_grads, precision=HIGH_ACCURACY)
    query_total = jnp.dot(query_flag, flat_grads, precision=HIGH_ACCURACY)
    example_norms = lax.optimization_barrier(jnp.sum(flat_grads * flat_grads, axis=1)) / (LAYERS * SMALL * L)
    influence = jnp.dot(flat_grads, query_total, precision=HIGH_ACCURACY) / jnp.sqrt(L * LAYERS * SMALL * (jnp.mean(query_total * query_total) + 1e-06))
    squared_entries = grad_train * grad_train + EPS_SQUARE
    col_stats = DECAY * col_state + (1.0 - DECAY) * lax.optimization_barrier(jnp.mean(squared_entries, axis=1))
    squared_groups = squared_entries.reshape(LAYERS, D, GROUPS, SLOT)
    grad_groups = grad_train.reshape(LAYERS, D, GROUPS, SLOT)
    master_groups = master.reshape(LAYERS, D, GROUPS, SLOT)
    col_groups = col_stats.reshape(LAYERS, GROUPS, SLOT)
    edges = [0] + group_cuts() + [SLOT]
    row_list = []
    master_list = []
    for matrix in range(4):
        col_begin = edges[matrix]
        col_end = edges[matrix + 1]
        block_sq = squared_groups[:, :, :, col_begin:col_end]
        row_new = DECAY * row_state[:, matrix] + (1.0 - DECAY) * lax.optimization_barrier(jnp.mean(block_sq, axis=(2, 3)))
        row_mean = lax.optimization_barrier(jnp.mean(row_new, axis=1))
        second = row_new[:, :, None, None] * col_groups[:, None, :, col_begin:col_end] / row_mean[:, None, None, None]
        update = grad_groups[:, :, :, col_begin:col_end] * lax.rsqrt(second)
        update_rms = jnp.sqrt(lax.optimization_barrier(jnp.mean(update * update, axis=(1, 2, 3))))
        clipped = update / jnp.maximum(1.0, update_rms)[:, None, None, None]
        old_block = master_groups[:, :, :, col_begin:col_end]
        weight_rms = jnp.sqrt(lax.optimization_barrier(jnp.mean(old_block * old_block, axis=(1, 2, 3))))
        master_list.append(old_block - RATE * weight_rms[:, None, None, None] * clipped)
        row_list.append(row_new)
    fresh_row_moments = jnp.stack(row_list, axis=1)
    new_master = jnp.concatenate(master_list, axis=3).reshape(LAYERS, D, PACK)
    small_grads = small_flat.reshape(LAYERS, SMALL)
    small_moments = DECAY * small_state + (1.0 - DECAY) * (small_grads * small_grads + EPS_SQUARE)
    small_update = small_grads * lax.rsqrt(small_moments)
    new_pieces = []
    for update_piece, param_piece in zip(unpack(small_update), unpack(small_params)):
        update_rms = jnp.sqrt(lax.optimization_barrier(jnp.mean(update_piece * update_piece, axis=-1, keepdims=True)))
        param_rms = jnp.sqrt(lax.optimization_barrier(jnp.mean(param_piece * param_piece, axis=-1, keepdims=True)))
        new_pieces.append(param_piece - RATE * param_rms * (update_piece / jnp.maximum(1.0, update_rms)))
    small_new = jnp.concatenate(new_pieces, axis=-1)
    return (outputs.astype(jnp.bfloat16), input_grad, example_norms, influence, grad_train, fresh_row_moments, col_stats, new_master, new_master.astype(jnp.bfloat16), small_grads, small_moments, small_new)
```

```python
import functools

import jax
import jax.numpy as jnp
from jax import lax
from jax.experimental import pallas as pl
from jax.experimental.pallas import tpu as pltpu
from jax.sharding import PartitionSpec as P

D = 768
HEADS = 12
FF = 3072
LAYERS = 2
HEAD_DIM = 64
ROT = 16
SMALL = 9984

EPS_NORM = 1e-05
EPS_SQUARE = 1e-30
RATE = 0.5
DECAY = 0.5
NEG_LARGE = -1e30
SCORE_SCALE = HEAD_DIM ** (-0.5)
CONTRACT_LAST = (((1,), (1,)), ((), ()))
CONTRACT_FIRST = (((0,), (0,)), ((), ()))
VMEM_BYTES = 56 * 1024 * 1024
BF16 = jnp.bfloat16
F32 = jnp.float32


def unpack(vector):
    return jnp.split(vector, [D, 2 * D, 3 * D, 4 * D, 7 * D, 8 * D, 8 * D + FF], axis=-1)


def apply_layer_norm(inputs):
    centred = inputs - jnp.mean(inputs, axis=-1, keepdims=True)
    variance = jnp.mean(centred * centred, axis=-1, keepdims=True)
    inverse = lax.rsqrt(variance + EPS_NORM)
    return (centred * inverse, inverse)


def norm_back(grad_scaled, scaled, inverse):
    mean_grad = jnp.mean(grad_scaled, axis=-1, keepdims=True)
    mean_cross = jnp.mean(grad_scaled * scaled, axis=-1, keepdims=True)
    return (grad_scaled - mean_grad - scaled * mean_cross) * inverse


def rotary_tables(length):
    halfway = ROT // 2
    frequency = 10000.0 ** (-2.0 * jnp.arange(halfway, dtype=F32) / ROT)
    angles = jnp.arange(length).astype(F32)[:, None] * frequency[None, :]
    cosine, sine = jnp.cos(angles), jnp.sin(angles)
    rest = jnp.ones((length, HEAD_DIM - ROT), F32)
    none = jnp.zeros((length, halfway), F32)
    keep = jnp.concatenate([cosine, cosine, rest], axis=1)
    ahead = jnp.concatenate([-sine, none, 0.0 * rest], axis=1)
    behind = jnp.concatenate([none, sine, 0.0 * rest], axis=1)
    return tuple(jnp.concatenate([table, table], axis=1) for table in (keep, ahead, behind))


def swap(values, axis, bits):
    size = lax.axis_size(axis)
    return lax.ppermute(values, axis, [(i, i ^ bits) for i in range(size)])


def sum_pairwise(values, axis, wire=F32):
    bits = 1
    while bits < lax.axis_size(axis):
        sent = values.astype(wire)
        values = sent.astype(F32) + swap(sent, axis, bits).astype(F32)
        bits *= 2
    return values


def gather_tokens(own):
    far = swap(own, "seq", 2)
    near = swap(own, "seq", 1)
    return (own, near, far, swap(far, "seq", 1))


def scatter_tokens(keep, send):
    total = keep + swap(send, "seq", 1).astype(F32)
    return total[0] + swap(total[1].astype(BF16), "seq", 2).astype(F32)


def gather_rows(rows):
    size = lax.axis_size("dp")
    if size != 8:
        return [lax.all_gather(rows, "dp", axis=0, tiled=True)]
    even = [rows] + [swap(rows, "dp", 2 * k) for k in (1, 2, 3)]
    pieces = []
    for piece in even:
        pieces += [piece, swap(piece, "dp", 1)]
    return pieces


def scatter_rows(values):
    size = lax.axis_size("dp")
    if size != 8:
        return lax.psum_scatter(values.astype(BF16), "dp", scatter_dimension=0, tiled=True).astype(
            F32
        )
    own = lax.axis_index("dp")
    x_bit, z_place = own % 2, own // 2
    blocks = values.reshape(4, 2, D // 8, -1)
    keep = lax.dynamic_index_in_dim(blocks, x_bit, 1, keepdims=False)
    send = lax.dynamic_index_in_dim(blocks, 1 - x_bit, 1, keepdims=False)
    summed = keep.astype(F32) + swap(send.astype(BF16), "dp", 1).astype(F32)
    total = lax.dynamic_index_in_dim(summed, z_place, 0, keepdims=False)
    for k in (1, 2, 3):
        part = lax.dynamic_index_in_dim(summed, z_place ^ k, 0, keepdims=False)
        total = total + swap(part.astype(BF16), "dp", 2 * k).astype(F32)
    return total


def in_place_order(pieces, index):
    stacked = list(pieces)
    bits = 1
    while bits < len(stacked):
        flag = (index // bits) % 2 == 1
        stacked = [
            jnp.where(flag, stacked[i ^ bits], stacked[i]) for i in range(len(stacked))
        ]
        bits *= 2
    return stacked


def exchange_blocks(blocks, index):
    size = lax.axis_size("seq")
    received = []
    for k in range(size):
        block = lax.dynamic_index_in_dim(blocks, index ^ k, 0, keepdims=False)
        received.append(block if k == 0 else swap(block, "seq", k))
    return in_place_order(received, index)


def heads_together(values):
    heads = values.shape[-1] // (3 * HEAD_DIM)
    lead = values.shape[:-1]
    by_head = values.reshape(*lead, heads, 3 * HEAD_DIM)
    return jnp.concatenate(
        [
            by_head[..., : 2 * HEAD_DIM].reshape(*lead, heads * 2 * HEAD_DIM),
            by_head[..., 2 * HEAD_DIM :].reshape(*lead, heads * HEAD_DIM),
        ],
        axis=-1,
    )


def heads_apart(values):
    heads = values.shape[-1] // (3 * HEAD_DIM)
    lead = values.shape[:-1]
    pairs, last = jnp.split(values, [heads * 2 * HEAD_DIM], axis=-1)
    return jnp.concatenate(
        [
            pairs.reshape(*lead, heads, 2 * HEAD_DIM),
            last.reshape(*lead, heads, HEAD_DIM),
        ],
        axis=-1,
    ).reshape(values.shape)


def weight_copies(dp_place, pieces, whole, sems, base):
    rows = pieces[0].shape[0]
    copies = []
    for k, piece in enumerate(pieces):
        offset = 0 if len(pieces) == 1 else pl.multiple_of((k ^ dp_place) * rows, 16)
        copies.append(
            pltpu.make_async_copy(piece, whole.at[pl.ds(offset, rows), :], sems.at[base + k])
        )
    return copies


def place_tokens(dst, own, near, far, far_near, core_bit, y_here, chunk):
    for here, left, right in ((0, own, near), (1, far, far_near)):
        for bit in (0, 1):

            @pl.when((y_here == here) & (core_bit == bit))
            def _():
                first, second = (left, right) if bit == 0 else (right, left)
                dst[0, :chunk] = first[0]
                dst[0, chunk:] = second[0]


def spread_tokens(value, keep, send, core_bit, y_here, chunk):
    for bit in (0, 1):

        @pl.when(core_bit == bit)
        def _():
            mine = value[:chunk] if bit == 0 else value[chunk:]
            other = value[chunk:] if bit == 0 else value[:chunk]
            keep[pl.ds(y_here, 1), 0] = mine[None]
            send[pl.ds(y_here, 1), 0] = other.astype(send.dtype)[None]


def gelu_and_slope(v):
    magnitude = jnp.abs(v) * 0.7071067811865476
    t = 1.0 / (1.0 + 0.3275911 * magnitude)
    falling = jnp.exp(-0.5 * v * v)
    poly = t * (
        0.254829592
        + t * (-0.284496736 + t * (1.421413741 + t * (-1.453152027 + t * 1.061405429)))
    )
    tail = 0.5 * poly * falling
    cdf = jnp.where(v >= 0.0, 1.0 - tail, tail)
    return v * cdf, cdf + v * falling * 0.3989422804014327


def forward_kernel(n_pieces, place, *refs):
    (own, near, far, far_near, vec, keep_tab, ahead_tab, behind_tab, w_out) = refs[:9]
    pieces_a = refs[9 : 9 + n_pieces]
    pieces_b = refs[9 + n_pieces : 9 + 2 * n_pieces]
    (keep, send, xhat, qk, val, att, lse, hid, slope) = refs[9 + 2 * n_pieces : 18 + 2 * n_pieces]
    (whole_a, whole_b, k_all, v_all, sems) = refs[18 + 2 * n_pieces :]
    core_bit, y_bit, dp_place = place[0], place[1], place[2]
    step = pl.program_id(1)
    begin = (pl.program_id(0) == 0) & (step == 0)
    copies_a = weight_copies(dp_place, pieces_a, whole_a, sems, 0)
    copies_b = weight_copies(dp_place, pieces_b, whole_b, sems, n_pieces)

    @pl.when(begin)
    def _():
        for copy in copies_a + copies_b:
            copy.start()

    chunk = own.shape[1]
    block = 2 * chunk
    y_here = step ^ y_bit
    place_tokens(xhat, own, near, far, far_near, core_bit, y_here, chunk)
    scaled = xhat[0].astype(F32)
    normed_one = (scaled * vec[0:1] + vec[1:2]).astype(BF16)
    normed_two = (scaled * vec[2:3] + vec[3:4]).astype(BF16)

    @pl.when(begin)
    def _():
        for copy in copies_a:
            copy.wait()

    heads = val.shape[-1] // HEAD_DIM
    wide = 3 * heads * HEAD_DIM
    joined = jnp.dot(normed_one, whole_a[:, :wide], preferred_element_type=F32) + vec[5:6, :wide]
    for h in range(heads):
        pair = joined[:, 2 * HEAD_DIM * h : 2 * HEAD_DIM * (h + 1)]
        turned = (
            pair * keep_tab[...]
            + pltpu.roll(pair, 2 * HEAD_DIM - ROT // 2, 1) * ahead_tab[...]
            + pltpu.roll(pair, ROT // 2, 1) * behind_tab[...]
        )
        qk[0, :, 2 * HEAD_DIM * h : 2 * HEAD_DIM * (h + 1)] = turned.astype(BF16)
        k_all[h, pl.ds(step * block, block)] = turned[:, HEAD_DIM:].astype(BF16)
        first = 2 * HEAD_DIM * heads + HEAD_DIM * h
        v_all[h, pl.ds(step * block, block)] = joined[:, first : first + HEAD_DIM].astype(BF16)
    val[0] = joined[:, 2 * HEAD_DIM * heads :].astype(BF16)
    row = lax.broadcasted_iota(jnp.int32, (block, block), 0)
    column = lax.broadcasted_iota(jnp.int32, (block, block), 1)
    lane = lax.broadcasted_iota(jnp.int32, (block, 128), 1)
    for here in range(2):

        @pl.when(step == here)
        def _():
            log_sums = jnp.zeros((block, 128), F32)
            for h in range(heads):
                query = qk[0, :, 2 * HEAD_DIM * h : 2 * HEAD_DIM * h + HEAD_DIM] * jnp.asarray(
                    SCORE_SCALE, BF16
                )
                scores = []
                for j in range(here + 1):
                    part = lax.dot_general(
                        query,
                        k_all[h, block * j : block * (j + 1)],
                        CONTRACT_LAST,
                        preferred_element_type=F32,
                    )
                    if j == here:
                        part = jnp.where(column <= row, part, NEG_LARGE)
                    scores.append(part)
                largest = functools.reduce(
                    jnp.maximum, [jnp.max(part, axis=-1, keepdims=True) for part in scores]
                )
                total = 0.0
                mixed = 0.0
                for j, part in enumerate(scores):
                    exponent = jnp.exp(part - largest)
                    total = total + jnp.sum(exponent, axis=-1, keepdims=True)
                    mixed = mixed + jnp.dot(
                        exponent.astype(BF16),
                        v_all[h, block * j : block * (j + 1)],
                        preferred_element_type=F32,
                    )
                att[0, :, HEAD_DIM * h : HEAD_DIM * (h + 1)] = (mixed / total).astype(BF16)
                log_sums = jnp.where(lane == h, largest + jnp.log(total), log_sums)
            lse[0] = log_sums.T[:8]

    @pl.when(begin)
    def _():
        for copy in copies_b:
            copy.wait()

    quarter = hid.shape[-1]
    hidden_pre = (
        jnp.dot(normed_two, whole_b[:, :quarter], preferred_element_type=F32) + vec[4:5, :quarter]
    )
    hidden, gradient = gelu_and_slope(hidden_pre)
    hid[0] = hidden.astype(BF16)
    slope[0] = gradient
    partial = jnp.dot(att[0], w_out[...], preferred_element_type=F32) + lax.dot_general(
        hid[0], whole_b[:, quarter:], CONTRACT_LAST, preferred_element_type=F32
    )
    spread_tokens(partial, keep, send, core_bit, y_here, chunk)


def backward_kernel(n_pieces, place, *refs):
    (own, near, far, far_near, vec, keep_tab, ahead_tab, behind_tab, w_out) = refs[:9]
    pieces_a = refs[9 : 9 + n_pieces]
    pieces_b = refs[9 + n_pieces : 9 + 2 * n_pieces]
    (xhat, qk, val, lse, slope) = refs[9 + 2 * n_pieces : 14 + 2 * n_pieces]
    (keep, send, grad, grad_pre, grad_joined, sums) = refs[
        14 + 2 * n_pieces : 20 + 2 * n_pieces
    ]
    (whole_a, whole_b, dk_all, dv_all, dq_all, sems) = refs[20 + 2 * n_pieces :]
    core_bit, y_bit, dp_place = place[0], place[1], place[2]
    step = 1 - pl.program_id(1)
    begin = (pl.program_id(0) == 0) & (step == 1)
    copies_a = weight_copies(dp_place, pieces_a, whole_a, sems, 0)
    copies_b = weight_copies(dp_place, pieces_b, whole_b, sems, n_pieces)

    @pl.when(begin)
    def _():
        for copy in copies_a + copies_b:
            copy.start()

    chunk = own.shape[1]
    block = 2 * chunk
    y_here = step ^ y_bit
    place_tokens(grad, own, near, far, far_near, core_bit, y_here, chunk)
    low_grad = grad[0]

    @pl.when(begin)
    def _():
        for copy in copies_a + copies_b:
            copy.wait()

    quarter = slope.shape[-1]
    heads = val.shape[-1] // HEAD_DIM
    wide = 3 * heads * HEAD_DIM
    grad_hidden = jnp.dot(low_grad, whole_b[:, quarter:], preferred_element_type=F32)
    grad_pre[0] = (grad_hidden * slope[0]).astype(BF16)
    grad_two = lax.dot_general(
        grad_pre[0], whole_b[:, :quarter], CONTRACT_LAST, preferred_element_type=F32
    )
    grad_att = lax.dot_general(
        low_grad, w_out[...], CONTRACT_LAST, preferred_element_type=F32
    ).astype(BF16)
    row = lax.broadcasted_iota(jnp.int32, (block, block), 0)
    column = lax.broadcasted_iota(jnp.int32, (block, block), 1)
    for here in range(2):

        @pl.when(step == here)
        def _():
            for h in range(heads):
                at_q = 2 * HEAD_DIM * h
                query = qk[0, block * here : block * (here + 1), at_q : at_q + HEAD_DIM]
                query = query * jnp.asarray(SCORE_SCALE, BF16)
                near_grad = grad_att[:, HEAD_DIM * h : HEAD_DIM * (h + 1)]
                log_row = lse[0, h : h + 1]
                probs, grad_probs, keys = [], [], []
                delta = 0.0
                for j in range(here + 1):
                    key = qk[0, block * j : block * (j + 1), at_q + HEAD_DIM : at_q + 2 * HEAD_DIM]
                    value = val[0, block * j : block * (j + 1), HEAD_DIM * h : HEAD_DIM * (h + 1)]
                    scores = lax.dot_general(
                        key, query, CONTRACT_LAST, preferred_element_type=F32
                    )
                    prob = jnp.exp(scores - log_row)
                    if j == here:
                        prob = jnp.where(row <= column, prob, 0.0)
                    grad_prob = lax.dot_general(
                        value, near_grad, CONTRACT_LAST, preferred_element_type=F32
                    )
                    delta = delta + jnp.sum(prob * grad_prob, axis=0, keepdims=True)
                    probs.append(prob)
                    grad_probs.append(grad_prob)
                    keys.append(key)
                dq = 0.0
                for j in range(here + 1):
                    grad_score = (probs[j] * (grad_probs[j] - delta)).astype(BF16)
                    dk = jnp.dot(grad_score, query, preferred_element_type=F32)
                    dv = jnp.dot(probs[j].astype(BF16), near_grad, preferred_element_type=F32)
                    if here == 1:
                        dk_all[h, block * j : block * (j + 1)] = dk
                        dv_all[h, block * j : block * (j + 1)] = dv
                    else:
                        dk_all[h, block * j : block * (j + 1)] += dk
                        dv_all[h, block * j : block * (j + 1)] += dv
                    dq = dq + lax.dot_general(
                        grad_score, keys[j], CONTRACT_FIRST, preferred_element_type=F32
                    )
                dq_all[h] = dq * SCORE_SCALE

    for h in range(heads):
        pair = jnp.concatenate([dq_all[h], dk_all[h, pl.ds(step * block, block)]], axis=1)
        turned = (
            pair * keep_tab[...]
            - pltpu.roll(pair, 2 * HEAD_DIM - ROT // 2, 1) * ahead_tab[...]
            - pltpu.roll(pair, ROT // 2, 1) * behind_tab[...]
        )
        grad_joined[0, :, 2 * HEAD_DIM * h : 2 * HEAD_DIM * (h + 1)] = turned.astype(BF16)
        first = 2 * HEAD_DIM * heads + HEAD_DIM * h
        grad_joined[0, :, first : first + HEAD_DIM] = dv_all[
            h, pl.ds(step * block, block)
        ].astype(BF16)
    grad_one = lax.dot_general(
        grad_joined[0], whole_a[:, :wide], CONTRACT_LAST, preferred_element_type=F32
    )
    spread_tokens(
        grad_one * vec[0:1] + grad_two * vec[2:3], keep, send, core_bit, y_here, chunk
    )
    scaled = xhat[0].astype(F32)

    @pl.when(step == 1)
    def _():
        sums[...] = jnp.zeros_like(sums)

    def add_up(place_row, values):
        width = values.shape[-1]
        sums[0, place_row : place_row + 1, :width] += jnp.sum(
            values.astype(F32), axis=0, keepdims=True
        )

    add_up(0, grad_one * scaled)
    add_up(1, grad_one)
    add_up(2, grad_two * scaled)
    add_up(3, grad_two)
    add_up(4, grad_pre[0])
    add_up(5, low_grad)
    add_up(6, grad_joined[0])


def common_specs(count, chunk, quarter, heads, block_of):
    tokens = pl.BlockSpec((1, chunk, D), lambda s, t, place: (s, 0, 0))
    table = pl.BlockSpec((2 * chunk, 2 * HEAD_DIM), lambda s, t, place: (block_of(t), 0))
    return [
        tokens,
        tokens,
        tokens,
        tokens,
        pl.BlockSpec((8, D), lambda s, t, place: (0, 0)),
        table,
        table,
        table,
        pl.BlockSpec((heads * HEAD_DIM, D), lambda s, t, place: (0, 0)),
    ] + [pl.BlockSpec(memory_space=pl.ANY)] * (2 * count)


def block_spec(rows, width, block_of):
    return pl.BlockSpec((1, rows, width), lambda s, t, place: (s, block_of(t), 0))


def run_forward(place, chunks, vec, tables, w_out, pieces_a, pieces_b):
    sequences, chunk, _ = chunks[0].shape
    length = 4 * chunk
    count = len(pieces_a)
    heads = w_out.shape[0] // HEAD_DIM
    quarter = pieces_b[0].shape[1] // 2
    half = 2 * chunk

    def same(t):
        return t

    spread = pl.BlockSpec((2, 1, chunk, D), lambda s, t, place: (0, s, 0, 0))
    widths = [
        (D, BF16),
        (2 * heads * HEAD_DIM, BF16),
        (heads * HEAD_DIM, BF16),
        (heads * HEAD_DIM, BF16),
    ]
    out_shape = [
        jax.ShapeDtypeStruct((2, sequences, chunk, D), F32),
        jax.ShapeDtypeStruct((2, sequences, chunk, D), BF16),
        *[jax.ShapeDtypeStruct((sequences, length, width), kind) for width, kind in widths],
        jax.ShapeDtypeStruct((sequences, 8, length), F32),
        jax.ShapeDtypeStruct((sequences, length, quarter), BF16),
        jax.ShapeDtypeStruct((sequences, length, quarter), F32),
    ]
    out_specs = [
        spread,
        spread,
        *[block_spec(half, width, same) for width, _ in widths],
        pl.BlockSpec((1, 8, half), lambda s, t, place: (s, 0, t)),
        block_spec(half, quarter, same),
        block_spec(half, quarter, same),
    ]
    return pl.pallas_call(
        functools.partial(forward_kernel, count),
        grid_spec=pltpu.PrefetchScalarGridSpec(
            num_scalar_prefetch=1,
            grid=(sequences, 2),
            in_specs=common_specs(count, chunk, quarter, heads, same),
            out_specs=out_specs,
            scratch_shapes=[
                pltpu.VMEM((D, pieces_a[0].shape[1]), BF16),
                pltpu.VMEM((D, pieces_b[0].shape[1]), BF16),
                pltpu.VMEM((heads, length, HEAD_DIM), BF16),
                pltpu.VMEM((heads, length, HEAD_DIM), BF16),
                pltpu.SemaphoreType.DMA((2 * count,)),
            ],
        ),
        out_shape=out_shape,
        compiler_params=pltpu.CompilerParams(vmem_limit_bytes=VMEM_BYTES),
        cost_estimate=pl.CostEstimate(
            flops=8 * 10**9, bytes_accessed=2 * 10**7, transcendentals=10**7
        ),
        name="layer_forward",
    )(place, *chunks, vec, *tables, w_out, *pieces_a, *pieces_b)


def run_backward(place, chunks, vec, tables, w_out, pieces_a, pieces_b, saved):
    xhat, qk, val, lse, slope = saved
    sequences, chunk, _ = chunks[0].shape
    length = 4 * chunk
    count = len(pieces_a)
    heads = w_out.shape[0] // HEAD_DIM
    quarter = pieces_b[0].shape[1] // 2
    wide = 3 * heads * HEAD_DIM
    half = 2 * chunk

    def turned(t):
        return 1 - t

    spread = pl.BlockSpec((2, 1, chunk, D), lambda s, t, place: (0, s, 0, 0))
    return pl.pallas_call(
        functools.partial(backward_kernel, count),
        grid_spec=pltpu.PrefetchScalarGridSpec(
            num_scalar_prefetch=1,
            grid=(sequences, 2),
            in_specs=common_specs(count, chunk, quarter, heads, turned)
            + [
                block_spec(half, D, turned),
                pl.BlockSpec((1, length, qk.shape[-1]), lambda s, t, place: (s, 0, 0)),
                pl.BlockSpec((1, length, val.shape[-1]), lambda s, t, place: (s, 0, 0)),
                pl.BlockSpec((1, 8, half), lambda s, t, place: (s, 0, 1 - t)),
                block_spec(half, quarter, turned),
            ],
            out_specs=[
                spread,
                spread,
                block_spec(half, D, turned),
                block_spec(half, quarter, turned),
                block_spec(half, wide, turned),
                pl.BlockSpec((1, 8, D), lambda s, t, place: (s, 0, 0)),
            ],
            scratch_shapes=[
                pltpu.VMEM((D, pieces_a[0].shape[1]), BF16),
                pltpu.VMEM((D, pieces_b[0].shape[1]), BF16),
                pltpu.VMEM((heads, length, HEAD_DIM), F32),
                pltpu.VMEM((heads, length, HEAD_DIM), F32),
                pltpu.VMEM((heads, half, HEAD_DIM), F32),
                pltpu.SemaphoreType.DMA((2 * count,)),
            ],
        ),
        out_shape=[
            jax.ShapeDtypeStruct((2, sequences, chunk, D), F32),
            jax.ShapeDtypeStruct((2, sequences, chunk, D), BF16),
            jax.ShapeDtypeStruct((sequences, length, D), BF16),
            jax.ShapeDtypeStruct((sequences, length, quarter), BF16),
            jax.ShapeDtypeStruct((sequences, length, wide), BF16),
            jax.ShapeDtypeStruct((sequences, 8, D), F32),
        ],
        compiler_params=pltpu.CompilerParams(vmem_limit_bytes=VMEM_BYTES),
        cost_estimate=pl.CostEstimate(
            flops=16 * 10**9, bytes_accessed=3 * 10**7, transcendentals=10**7
        ),
        name="layer_backward",
    )(place, *chunks, vec, *tables, w_out, *pieces_a, *pieces_b, *saved)


def out_rows(pieces_a, wide, dp_place, seq_place):
    columns = [piece[:, wide:] for piece in pieces_a]
    stacked = jnp.concatenate(
        in_place_order(columns, dp_place) if len(columns) > 1 else columns, axis=0
    )
    size = lax.axis_size("seq")
    blocks = stacked.reshape(size, D // size, -1)
    return jnp.concatenate(exchange_blocks(blocks, seq_place), axis=1)


def on_device(block_in, cotangent, labels, master, small_params, row_state, col_state, small_state):
    sequences, chunk = block_in.shape[:2]
    group_count = lax.axis_size("seq")
    seq_place, dp_place = lax.axis_index("seq"), lax.axis_index("dp")
    place = jnp.stack([seq_place % 2, seq_place // 2, dp_place]).astype(jnp.int32)
    length = chunk * group_count
    train_flag = (labels == 0).astype(F32)
    query_flag = 1.0 - train_flag
    qkv_wide, out_wide, quarter = 3 * D // group_count, D // group_count, FF // group_count
    cuts = [0, qkv_wide, qkv_wide + out_wide, qkv_wide + out_wide + quarter, master.shape[2]]
    tables = rotary_tables(length)

    low = master.astype(BF16)
    weights, vectors, params = [], [], []
    for i in range(LAYERS):
        piece_a = jnp.concatenate(
            [heads_together(low[i, :, : cuts[1]]), low[i, :, cuts[1] : cuts[2]]], axis=1
        )
        pieces_a = gather_rows(piece_a)
        pieces_b = gather_rows(low[i, :, cuts[2] :])
        weights.append((out_rows(pieces_a, qkv_wide, dp_place, seq_place), pieces_a, pieces_b))
        param = unpack(small_params[i])
        params.append(param)
        bias_qkv = heads_together(
            lax.dynamic_slice_in_dim(param[4], seq_place * qkv_wide, qkv_wide)
        )
        bias_up = lax.dynamic_slice_in_dim(param[6], seq_place * quarter, quarter)
        vectors.append(
            jnp.stack(
                [
                    *param[:4],
                    jnp.pad(bias_up, (0, D - quarter)),
                    jnp.pad(bias_qkv, (0, D - qkv_wide)),
                    jnp.zeros((D,), F32),
                    jnp.zeros((D,), F32),
                ]
            )
        )

    stream = block_in.astype(F32)
    norms, saved_all = [], []
    for i in range(LAYERS):
        scaled, inverse = apply_layer_norm(stream)
        norms.append((scaled, inverse))
        chunks = gather_tokens(scaled.astype(BF16))
        keep, send, *saved = run_forward(place, chunks, vectors[i], tables, *weights[i])
        saved_all.append(saved)
        stream = (
            stream + scatter_tokens(keep, send) + (params[i][5] + params[i][7])
        )
    block_out = stream.astype(BF16)

    grad_stream = cotangent.astype(F32)
    row_flag = train_flag.astype(BF16)[:, None, None]
    example_parts, grad_list = [None] * LAYERS, [None] * LAYERS
    for i in reversed(range(LAYERS)):
        xhat, qk, val, att, lse, hid, slope = saved_all[i]
        chunks = gather_tokens(grad_stream.astype(BF16))
        keep, send, grad_low, grad_pre, grad_joined, sums = run_backward(
            place, chunks, vectors[i], tables, *weights[i], (xhat, qk, val, lse, slope)
        )
        grad_scaled = scatter_tokens(keep, send)
        grad_stream = grad_stream + norm_back(grad_scaled, *norms[i])
        wide_scaled = xhat.astype(F32)
        normed_one = (wide_scaled * params[i][0] + params[i][1]).astype(BF16)
        normed_two = (wide_scaled * params[i][2] + params[i][3]).astype(BF16)

        def tokens(values):
            return values.reshape(sequences * length, values.shape[-1])

        def outer(left, right):
            return lax.dot_general(
                tokens(left), tokens(right), CONTRACT_FIRST, preferred_element_type=F32
            )

        kept = grad_low * row_flag
        grad_up = outer(normed_two, grad_pre * row_flag)
        grad_down = outer(kept, hid)
        grad_out = outer(att, kept).astype(BF16)
        blocks = grad_out.reshape(out_wide, group_count, out_wide).transpose(1, 0, 2)
        grad_out = jnp.concatenate(exchange_blocks(blocks, seq_place), axis=0)
        grad_qkv = outer(normed_one, grad_joined * row_flag)
        part_b = scatter_rows(jnp.concatenate([grad_up, grad_down], axis=1))
        part_a = scatter_rows(jnp.concatenate([grad_qkv, grad_out.astype(F32)], axis=1))
        grad_list[i] = jnp.concatenate(
            [heads_apart(part_a[:, :qkv_wide]), part_a[:, qkv_wide:], part_b], axis=1
        )
        only_one = jnp.where(seq_place == 0, 1.0, 0.0)
        grad_sum = sums[:, 5] * only_one

        def spread(values, width):
            return lax.dynamic_update_slice(
                jnp.zeros((sequences, group_count * width), F32), values, (0, seq_place * width)
            )

        example_parts[i] = jnp.concatenate(
            [
                sums[:, 0],
                sums[:, 1],
                sums[:, 2],
                sums[:, 3],
                spread(heads_apart(sums[:, 6, :qkv_wide]), qkv_wide),
                grad_sum,
                spread(sums[:, 4, :quarter], quarter),
                grad_sum,
            ],
            axis=1,
        )

    examples = sum_pairwise(jnp.concatenate(example_parts, axis=1), "seq", BF16)
    totals = sum_pairwise(
        jnp.stack(
            [
                jnp.sum(train_flag[:, None] * examples, axis=0),
                jnp.sum(query_flag[:, None] * examples, axis=0),
            ]
        ),
        "dp",
        BF16,
    )
    small_flat, query_total = totals[0], totals[1]
    example_norms = jnp.sum(examples * examples, axis=1) / (LAYERS * SMALL * length)
    influence = jnp.sum(examples * query_total, axis=1) / jnp.sqrt(
        length * LAYERS * SMALL * (jnp.mean(query_total * query_total) + 1e-06)
    )

    def by_matrix(values):
        return [values[..., cuts[m] : cuts[m + 1]] for m in range(4)]

    def matrix_sums(values):
        return jnp.stack([jnp.sum(piece, axis=(1, 2)) for piece in by_matrix(values)], axis=1)

    reduced_all = jnp.stack(grad_list, axis=0)
    squared = reduced_all * reduced_all + EPS_SQUARE
    matrix_width = jnp.array([3 * D, D, FF, FF], F32)
    row_total = sum_pairwise(
        jnp.stack([jnp.sum(piece, axis=2) for piece in by_matrix(squared)], axis=1), "seq"
    )
    fresh_row_moments = DECAY * row_state + (1.0 - DECAY) * (
        row_total / matrix_width[None, :, None]
    )
    packed = sum_pairwise(
        jnp.concatenate(
            [jnp.sum(squared, axis=1), jnp.sum(fresh_row_moments, axis=2)], axis=1
        ),
        "dp",
    )
    col_stats = DECAY * col_state + (1.0 - DECAY) * (packed[:, : cuts[4]] / D)
    row_mean = packed[:, cuts[4] :] / D
    col_inverse = by_matrix(lax.rsqrt(col_stats))
    row_inverse = lax.rsqrt(fresh_row_moments / row_mean[:, :, None])
    update = jnp.concatenate(
        [
            piece * row_inverse[:, m, :, None] * col_inverse[m][:, None, :]
            for m, piece in enumerate(by_matrix(reduced_all))
        ],
        axis=2,
    )
    square_totals = jnp.stack([matrix_sums(update * update), matrix_sums(master * master)])
    square_totals = sum_pairwise(sum_pairwise(square_totals, "seq"), "dp")
    entry_count = D * matrix_width
    update_rms = jnp.sqrt(square_totals[0] / entry_count[None, :])
    weight_rms = jnp.sqrt(square_totals[1] / entry_count[None, :])
    factor = RATE * weight_rms / jnp.maximum(1.0, update_rms)
    new_master = jnp.concatenate(
        [
            old - factor[:, m, None, None] * piece
            for m, (old, piece) in enumerate(zip(by_matrix(master), by_matrix(update)))
        ],
        axis=2,
    )
    small_grads = small_flat.reshape(LAYERS, SMALL)
    small_moments = DECAY * small_state + (1.0 - DECAY) * (small_grads * small_grads + EPS_SQUARE)
    small_update = small_grads * lax.rsqrt(small_moments)
    new_pieces = []
    for update_piece, param_piece in zip(unpack(small_update), unpack(small_params)):
        piece_rms = jnp.sqrt(jnp.mean(update_piece * update_piece, axis=-1, keepdims=True))
        param_rms = jnp.sqrt(jnp.mean(param_piece * param_piece, axis=-1, keepdims=True))
        new_pieces.append(
            param_piece - RATE * param_rms * (update_piece / jnp.maximum(1.0, piece_rms))
        )
    small_new = jnp.concatenate(new_pieces, axis=-1)
    return (
        block_out,
        grad_stream,
        example_norms,
        influence,
        reduced_all,
        fresh_row_moments,
        col_stats,
        new_master,
        new_master.astype(BF16),
        small_grads,
        small_moments,
        small_new,
    )


def solution(mesh):
    placed = (
        P("dp", "seq", None),
        P("dp", "seq", None),
        P("dp"),
        P(None, "dp", "seq"),
        P(),
        P(None, None, "dp"),
        P(None, "seq"),
        P(),
    )
    return jax.shard_map(
        on_device,
        mesh=mesh,
        in_specs=placed,
        out_specs=(
            P("dp", "seq", None),
            P("dp", "seq", None),
            P("dp"),
            P("dp"),
            P(None, "dp", "seq"),
            P(None, None, "dp"),
            P(None, "seq"),
            P(None, "dp", "seq"),
            P(None, "dp", "seq"),
            P(),
            P(),
            P(),
        ),
        check_vma=False,
    )
```

```python
import functools

import jax
import jax.numpy as jnp
from jax import lax
from jax.experimental import pallas as pl
from jax.experimental.pallas import tpu as pltpu
from jax.sharding import PartitionSpec as P

D = 768
HEADS = 12
FF = 3072
LAYERS = 2
HEAD_DIM = 64
ROT = 16
SMALL = 9984

EPS_NORM = 1e-05
EPS_SQUARE = 1e-30
RATE = 0.5
DECAY = 0.5
NEG_LARGE = -1e30
SCORE_SCALE = HEAD_DIM ** (-0.5)
CONTRACT_LAST = (((1,), (1,)), ((), ()))
CONTRACT_FIRST = (((0,), (0,)), ((), ()))
VMEM_BYTES = 56 * 1024 * 1024
BF16 = jnp.bfloat16
F32 = jnp.float32


def unpack(vector):
    return jnp.split(vector, [D, 2 * D, 3 * D, 4 * D, 7 * D, 8 * D, 8 * D + FF], axis=-1)


def apply_layer_norm(inputs):
    centred = inputs - jnp.mean(inputs, axis=-1, keepdims=True)
    variance = jnp.mean(centred * centred, axis=-1, keepdims=True)
    inverse = lax.rsqrt(variance + EPS_NORM)
    return (centred * inverse, inverse)


def norm_back(grad_scaled, scaled, inverse):
    mean_grad = jnp.mean(grad_scaled, axis=-1, keepdims=True)
    mean_cross = jnp.mean(grad_scaled * scaled, axis=-1, keepdims=True)
    return (grad_scaled - mean_grad - scaled * mean_cross) * inverse


def rotary_tables(length):
    halfway = ROT // 2
    frequency = 10000.0 ** (-2.0 * jnp.arange(halfway, dtype=F32) / ROT)
    angles = jnp.arange(length).astype(F32)[:, None] * frequency[None, :]
    cosine, sine = jnp.cos(angles), jnp.sin(angles)
    rest = jnp.ones((length, HEAD_DIM - ROT), F32)
    none = jnp.zeros((length, halfway), F32)
    keep = jnp.concatenate([cosine, cosine, rest], axis=1)
    ahead = jnp.concatenate([-sine, none, 0.0 * rest], axis=1)
    behind = jnp.concatenate([none, sine, 0.0 * rest], axis=1)
    return tuple(jnp.concatenate([table, table], axis=1) for table in (keep, ahead, behind))


def swap(values, axis, bits):
    size = lax.axis_size(axis)
    return lax.ppermute(values, axis, [(i, i ^ bits) for i in range(size)])


def sum_pairwise(values, axis, wire=F32):
    bits = 1
    while bits < lax.axis_size(axis):
        sent = values.astype(wire)
        values = sent.astype(F32) + swap(sent, axis, bits).astype(F32)
        bits *= 2
    return values


def both_halves(own):
    return jnp.stack([own, swap(own, "seq", 2)], axis=-3)


def core_sum(keep, send):
    total = keep + swap(send, "seq", 1).astype(F32)
    return total, total.astype(BF16)


def finish_sum(total, low_total):
    return total + jnp.flip(swap(low_total, "seq", 2), axis=0).astype(F32)


def own_sum_over_seq(keep, send):
    total, low_total = core_sum(keep, send)
    return total[0] + swap(low_total[1], "seq", 2).astype(F32)


def gather_rows(rows):
    if lax.axis_size("dp") != 8:
        return [lax.all_gather(rows, "dp", axis=0, tiled=True)]
    even = [rows] + [swap(rows, "dp", 2 * k) for k in (1, 2, 3)]
    pieces = []
    for piece in even:
        pieces += [piece, swap(piece, "dp", 1)]
    return pieces


def pair_sum(keep, send, z_place):
    summed = keep + swap(send, "dp", 1).astype(F32)
    own = lax.dynamic_index_in_dim(summed, z_place, 0, keepdims=False)
    return own, [
        lax.dynamic_index_in_dim(summed, z_place ^ k, 0, keepdims=False).astype(BF16)
        for k in range(1, summed.shape[0])
    ]


def exchange_parts(parts):
    return [swap(part, "dp", 2 * (k + 1)) for k, part in enumerate(parts)]


def in_place_order(pieces, index):
    stacked = list(pieces)
    bits = 1
    while bits < len(stacked):
        flag = (index // bits) % 2 == 1
        stacked = [
            jnp.where(flag, stacked[i ^ bits], stacked[i]) for i in range(len(stacked))
        ]
        bits *= 2
    return stacked


def exchange_blocks(blocks, index):
    size = lax.axis_size("seq")
    received = []
    for k in range(size):
        block = lax.dynamic_index_in_dim(blocks, index ^ k, 0, keepdims=False)
        received.append(block if k == 0 else swap(block, "seq", k))
    return in_place_order(received, index)


def heads_together(values):
    heads = values.shape[-1] // (3 * HEAD_DIM)
    lead = values.shape[:-1]
    by_head = values.reshape(*lead, heads, 3 * HEAD_DIM)
    return jnp.concatenate(
        [
            by_head[..., : 2 * HEAD_DIM].reshape(*lead, heads * 2 * HEAD_DIM),
            by_head[..., 2 * HEAD_DIM :].reshape(*lead, heads * HEAD_DIM),
        ],
        axis=-1,
    )


def heads_apart(values):
    heads = values.shape[-1] // (3 * HEAD_DIM)
    lead = values.shape[:-1]
    pairs, last = jnp.split(values, [heads * 2 * HEAD_DIM], axis=-1)
    return jnp.concatenate(
        [
            pairs.reshape(*lead, heads, 2 * HEAD_DIM),
            last.reshape(*lead, heads, HEAD_DIM),
        ],
        axis=-1,
    ).reshape(values.shape)


def place_tokens(dst, own, near, core_bit, y_here, chunk):
    for bit in (0, 1):

        @pl.when(core_bit == bit)
        def _():
            first, second = (own, near) if bit == 0 else (near, own)
            dst[:chunk] = first[y_here]
            dst[chunk:] = second[y_here]


def spread_tokens(value, keep, send, core_bit, y_here, chunk):
    for bit in (0, 1):

        @pl.when(core_bit == bit)
        def _():
            mine = value[:chunk] if bit == 0 else value[chunk:]
            other = value[chunk:] if bit == 0 else value[:chunk]
            keep[pl.ds(y_here, 1)] = mine[None]
            send[pl.ds(y_here, 1)] = other.astype(send.dtype)[None]


def gelu_and_slope(v):
    magnitude = jnp.abs(v) * 0.7071067811865476
    t = 1.0 / (1.0 + 0.3275911 * magnitude)
    falling = jnp.exp(-0.5 * v * v)
    poly = t * (
        0.254829592
        + t * (-0.284496736 + t * (1.421413741 + t * (-1.453152027 + t * 1.061405429)))
    )
    tail = 0.5 * poly * falling
    cdf = jnp.where(v >= 0.0, 1.0 - tail, tail)
    return v * cdf, cdf + v * falling * 0.3989422804014327


def weight_copies(dp_place, sources, targets, sems):
    copies = []
    for (pieces, first), target in zip(sources, targets):
        rows, width = pieces[0].shape[0], target.shape[1]
        for k, piece in enumerate(pieces):
            offset = 0 if len(pieces) == 1 else pl.multiple_of((k ^ dp_place) * rows, 16)
            copies.append(
                pltpu.make_async_copy(
                    piece if piece.shape[1] == width else piece.at[:, pl.ds(first, width)],
                    target.at[pl.ds(offset, rows), :],
                    sems.at[len(copies)],
                )
            )
    return copies


def start_all(copies):
    for copy in copies:
        copy.start()


def wait_all(copies):
    for copy in copies:
        copy.wait()


def turn(pair, tables, sign):
    keep_tab, ahead_tab, behind_tab = tables
    ahead = pltpu.roll(pair, 2 * HEAD_DIM - ROT // 2, 1) * ahead_tab[...]
    behind = pltpu.roll(pair, ROT // 2, 1) * behind_tab[...]
    return pair * keep_tab[...] + sign * (ahead + behind)


def forward_kernel(count_a, count_b, place, *refs):
    refs = list(refs)

    def take(count):
        taken, refs[:] = refs[:count], refs[count:]
        return taken

    own, near, vec = take(3)
    tables = take(3)
    (w_out,) = take(1)
    pieces_a, pieces_b = take(count_a), take(count_b)
    keep, send, xhat, qk, val, att, lse, hid, slope = refs[-14:-5]
    whole_a, whole_b, k_all, v_all, sems = refs[-5:]
    core_bit, y_bit, dp_place = place[0], place[1], place[2]
    step = pl.program_id(0)
    wide = 3 * val.shape[1]
    source_b = (pieces_b, 0) if count_b else (pieces_a, pieces_a[0].shape[1] - whole_b.shape[1])
    copies = weight_copies(dp_place, [(pieces_a, 0), source_b], [whole_a, whole_b], sems)
    copies_a, copies_b = copies[:count_a], copies[count_a:]

    @pl.when(step == 0)
    def _():
        start_all(copies)

    chunk = own.shape[1]
    block = 2 * chunk
    y_here = step ^ y_bit
    place_tokens(xhat, own, near, core_bit, y_here, chunk)
    scaled = xhat[...].astype(F32)
    normed_one = (scaled * vec[0:1] + vec[1:2]).astype(BF16)
    normed_two = (scaled * vec[2:3] + vec[3:4]).astype(BF16)

    @pl.when(step == 0)
    def _():
        wait_all(copies_a)

    heads = val.shape[-1] // HEAD_DIM
    joined = jnp.dot(normed_one, whole_a[:, :wide], preferred_element_type=F32) + vec[5:6, :wide]
    for h in range(heads):
        at_q, at_k = 2 * HEAD_DIM * h, 2 * HEAD_DIM * h + HEAD_DIM
        turned = turn(joined[:, at_q : at_k + HEAD_DIM], tables, 1.0)
        qk[:, at_q : at_k + HEAD_DIM] = turned.astype(BF16)
        k_all[h, pl.ds(step * block, block)] = turned[:, HEAD_DIM:].astype(BF16)
        first = 2 * HEAD_DIM * heads + HEAD_DIM * h
        v_all[h, pl.ds(step * block, block)] = joined[:, first : first + HEAD_DIM].astype(BF16)
    val[...] = joined[:, 2 * HEAD_DIM * heads :].astype(BF16)
    row = lax.broadcasted_iota(jnp.int32, (block, block), 0)
    column = lax.broadcasted_iota(jnp.int32, (block, block), 1)
    lane = lax.broadcasted_iota(jnp.int32, (block, 128), 1)
    for here in range(2):

        @pl.when(step == here)
        def _():
            log_sums = jnp.zeros((block, 128), F32)
            for h in range(heads):
                at_q = 2 * HEAD_DIM * h
                query = qk[:, at_q : at_q + HEAD_DIM] * jnp.asarray(SCORE_SCALE, BF16)
                scores = []
                for j in range(here + 1):
                    part = lax.dot_general(
                        query,
                        k_all[h, block * j : block * (j + 1)],
                        CONTRACT_LAST,
                        preferred_element_type=F32,
                    )
                    if j == here:
                        part = jnp.where(column <= row, part, NEG_LARGE)
                    scores.append(part)
                largest = functools.reduce(
                    jnp.maximum, [jnp.max(part, axis=-1, keepdims=True) for part in scores]
                )
                total = 0.0
                mixed = 0.0
                for j, part in enumerate(scores):
                    exponent = jnp.exp(part - largest)
                    total = total + jnp.sum(exponent, axis=-1, keepdims=True)
                    mixed = mixed + jnp.dot(
                        exponent.astype(BF16),
                        v_all[h, block * j : block * (j + 1)],
                        preferred_element_type=F32,
                    )
                att[:, HEAD_DIM * h : HEAD_DIM * (h + 1)] = (mixed / total).astype(BF16)
                log_sums = jnp.where(lane == h, largest + jnp.log(total), log_sums)
            lse[...] = log_sums.T[:8]

    @pl.when(step == 0)
    def _():
        wait_all(copies_b)

    quarter = hid.shape[-1]
    hidden_pre = (
        jnp.dot(normed_two, whole_b[:, :quarter], preferred_element_type=F32) + vec[4:5, :quarter]
    )
    hidden, gradient = gelu_and_slope(hidden_pre)
    hid[...] = hidden.astype(BF16)
    slope[...] = gradient
    partial = jnp.dot(att[...], w_out[...], preferred_element_type=F32) + lax.dot_general(
        hid[...], whole_b[:, quarter:], CONTRACT_LAST, preferred_element_type=F32
    )
    spread_tokens(partial, keep, send, core_bit, y_here, chunk)


def add_up(sums, place_row, values):
    sums[place_row : place_row + 1, : values.shape[-1]] += jnp.sum(
        values.astype(F32), axis=0, keepdims=True
    )


def mlp_backward_kernel(count, place, *refs):
    own, near, vec, xhat, slope = refs[:5]
    pieces = refs[5 : 5 + count]
    grad, grad_pre, grad_two, sums, whole_b, sems = refs[-6:]
    core_bit, y_bit, dp_place = place[0], place[1], place[2]
    step = pl.program_id(0)
    copies = weight_copies(
        dp_place, [(pieces, pieces[0].shape[1] - whole_b.shape[1])], [whole_b], sems
    )

    @pl.when(step == 0)
    def _():
        start_all(copies)
        sums[...] = jnp.zeros_like(sums)

    chunk = own.shape[1]
    place_tokens(grad, own, near, core_bit, step ^ y_bit, chunk)

    @pl.when(step == 0)
    def _():
        wait_all(copies)

    quarter = slope.shape[-1]
    grad_hidden = jnp.dot(grad[...], whole_b[:, quarter:], preferred_element_type=F32)
    low_pre = (grad_hidden * slope[...]).astype(BF16)
    grad_pre[...] = low_pre
    normed = lax.dot_general(
        low_pre, whole_b[:, :quarter], CONTRACT_LAST, preferred_element_type=F32
    )
    grad_two[...] = normed * vec[2:3]
    add_up(sums, 0, normed * xhat[...].astype(F32))
    add_up(sums, 1, normed)
    add_up(sums, 2, low_pre)
    add_up(sums, 3, grad[...])


def attention_backward_kernel(count, place, *refs):
    refs = list(refs)

    def take(number):
        taken, refs[:] = refs[:number], refs[number:]
        return taken

    grad, vec = take(2)
    tables = take(3)
    w_out, xhat, qk, val, lse, grad_two = take(6)
    pieces = take(count)
    keep, send, grad_joined, sums, whole_a, dk_all, dv_all, dq_all, sems = refs[-9:]
    core_bit, y_bit, dp_place = place[0], place[1], place[2]
    step = 1 - pl.program_id(0)
    copies = weight_copies(dp_place, [(pieces, 0)], [whole_a], sems)

    @pl.when(step == 1)
    def _():
        start_all(copies)
        sums[...] = jnp.zeros_like(sums)

    block = grad.shape[0]
    chunk = block // 2
    heads = val.shape[-1] // HEAD_DIM
    grad_att = lax.dot_general(
        grad[...], w_out[...], CONTRACT_LAST, preferred_element_type=F32
    ).astype(BF16)
    row = lax.broadcasted_iota(jnp.int32, (block, block), 0)
    column = lax.broadcasted_iota(jnp.int32, (block, block), 1)
    for here in range(2):

        @pl.when(step == here)
        def _():
            for h in range(heads):
                at_q, at_k = 2 * HEAD_DIM * h, 2 * HEAD_DIM * h + HEAD_DIM
                query = qk[block * here : block * (here + 1), at_q:at_k]
                query = query * jnp.asarray(SCORE_SCALE, BF16)
                near_grad = grad_att[:, HEAD_DIM * h : HEAD_DIM * (h + 1)]
                log_row = lse[h : h + 1]
                probs, grad_probs, keys = [], [], []
                delta = 0.0
                for j in range(here + 1):
                    key = qk[block * j : block * (j + 1), at_k : at_k + HEAD_DIM]
                    value = val[block * j : block * (j + 1), HEAD_DIM * h : HEAD_DIM * (h + 1)]
                    scores = lax.dot_general(
                        key, query, CONTRACT_LAST, preferred_element_type=F32
                    )
                    prob = jnp.exp(scores - log_row)
                    if j == here:
                        prob = jnp.where(row <= column, prob, 0.0)
                    grad_prob = lax.dot_general(
                        value, near_grad, CONTRACT_LAST, preferred_element_type=F32
                    )
                    delta = delta + jnp.sum(prob * grad_prob, axis=0, keepdims=True)
                    probs.append(prob)
                    grad_probs.append(grad_prob)
                    keys.append(key)
                dq = 0.0
                for j in range(here + 1):
                    grad_score = (probs[j] * (grad_probs[j] - delta)).astype(BF16)
                    dk = jnp.dot(grad_score, query, preferred_element_type=F32)
                    dv = jnp.dot(probs[j].astype(BF16), near_grad, preferred_element_type=F32)
                    if here == 1:
                        dk_all[h, block * j : block * (j + 1)] = dk
                        dv_all[h, block * j : block * (j + 1)] = dv
                    else:
                        dk_all[h, block * j : block * (j + 1)] += dk
                        dv_all[h, block * j : block * (j + 1)] += dv
                    dq = dq + lax.dot_general(
                        grad_score, keys[j], CONTRACT_FIRST, preferred_element_type=F32
                    )
                dq_all[h] = dq * SCORE_SCALE

    for h in range(heads):
        pair = jnp.concatenate([dq_all[h], dk_all[h, pl.ds(step * block, block)]], axis=1)
        at_q = 2 * HEAD_DIM * h
        grad_joined[:, at_q : at_q + 2 * HEAD_DIM] = turn(pair, tables, -1.0).astype(BF16)
        first = 2 * HEAD_DIM * heads + HEAD_DIM * h
        grad_joined[:, first : first + HEAD_DIM] = dv_all[h, pl.ds(step * block, block)].astype(
            BF16
        )

    @pl.when(step == 1)
    def _():
        wait_all(copies)

    normed = lax.dot_general(
        grad_joined[...], whole_a[:, : grad_joined.shape[1]], CONTRACT_LAST, preferred_element_type=F32
    )
    spread_tokens(
        normed * vec[0:1] + grad_two[...], keep, send, core_bit, step ^ y_bit, chunk
    )
    add_up(sums, 0, normed * xhat[...].astype(F32))
    add_up(sums, 1, normed)
    add_up(sums, 2, grad_joined[...])


def outer_sum(flags, lefts, rights):
    total = 0.0
    for s, (left, right) in enumerate(zip(lefts, rights)):
        kept = jnp.where(flags[s] > 0, right, jnp.zeros_like(right))
        total = total + lax.dot_general(left, kept, CONTRACT_FIRST, preferred_element_type=F32)
    return total


def store_rows(value, outs, first, x_bit):
    columns = pl.ds(first, value.shape[1])
    if len(outs) == 1:
        outs[0][:, columns] = value.astype(BF16)
        return
    keep, send = outs
    rows = keep.shape[1]
    for bit in (0, 1):

        @pl.when(x_bit == bit)
        def _():
            for z in range(keep.shape[0]):
                at = rows * (2 * z + bit)
                to = rows * (2 * z + 1 - bit)
                keep[z, :, columns] = value[at : at + rows]
                send[z, :, columns] = value[to : to + rows].astype(BF16)


def mlp_outer_kernel(count, n_outs, scalars, vec, *refs):
    groups = [refs[count * n : count * (n + 1)] for n in range(5)]
    outs, outward = refs[-1 - n_outs : -1], refs[-1]
    xhat, grad, grad_pre, hid, att = ([ref[...] for ref in group] for group in groups)
    quarter = hid[0].shape[1]
    x_bit, flags = scalars[0], [scalars[1 + s] for s in range(count)]
    normed = [(x.astype(F32) * vec[2:3] + vec[3:4]).astype(BF16) for x in xhat]
    outward[...] = outer_sum(flags, att, grad).astype(BF16)
    store_rows(outer_sum(flags, normed, grad_pre), outs, 0, x_bit)
    store_rows(outer_sum(flags, grad, hid), outs, quarter, x_bit)


def qkv_outer_kernel(count, n_outs, scalars, vec, *refs):
    groups = [refs[count * n : count * (n + 1)] for n in range(2)]
    outward, outs = refs[2 * count], refs[-n_outs:]
    xhat, grad_joined = ([ref[...] for ref in group] for group in groups)
    wide = grad_joined[0].shape[1]
    x_bit, flags = scalars[0], [scalars[1 + s] for s in range(count)]
    normed = [(x.astype(F32) * vec[0:1] + vec[1:2]).astype(BF16) for x in xhat]
    store_rows(outer_sum(flags, normed, grad_joined), outs, 0, x_bit)
    store_rows(outward[...].astype(F32), outs, wide, x_bit)


def natural_heads(values):
    heads = values.shape[1] // (3 * HEAD_DIM)
    parts = []
    for h in range(heads):
        parts.append(values[:, 2 * HEAD_DIM * h : 2 * HEAD_DIM * (h + 1)])
        at = 2 * HEAD_DIM * heads + HEAD_DIM * h
        parts.append(values[:, at : at + HEAD_DIM])
    return parts


def matrix_cuts(width):
    unit = width // 12
    return [0, 3 * unit, 4 * unit, 8 * unit, width]


def gradient_kernel(counts, cuts, *refs):
    sources_b = refs[: counts[0]]
    sources_a = refs[counts[0] : counts[0] + counts[1]]
    grads, row_sums, col_sums = refs[-3:]
    part_b = sum(ref[...].astype(F32) for ref in sources_b)
    part_a = sum(ref[...].astype(F32) for ref in sources_a) if sources_a else None
    if part_a is None:
        part_a, part_b = part_b[:, cuts[4] - cuts[2] :], part_b[:, : cuts[4] - cuts[2]]
    at = 0
    for part in natural_heads(part_a[:, : cuts[1]]):
        grads[0, :, at : at + part.shape[1]] = part
        at += part.shape[1]
    grads[0, :, at : cuts[2]] = part_a[:, cuts[1] :]
    grads[0, :, cuts[2] :] = part_b
    whole = grads[0]
    squares = whole * whole + EPS_SQUARE
    col_sums[0] = jnp.sum(squares, axis=0, keepdims=True)
    lane = lax.broadcasted_iota(jnp.int32, (whole.shape[0], 128), 1)
    by_row = jnp.zeros((whole.shape[0], 128), F32)
    for m in range(4):
        total = jnp.sum(squares[:, cuts[m] : cuts[m + 1]], axis=1, keepdims=True)
        by_row = jnp.where(lane == m, total, by_row)
    row_sums[0] = by_row


def scaled_update(grads, row_inverse, col_inverse, cuts, m):
    columns = slice(cuts[m], cuts[m + 1])
    return grads[0, :, columns] * row_inverse[0, :, m : m + 1] * col_inverse[0, :, columns]


def square_kernel(cuts, grads, master, row_inverse, col_inverse, sums):
    row = lax.broadcasted_iota(jnp.int32, (8, 128), 0)
    lane = lax.broadcasted_iota(jnp.int32, (8, 128), 1)
    result = jnp.zeros((8, 128), F32)
    for m in range(4):
        update = scaled_update(grads, row_inverse, col_inverse, cuts, m)
        old = master[0, :, cuts[m] : cuts[m + 1]]
        for at, values in ((0, update), (1, old)):
            total = jnp.sum(jnp.sum(values * values, axis=0, keepdims=True), axis=1, keepdims=True)
            result = jnp.where((row == at) & (lane == m), total, result)
    sums[0] = result


def update_kernel(cuts, grads, master, row_inverse, col_inverse, factor, new, new_low):
    for m in range(4):
        update = scaled_update(grads, row_inverse, col_inverse, cuts, m)
        columns = slice(cuts[m], cuts[m + 1])
        fresh = master[0, :, columns] - factor[0, :, m : m + 1] * update
        new[0, :, columns] = fresh
        new_low[0, :, columns] = fresh.astype(BF16)


def whole_spec(shape):
    return pl.BlockSpec(shape, lambda *_: (0,) * len(shape))


def in_any(count):
    return [pl.BlockSpec(memory_space=pl.ANY)] * count


def cost(micros):
    return pl.CostEstimate(
        flops=int(micros * 10**9), bytes_accessed=int(micros * 10**6), transcendentals=0
    )


def rows_spec(rows, width, block_of):
    return pl.BlockSpec((rows, width), lambda t, *_: (block_of(t), 0))


def run_forward(place, chunks, vec, tables, weight, riders=()):
    w_out, pieces_a, pieces_b = weight
    chunk = chunks[0].shape[1]
    block, length = 2 * chunk, 4 * chunk
    count_a, count_b = len(pieces_a), len(pieces_b)
    out_wide = w_out.shape[0]
    heads = out_wide // HEAD_DIM
    wide = 3 * out_wide
    quarter = FF * out_wide // D

    def same(t):
        return t

    widths = [
        (D, BF16),
        (2 * out_wide, BF16),
        (out_wide, BF16),
        (out_wide, BF16),
        (quarter, BF16),
        (quarter, F32),
    ]
    shapes = [jax.ShapeDtypeStruct((length, width), kind) for width, kind in widths]
    specs = [rows_spec(block, width, same) for width, _ in widths]
    shapes.insert(4, jax.ShapeDtypeStruct((8, length), F32))
    specs.insert(4, pl.BlockSpec((8, block), lambda t, *_: (0, t)))
    return pl.pallas_call(
        functools.partial(forward_kernel, count_a, count_b),
        grid_spec=pltpu.PrefetchScalarGridSpec(
            num_scalar_prefetch=1,
            grid=(2,),
            in_specs=[
                *[whole_spec((2, chunk, D))] * 2,
                whole_spec((8, D)),
                *[rows_spec(block, 2 * HEAD_DIM, same)] * 3,
                whole_spec(w_out.shape),
                *in_any(count_a + count_b + len(riders)),
            ],
            out_specs=[whole_spec((2, chunk, D))] * 2 + specs,
            scratch_shapes=[
                pltpu.VMEM((D, wide + out_wide), BF16),
                pltpu.VMEM((D, 2 * quarter), BF16),
                pltpu.VMEM((heads, length, HEAD_DIM), BF16),
                pltpu.VMEM((heads, length, HEAD_DIM), BF16),
                pltpu.SemaphoreType.DMA((count_a + max(count_b, 1),)),
            ],
        ),
        out_shape=[
            jax.ShapeDtypeStruct((2, chunk, D), F32),
            jax.ShapeDtypeStruct((2, chunk, D), BF16),
            *shapes,
        ],
        compiler_params=pltpu.CompilerParams(vmem_limit_bytes=VMEM_BYTES),
        cost_estimate=cost(13),
        name="layer_forward",
    )(place, *chunks, vec, *tables, w_out, *pieces_a, *pieces_b, *riders)


def run_mlp_backward(place, chunks, vec, weight, xhat, slope, riders=()):
    _, pieces_a, pieces_b = weight
    pieces = pieces_b or pieces_a
    chunk = chunks[0].shape[1]
    block, length = 2 * chunk, 4 * chunk
    quarter = slope.shape[1]

    def same(t):
        return t

    return pl.pallas_call(
        functools.partial(mlp_backward_kernel, len(pieces)),
        grid_spec=pltpu.PrefetchScalarGridSpec(
            num_scalar_prefetch=1,
            grid=(2,),
            in_specs=[
                *[whole_spec((2, chunk, D))] * 2,
                whole_spec((8, D)),
                rows_spec(block, D, same),
                rows_spec(block, quarter, same),
                *in_any(len(pieces) + len(riders)),
            ],
            out_specs=[
                rows_spec(block, D, same),
                rows_spec(block, quarter, same),
                rows_spec(block, D, same),
                whole_spec((8, D)),
            ],
            scratch_shapes=[
                pltpu.VMEM((D, 2 * quarter), BF16),
                pltpu.SemaphoreType.DMA((len(pieces),)),
            ],
        ),
        out_shape=[
            jax.ShapeDtypeStruct((length, D), BF16),
            jax.ShapeDtypeStruct((length, quarter), BF16),
            jax.ShapeDtypeStruct((length, D), F32),
            jax.ShapeDtypeStruct((8, D), F32),
        ],
        compiler_params=pltpu.CompilerParams(vmem_limit_bytes=VMEM_BYTES),
        cost_estimate=cost(6),
        name="mlp_backward",
    )(place, *chunks, vec, xhat, slope, *pieces, *riders)


def run_attention_backward(
    place, grad, vec, tables, weight, xhat, qk, val, lse, grad_two, riders=()
):
    w_out, pieces, _ = weight
    length = grad.shape[0]
    block, chunk = length // 2, length // 4
    out_wide = w_out.shape[0]
    heads = out_wide // HEAD_DIM
    wide = 3 * out_wide

    def turned(t):
        return 1 - t

    return pl.pallas_call(
        functools.partial(attention_backward_kernel, len(pieces)),
        grid_spec=pltpu.PrefetchScalarGridSpec(
            num_scalar_prefetch=1,
            grid=(2,),
            in_specs=[
                rows_spec(block, D, turned),
                whole_spec((8, D)),
                *[rows_spec(block, 2 * HEAD_DIM, turned)] * 3,
                whole_spec(w_out.shape),
                rows_spec(block, D, turned),
                whole_spec(qk.shape),
                whole_spec(val.shape),
                pl.BlockSpec((8, block), lambda t, *_: (0, 1 - t)),
                rows_spec(block, D, turned),
                *in_any(len(pieces) + len(riders)),
            ],
            out_specs=[
                *[whole_spec((2, chunk, D))] * 2,
                rows_spec(block, wide, turned),
                whole_spec((8, D)),
            ],
            scratch_shapes=[
                pltpu.VMEM((D, wide + out_wide), BF16),
                pltpu.VMEM((heads, length, HEAD_DIM), F32),
                pltpu.VMEM((heads, length, HEAD_DIM), F32),
                pltpu.VMEM((heads, block, HEAD_DIM), F32),
                pltpu.SemaphoreType.DMA((len(pieces),)),
            ],
        ),
        out_shape=[
            jax.ShapeDtypeStruct((2, chunk, D), F32),
            jax.ShapeDtypeStruct((2, chunk, D), BF16),
            jax.ShapeDtypeStruct((length, wide), BF16),
            jax.ShapeDtypeStruct((8, D), F32),
        ],
        compiler_params=pltpu.CompilerParams(vmem_limit_bytes=VMEM_BYTES),
        cost_estimate=cost(11),
        name="attention_backward",
    )(place, grad, vec, *tables, w_out, xhat, qk, val, lse, grad_two, *pieces, *riders)


def outer_outputs(split, columns, total, place):
    if split:
        shape = (4, D // 8, columns)
        return [jax.ShapeDtypeStruct(shape, F32), jax.ShapeDtypeStruct(shape, BF16)], [
            whole_spec(shape)
        ] * 2
    return [jax.ShapeDtypeStruct((D, total), BF16)], [
        pl.BlockSpec((D, columns), lambda *_: (0, place))
    ]


def run_mlp_outer(scalars, vec, groups, split, total, riders=()):
    arrays = [array for group in groups for array in group]
    out_wide, quarter = groups[4][0].shape[1], groups[3][0].shape[1]
    shapes, specs = outer_outputs(split, 2 * quarter, total, 0)
    return pl.pallas_call(
        functools.partial(mlp_outer_kernel, len(groups[0]), len(shapes)),
        grid_spec=pltpu.PrefetchScalarGridSpec(
            num_scalar_prefetch=1,
            grid=(1,),
            in_specs=[
                whole_spec((8, D)),
                *[whole_spec(array.shape) for array in arrays],
                *in_any(len(riders)),
            ],
            out_specs=specs + [whole_spec((out_wide, D))],
        ),
        out_shape=shapes + [jax.ShapeDtypeStruct((out_wide, D), BF16)],
        compiler_params=pltpu.CompilerParams(vmem_limit_bytes=VMEM_BYTES),
        cost_estimate=cost(10),
        name="mlp_outer",
    )(scalars, vec, *arrays, *riders)


def run_qkv_outer(scalars, vec, groups, outward, split, both=None, riders=()):
    arrays = [array for group in groups for array in group] + [outward]
    columns = groups[1][0].shape[1] + outward.shape[1]
    total = columns if both is None else both.shape[1]
    shapes, specs = outer_outputs(split, columns, total, total // columns - 1)
    riders = list(riders) if both is None else [both, *riders]
    return pl.pallas_call(
        functools.partial(qkv_outer_kernel, len(groups[0]), len(shapes)),
        grid_spec=pltpu.PrefetchScalarGridSpec(
            num_scalar_prefetch=1,
            grid=(1,),
            in_specs=[
                whole_spec((8, D)),
                *[whole_spec(array.shape) for array in arrays],
                *in_any(len(riders)),
            ],
            out_specs=specs,
        ),
        out_shape=shapes,
        input_output_aliases={} if both is None else {2 + len(arrays): 0},
        compiler_params=pltpu.CompilerParams(vmem_limit_bytes=VMEM_BYTES),
        cost_estimate=cost(6),
        name="qkv_outer",
    )(scalars, vec, *arrays, *riders)


def run_gradient(sources_b, sources_a, layer, shape, earlier=None):
    _, rows, width = shape
    arrays = [*sources_b, *sources_a]
    riders = [] if earlier is None else [earlier]
    return pl.pallas_call(
        functools.partial(
            gradient_kernel, (len(sources_b), len(sources_a)), matrix_cuts(width)
        ),
        grid=(1,),
        in_specs=[whole_spec(array.shape) for array in arrays] + in_any(len(riders)),
        out_specs=[
            pl.BlockSpec((1, rows, width), lambda *_: (layer, 0, 0)),
            whole_spec((1, rows, 128)),
            whole_spec((1, 1, width)),
        ],
        out_shape=[
            jax.ShapeDtypeStruct(shape, F32),
            jax.ShapeDtypeStruct((1, rows, 128), F32),
            jax.ShapeDtypeStruct((1, 1, width), F32),
        ],
        input_output_aliases={len(arrays): 0} if riders else {},
        compiler_params=pltpu.CompilerParams(vmem_limit_bytes=VMEM_BYTES),
        cost_estimate=cost(2),
        name="gradient",
    )(*arrays, *riders)


def layer_spec(*shape):
    return pl.BlockSpec((1, *shape), lambda i: (i, 0, 0))


def run_squares(grads, master, row_inverse, col_inverse):
    layers, rows, width = grads.shape
    return pl.pallas_call(
        functools.partial(square_kernel, matrix_cuts(width)),
        grid=(layers,),
        in_specs=[
            layer_spec(rows, width),
            layer_spec(rows, width),
            layer_spec(rows, 4),
            layer_spec(1, width),
        ],
        out_specs=layer_spec(8, 128),
        out_shape=jax.ShapeDtypeStruct((layers, 8, 128), F32),
        compiler_params=pltpu.CompilerParams(vmem_limit_bytes=VMEM_BYTES),
        cost_estimate=cost(2),
        name="squares",
    )(grads, master, row_inverse, col_inverse)


def run_update(grads, master, row_inverse, col_inverse, factor):
    layers, rows, width = grads.shape
    return pl.pallas_call(
        functools.partial(update_kernel, matrix_cuts(width)),
        grid=(layers,),
        in_specs=[
            layer_spec(rows, width),
            layer_spec(rows, width),
            layer_spec(rows, 4),
            layer_spec(1, width),
            layer_spec(1, 4),
        ],
        out_specs=[layer_spec(rows, width)] * 2,
        out_shape=[
            jax.ShapeDtypeStruct(grads.shape, F32),
            jax.ShapeDtypeStruct(grads.shape, BF16),
        ],
        compiler_params=pltpu.CompilerParams(vmem_limit_bytes=VMEM_BYTES),
        cost_estimate=cost(2),
        name="update",
    )(grads, master, row_inverse, col_inverse, factor)


def pass_through_kernel(*refs):
    del refs


def after(values, *others):
    return pl.pallas_call(
        pass_through_kernel,
        in_specs=in_any(1 + len(others)),
        out_specs=pl.BlockSpec(memory_space=pl.ANY),
        out_shape=jax.ShapeDtypeStruct(values.shape, values.dtype),
        input_output_aliases={0: 0},
        name="after",
    )(values, *others)


def out_rows(columns, dp_place, seq_place):
    stacked = jnp.concatenate(
        in_place_order(columns, dp_place) if len(columns) > 1 else columns, axis=0
    )
    size = lax.axis_size("seq")
    blocks = stacked.reshape(size, D // size, -1)
    return jnp.concatenate(exchange_blocks(blocks, seq_place), axis=1)


def on_device(block_in, cotangent, labels, master, small_params, row_state, col_state, small_state):
    sequences, chunk = block_in.shape[:2]
    group_count = lax.axis_size("seq")
    seq_place, dp_place = lax.axis_index("seq"), lax.axis_index("dp")
    place = jnp.stack([seq_place % 2, seq_place // 2, dp_place]).astype(jnp.int32)
    length = chunk * group_count
    flags = (labels == 0).astype(jnp.int32)
    train_flag = flags.astype(F32)
    scalars = jnp.concatenate([(dp_place % 2).astype(jnp.int32)[None], flags])
    query_flag = 1.0 - train_flag
    wide, out_wide, quarter = 3 * D // group_count, D // group_count, FF // group_count
    cuts = matrix_cuts(master.shape[2])
    split = lax.axis_size("dp") == 8
    x_bit, z_place = dp_place % 2, dp_place // 2
    tables = rotary_tables(length)

    def normalise(stream):
        scaled, inverse = apply_layer_norm(stream)
        low_scaled = scaled.astype(BF16)
        return (scaled, inverse), low_scaled

    stream = both_halves(block_in).astype(F32)
    norm, low_scaled = normalise(stream)
    near = swap(low_scaled, "seq", 1)
    chunks = [(low_scaled[s], near[s]) for s in range(sequences)]

    low = master.astype(BF16)
    first_a = jnp.concatenate(
        [heads_together(low[0, :, : cuts[1]]), low[0, :, cuts[1] : cuts[2]]], axis=1
    )
    pieces_a = gather_rows(first_a)
    pieces_b = [lax.all_gather(low[0, :, cuts[2] :], "dp", axis=0, tiled=True)]
    rows_one = jnp.concatenate(
        [heads_together(low[1, :, : cuts[1]]), low[1, :, cuts[1] :]], axis=1
    )
    whole_one = lax.all_gather(
        after(rows_one, *pieces_b), "dp", axis=0, tiled=True
    )
    weights = [
        (out_rows([piece[:, wide:] for piece in pieces_a], dp_place, seq_place), pieces_a, pieces_b)
    ]
    vectors, params = [], []
    for i in range(LAYERS):
        param = unpack(small_params[i])
        params.append(param)
        bias_qkv = heads_together(lax.dynamic_slice_in_dim(param[4], seq_place * wide, wide))
        bias_up = lax.dynamic_slice_in_dim(param[6], seq_place * quarter, quarter)
        vectors.append(
            jnp.stack(
                [
                    *param[:4],
                    jnp.pad(bias_up, (0, D - quarter)),
                    jnp.pad(bias_qkv, (0, D - wide)),
                    jnp.zeros((D,), F32),
                    jnp.zeros((D,), F32),
                ]
            )
        )

    streams = [stream[s] for s in range(sequences)]
    norms, saved_all = [[(norm[0][s], norm[1][s]) for s in range(sequences)]], []
    for i in range(LAYERS):
        last = i == LAYERS - 1
        saved_all.append([])
        next_chunks, next_norms = [], []
        riders = []
        for s in range(sequences):
            keep, send, *saved = run_forward(
                place, chunks[s], vectors[i], tables, weights[i], riders
            )
            saved_all[i].append(saved)
            bias = params[i][5] + params[i][7]
            if last:
                streams[s] = streams[s][0] + own_sum_over_seq(keep, send) + bias
                continue
            total, low_total = core_sum(keep, send)
            riders = [low_total]
            streams[s] = streams[s] + finish_sum(total, low_total) + bias
            norm, low_scaled = normalise(streams[s])
            next_norms.append(norm)
            next_chunks.append((low_scaled, swap(low_scaled, "seq", 1)))
        if i == 0:
            whole_one = after(whole_one, keep)
            weights.append(
                (
                    out_rows([whole_one[:, wide : wide + out_wide]], dp_place, seq_place),
                    [whole_one],
                    [],
                )
            )
        chunks = next_chunks
        norms.append(next_norms)
    block_out = jnp.stack(streams).astype(BF16)

    low_grad = both_halves(cotangent)
    near = swap(low_grad, "seq", 1)
    chunks = [(low_grad[s], near[s]) for s in range(sequences)]
    grads = [low_grad[s].astype(F32) for s in range(sequences)]
    example_parts, sources = [None] * LAYERS, [None] * LAYERS
    only_one = jnp.where(seq_place == 0, 1.0, 0.0)
    for i in reversed(range(LAYERS)):
        last = i == 0
        xhats, qks, vals, atts, lses, hids, slopes = zip(*saved_all[i])
        mlp, attention, next_chunks = [], [], []
        riders = []

        def attention_part(s, riders=()):
            out = run_attention_backward(
                place,
                mlp[s][0],
                vectors[i],
                tables,
                weights[i],
                xhats[s],
                qks[s],
                vals[s],
                lses[s],
                mlp[s][2],
                riders,
            )
            attention.append(out)
            norm = norms[i][s]
            if last:
                grad_scaled = own_sum_over_seq(out[0], out[1])
                grads[s] = grads[s][0] + norm_back(grad_scaled, norm[0][0], norm[1][0])
                return []
            total, low_total = core_sum(out[0], out[1])
            grads[s] = grads[s] + norm_back(finish_sum(total, low_total), *norm)
            low_grad = grads[s].astype(BF16)
            next_chunks.append((low_grad, swap(low_grad, "seq", 1)))
            return [low_total]

        for s in range(sequences):
            mlp.append(
                run_mlp_backward(
                    place, chunks[s], vectors[i], weights[i], xhats[s], slopes[s], riders
                )
            )
            if not last:
                riders = attention_part(s)
        *both, outward = run_mlp_outer(
            scalars,
            vectors[i],
            [xhats, [out[0] for out in mlp], [out[1] for out in mlp], hids, atts],
            split and last,
            2 * quarter if last else master.shape[2],
            riders,
        )
        blocks = outward.reshape(out_wide, group_count, out_wide).transpose(1, 0, 2)
        outward = jnp.concatenate(exchange_blocks(blocks, seq_place), axis=0)
        if last:
            riders = both[-1:]
            for s in range(sequences):
                attention_part(s, riders)
                if split and s == 0:
                    own_b, parts_b = pair_sum(*both, z_place)
                    riders = parts_b
        groups = [xhats, [out[2] for out in attention]]
        if not last:
            (both,) = run_qkv_outer(scalars, vectors[i], groups, outward, False, both[0])
            parts = lax.psum_scatter(both, "dp", scatter_dimension=0, tiled=True)
            sources[i] = ([parts], [])
        else:
            rest = run_qkv_outer(scalars, vectors[i], groups, outward, split)
            if split:
                own_a, parts_a = pair_sum(*rest, z_place)
                sources[i] = (
                    [own_b, *exchange_parts(parts_b)],
                    [own_a, *exchange_parts(parts_a)],
                )
            else:
                sources[i] = tuple(
                    [lax.psum_scatter(part[0], "dp", scatter_dimension=0, tiled=True)]
                    for part in (both, rest)
                )
        chunks = next_chunks
        def spread(values, width):
            return lax.dynamic_update_slice(
                jnp.zeros((sequences, group_count * width), F32), values, (0, seq_place * width)
            )

        sums_m = jnp.stack([out[3] for out in mlp])
        sums_t = jnp.stack([out[3] for out in attention])
        grad_sum = sums_m[:, 3] * only_one
        example_parts[i] = jnp.concatenate(
            [
                sums_t[:, 0],
                sums_t[:, 1],
                sums_m[:, 0],
                sums_m[:, 1],
                spread(heads_apart(sums_t[:, 2, :wide]), wide),
                grad_sum,
                spread(sums_m[:, 2, :quarter], quarter),
                grad_sum,
            ],
            axis=1,
        )
    grad_stream = jnp.stack(grads)

    examples = sum_pairwise(jnp.concatenate(example_parts, axis=1), "seq", BF16)
    totals = sum_pairwise(
        jnp.stack(
            [
                jnp.sum(train_flag[:, None] * examples, axis=0),
                jnp.sum(query_flag[:, None] * examples, axis=0),
            ]
        ),
        "dp",
        BF16,
    )
    small_flat, query_total = totals[0], totals[1]
    example_norms = jnp.sum(examples * examples, axis=1) / (LAYERS * SMALL * length)
    influence = jnp.sum(examples * query_total, axis=1) / jnp.sqrt(
        length * LAYERS * SMALL * (jnp.mean(query_total * query_total) + 1e-06)
    )

    reduced_all, row_sums, col_sums = None, [None] * LAYERS, [None] * LAYERS
    for i in reversed(range(LAYERS)):
        reduced_all, row_sums[i], col_sums[i] = run_gradient(
            *sources[i], i, master.shape, reduced_all
        )
    matrix_width = jnp.array([3 * D, D, FF, FF], F32)
    row_part = jnp.concatenate(row_sums, axis=0)[:, :, :4].transpose(0, 2, 1)
    col_part = jnp.concatenate(col_sums, axis=0)[:, 0]
    row_total = sum_pairwise(row_part, "seq")
    fresh_row_moments = DECAY * row_state + (1.0 - DECAY) * (
        row_total / matrix_width[None, :, None]
    )
    packed = sum_pairwise(
        jnp.concatenate(
            [col_part, jnp.sum(row_part, axis=2), jnp.sum(row_state, axis=2)], axis=1
        ),
        "dp",
    )
    col_stats = DECAY * col_state + (1.0 - DECAY) * (packed[:, : cuts[4]] / D)
    square_part, state_sum = packed[:, cuts[4] : cuts[4] + 4], packed[:, cuts[4] + 4 :]
    row_inverse = lax.rsqrt(fresh_row_moments).transpose(0, 2, 1)
    col_inverse = lax.rsqrt(col_stats)[:, None]
    square_sums = run_squares(reduced_all, master, row_inverse, col_inverse)
    group_sums = sum_pairwise(
        jnp.concatenate([square_sums[:, :2, :4], square_part[:, None]], axis=1), "seq"
    )
    square_totals = sum_pairwise(group_sums[:, :2], "dp")
    row_mean = (
        DECAY * state_sum + (1.0 - DECAY) * (group_sums[:, 2] / matrix_width[None, :])
    ) / D
    entry_count = D * matrix_width
    update_rms = jnp.sqrt(row_mean * square_totals[:, 0] / entry_count[None, :])
    weight_rms = jnp.sqrt(square_totals[:, 1] / entry_count[None, :])
    factor = RATE * weight_rms * jnp.sqrt(row_mean) / jnp.maximum(1.0, update_rms)
    new_master, new_low = run_update(
        reduced_all, master, row_inverse, col_inverse, factor[:, None]
    )
    small_grads = small_flat.reshape(LAYERS, SMALL)
    small_moments = DECAY * small_state + (1.0 - DECAY) * (small_grads * small_grads + EPS_SQUARE)
    small_update = small_grads * lax.rsqrt(small_moments)
    new_pieces = []
    for update_piece, param_piece in zip(unpack(small_update), unpack(small_params)):
        piece_rms = jnp.sqrt(jnp.mean(update_piece * update_piece, axis=-1, keepdims=True))
        param_rms = jnp.sqrt(jnp.mean(param_piece * param_piece, axis=-1, keepdims=True))
        new_pieces.append(
            param_piece - RATE * param_rms * (update_piece / jnp.maximum(1.0, piece_rms))
        )
    small_new = jnp.concatenate(new_pieces, axis=-1)
    return (
        block_out,
        grad_stream,
        example_norms,
        influence,
        reduced_all,
        fresh_row_moments,
        col_stats,
        new_master,
        new_low,
        small_grads,
        small_moments,
        small_new,
    )


def solution(mesh):
    placed = (
        P("dp", "seq", None),
        P("dp", "seq", None),
        P("dp"),
        P(None, "dp", "seq"),
        P(),
        P(None, None, "dp"),
        P(None, "seq"),
        P(),
    )
    return jax.shard_map(
        on_device,
        mesh=mesh,
        in_specs=placed,
        out_specs=(
            P("dp", "seq", None),
            P("dp", "seq", None),
            P("dp"),
            P("dp"),
            P(None, "dp", "seq"),
            P(None, None, "dp"),
            P(None, "seq"),
            P(None, "dp", "seq"),
            P(None, "dp", "seq"),
            P(),
            P(),
            P(),
        ),
        check_vma=False,
    )
```

```python
import functools

import jax
import numpy as np
import jax.numpy as jnp
from jax import lax
from jax.experimental import pallas as pl
from jax.experimental.pallas import tpu as pltpu
from jax.sharding import PartitionSpec as P

D = 768
HEADS = 12
FF = 3072
LAYERS = 2
HEAD_DIM = 64
ROT = 16
SMALL = 9984

EPS_NORM = 1e-05
EPS_SQUARE = 1e-30
RATE = 0.5
DECAY = 0.5
NEG_LARGE = -1e30
SCORE_SCALE = HEAD_DIM ** (-0.5)
CONTRACT_LAST = (((1,), (1,)), ((), ()))
CONTRACT_FIRST = (((0,), (0,)), ((), ()))
VMEM_BYTES = 56 * 1024 * 1024
BF16 = jnp.bfloat16
F32 = jnp.float32


def unpack(vector):
    return jnp.split(vector, [D, 2 * D, 3 * D, 4 * D, 7 * D, 8 * D, 8 * D + FF], axis=-1)


def apply_layer_norm(inputs):
    centred = inputs - jnp.mean(inputs, axis=-1, keepdims=True)
    variance = jnp.mean(centred * centred, axis=-1, keepdims=True)
    inverse = lax.rsqrt(variance + EPS_NORM)
    return (centred * inverse, inverse)


def norm_back(grad_scaled, scaled, inverse):
    mean_grad = jnp.mean(grad_scaled, axis=-1, keepdims=True)
    mean_cross = jnp.mean(grad_scaled * scaled, axis=-1, keepdims=True)
    return (grad_scaled - mean_grad - scaled * mean_cross) * inverse


def rotary_tables(length):
    halfway = ROT // 2
    frequency = 10000.0 ** (-2.0 * np.arange(halfway) / ROT)
    angles = np.arange(length)[:, None] * frequency[None, :]
    cosine, sine = np.cos(angles), np.sin(angles)
    rest = np.ones((length, HEAD_DIM - ROT))
    none = np.zeros((length, halfway))
    keep = np.concatenate([cosine, cosine, rest], axis=1)
    ahead = np.concatenate([-sine, none, 0.0 * rest], axis=1)
    behind = np.concatenate([none, sine, 0.0 * rest], axis=1)
    return tuple(
        jnp.asarray(np.concatenate([table, table], axis=1), F32) for table in (keep, ahead, behind)
    )


def swap(values, axis, bits):
    size = lax.axis_size(axis)
    return lax.ppermute(values, axis, [(i, i ^ bits) for i in range(size)])


def sum_pairwise(values, axis, wire=F32):
    bits = 1
    while bits < lax.axis_size(axis):
        sent = values.astype(wire)
        values = sent.astype(F32) + swap(sent, axis, bits).astype(F32)
        bits *= 2
    return values


def both_halves(own):
    return jnp.stack([own, swap(own, "seq", 2)], axis=-3)


def core_sum(keep, send):
    total = keep + swap(send, "seq", 1).astype(F32)
    return total, total.astype(BF16)


def finish_sum(total, received):
    return total + jnp.flip(received, axis=0).astype(F32)


def own_sum_over_seq(keep, send):
    total, low_total = core_sum(keep, send)
    return total[0] + swap(low_total[1], "seq", 2).astype(F32)


def gather_rows(rows):
    if lax.axis_size("dp") != 8:
        return [lax.all_gather(rows, "dp", axis=0, tiled=True)]
    pieces = []
    for k in range(4):
        pieces += [rows, swap(rows, "dp", 1)]
        if k < 3:
            rows = lax.ppermute(rows, "dp", [(i, (i + 2) % 8) for i in range(8)])
    return pieces


def piece_places(count, dp_place):
    if count == 1:
        return [0]
    return [(dp_place + 8 - 2 * (k // 2)) % 8 ^ (k % 2) for k in range(count)]


def pair_sum(keep, send, z_place):
    summed = keep + swap(send, "dp", 1).astype(F32)
    own = lax.dynamic_index_in_dim(summed, z_place, 0, keepdims=False)
    return own, [
        lax.dynamic_index_in_dim(summed, z_place ^ k, 0, keepdims=False).astype(BF16)
        for k in range(1, summed.shape[0])
    ]


def pair_total(keep, send):
    return (keep + swap(send, "dp", 1).astype(F32)).astype(BF16).reshape(-1, keep.shape[-1])


def scatter_along_z(total):
    groups = [[2 * z + x for z in range(4)] for x in range(2)]
    return lax.psum_scatter(
        total, "dp", scatter_dimension=0, tiled=True, axis_index_groups=groups
    )


def exchange_parts(parts):
    return [swap(part, "dp", 2 * (k + 1)) for k, part in enumerate(parts)]


def in_place_order(pieces, index):
    stacked = list(pieces)
    bits = 1
    while bits < len(stacked):
        flag = (index // bits) % 2 == 1
        stacked = [
            jnp.where(flag, stacked[i ^ bits], stacked[i]) for i in range(len(stacked))
        ]
        bits *= 2
    return stacked


def exchange_blocks(blocks, index):
    size = lax.axis_size("seq")
    received = []
    for k in range(size):
        block = lax.dynamic_index_in_dim(blocks, index ^ k, 0, keepdims=False)
        received.append(block if k == 0 else swap(block, "seq", k))
    return in_place_order(received, index)


def heads_together(values):
    heads = values.shape[-1] // (3 * HEAD_DIM)
    lead = values.shape[:-1]
    by_head = values.reshape(*lead, heads, 3 * HEAD_DIM)
    return jnp.concatenate(
        [
            by_head[..., : 2 * HEAD_DIM].reshape(*lead, heads * 2 * HEAD_DIM),
            by_head[..., 2 * HEAD_DIM :].reshape(*lead, heads * HEAD_DIM),
        ],
        axis=-1,
    )


def heads_apart(values):
    heads = values.shape[-1] // (3 * HEAD_DIM)
    lead = values.shape[:-1]
    pairs, last = jnp.split(values, [heads * 2 * HEAD_DIM], axis=-1)
    return jnp.concatenate(
        [
            pairs.reshape(*lead, heads, 2 * HEAD_DIM),
            last.reshape(*lead, heads, HEAD_DIM),
        ],
        axis=-1,
    ).reshape(values.shape)


def place_tokens(dst, own, near, core_bit, y_here, chunk):
    for bit in (0, 1):

        @pl.when(core_bit == bit)
        def _():
            first, second = (own, near) if bit == 0 else (near, own)
            dst[:chunk] = first[y_here]
            dst[chunk:] = second[y_here]


def spread_tokens(value, keep, send, core_bit, y_here, chunk):
    for bit in (0, 1):

        @pl.when(core_bit == bit)
        def _():
            mine = value[:chunk] if bit == 0 else value[chunk:]
            other = value[chunk:] if bit == 0 else value[:chunk]
            keep[pl.ds(y_here, 1)] = mine[None]
            send[pl.ds(y_here, 1)] = other.astype(send.dtype)[None]


def gelu_and_slope(v):
    magnitude = jnp.abs(v) * 0.7071067811865476
    t = 1.0 / (1.0 + 0.3275911 * magnitude)
    falling = jnp.exp(-0.5 * v * v)
    poly = t * (
        0.254829592
        + t * (-0.284496736 + t * (1.421413741 + t * (-1.453152027 + t * 1.061405429)))
    )
    tail = 0.5 * poly * falling
    cdf = jnp.where(v >= 0.0, 1.0 - tail, tail)
    return v * cdf, cdf + v * falling * 0.3989422804014327


def weight_copies(dp_place, sources, targets, sems):
    copies = []
    for (pieces, first), target in zip(sources, targets):
        rows, width = pieces[0].shape[0], target.shape[1]
        for piece, place in zip(pieces, piece_places(len(pieces), dp_place)):
            offset = 0 if len(pieces) == 1 else pl.multiple_of(place * rows, 16)
            copies.append(
                pltpu.make_async_copy(
                    piece.at[:, pl.ds(first, width)],
                    target.at[pl.ds(offset, rows), :],
                    sems.at[len(copies)],
                )
            )
    return copies


def start_all(copies):
    for copy in copies:
        copy.start()


def wait_all(copies):
    for copy in copies:
        copy.wait()


def turn(pair, tables, sign):
    keep_tab, ahead_tab, behind_tab = tables
    ahead = pltpu.roll(pair, 2 * HEAD_DIM - ROT // 2, 1) * ahead_tab[...]
    behind = pltpu.roll(pair, ROT // 2, 1) * behind_tab[...]
    return pair * keep_tab[...] + sign * (ahead + behind)


def forward_kernel(count, place, *refs):
    refs = list(refs)

    def take(count):
        taken, refs[:] = refs[:count], refs[count:]
        return taken

    own, near, vec = take(3)
    tables = take(3)
    (w_out,) = take(1)
    pieces = take(count)
    keep, send, xhat, qk, val, att, lse, hid, slope = refs[-14:-5]
    whole_a, whole_b, k_all, v_all, sems = refs[-5:]
    core_bit, y_bit, dp_place = place[0], place[1], place[2]
    step = pl.program_id(0)
    wide = 3 * val.shape[1]
    sources = [(pieces, 0), (pieces, whole_a.shape[1])]
    copies = weight_copies(dp_place, sources, [whole_a, whole_b], sems)
    copies_a, copies_b = copies[:count], copies[count:]

    @pl.when(step == 0)
    def _():
        start_all(copies)

    chunk = own.shape[1]
    block = 2 * chunk
    y_here = step ^ y_bit
    place_tokens(xhat, own, near, core_bit, y_here, chunk)
    scaled = xhat[...].astype(F32)
    normed_one = (scaled * vec[0:1] + vec[1:2]).astype(BF16)
    normed_two = (scaled * vec[2:3] + vec[3:4]).astype(BF16)

    @pl.when(step == 0)
    def _():
        wait_all(copies_a)

    heads = val.shape[-1] // HEAD_DIM
    joined = jnp.dot(normed_one, whole_a[:, :wide], preferred_element_type=F32) + vec[5:6, :wide]
    for h in range(heads):
        at_q, at_k = 2 * HEAD_DIM * h, 2 * HEAD_DIM * h + HEAD_DIM
        turned = turn(joined[:, at_q : at_k + HEAD_DIM], tables, 1.0)
        qk[:, at_q : at_k + HEAD_DIM] = turned.astype(BF16)
        k_all[h, pl.ds(step * block, block)] = turned[:, HEAD_DIM:].astype(BF16)
        first = 2 * HEAD_DIM * heads + HEAD_DIM * h
        v_all[h, pl.ds(step * block, block)] = joined[:, first : first + HEAD_DIM].astype(BF16)
    val[...] = joined[:, 2 * HEAD_DIM * heads :].astype(BF16)
    row = lax.broadcasted_iota(jnp.int32, (block, block), 0)
    column = lax.broadcasted_iota(jnp.int32, (block, block), 1)
    lane = lax.broadcasted_iota(jnp.int32, (block, 128), 1)
    for here in range(2):

        @pl.when(step == here)
        def _():
            log_sums = jnp.zeros((block, 128), F32)
            for h in range(heads):
                at_q = 2 * HEAD_DIM * h
                query = qk[:, at_q : at_q + HEAD_DIM] * jnp.asarray(SCORE_SCALE, BF16)
                scores = []
                for j in range(here + 1):
                    part = lax.dot_general(
                        query,
                        k_all[h, block * j : block * (j + 1)],
                        CONTRACT_LAST,
                        preferred_element_type=F32,
                    )
                    if j == here:
                        part = jnp.where(column <= row, part, NEG_LARGE)
                    scores.append(part)
                largest = functools.reduce(
                    jnp.maximum, [jnp.max(part, axis=-1, keepdims=True) for part in scores]
                )
                total = 0.0
                mixed = 0.0
                for j, part in enumerate(scores):
                    exponent = jnp.exp(part - largest)
                    total = total + jnp.sum(exponent, axis=-1, keepdims=True)
                    mixed = mixed + jnp.dot(
                        exponent.astype(BF16),
                        v_all[h, block * j : block * (j + 1)],
                        preferred_element_type=F32,
                    )
                att[:, HEAD_DIM * h : HEAD_DIM * (h + 1)] = (mixed / total).astype(BF16)
                log_sums = jnp.where(lane == h, largest + jnp.log(total), log_sums)
            lse[...] = log_sums.T[:8]

    @pl.when(step == 0)
    def _():
        wait_all(copies_b)

    quarter = hid.shape[-1]
    hidden_pre = (
        jnp.dot(normed_two, whole_b[:, :quarter], preferred_element_type=F32) + vec[4:5, :quarter]
    )
    hidden, gradient = gelu_and_slope(hidden_pre)
    hid[...] = hidden.astype(BF16)
    slope[...] = gradient
    partial = jnp.dot(att[...], w_out[...], preferred_element_type=F32) + lax.dot_general(
        hid[...], whole_b[:, quarter:], CONTRACT_LAST, preferred_element_type=F32
    )
    spread_tokens(partial, keep, send, core_bit, y_here, chunk)


def add_up(sums, place_row, values):
    sums[place_row : place_row + 1, : values.shape[-1]] += jnp.sum(
        values.astype(F32), axis=0, keepdims=True
    )


def mlp_backward_kernel(count, sequence, place, *refs):
    own, near, vec, xhat, slope, att = refs[:6]
    pieces = refs[6 : 6 + count]
    grad, grad_pre, grad_two, sums, outward, whole_b, sems = refs[-7:]
    core_bit, y_bit, dp_place = place[0], place[1], place[2]
    step = pl.program_id(0)
    copies = weight_copies(
        dp_place, [(pieces, pieces[0].shape[1] - whole_b.shape[1])], [whole_b], sems
    )

    @pl.when(step == 0)
    def _():
        start_all(copies)
        sums[...] = jnp.zeros_like(sums)

    chunk = own.shape[1]
    place_tokens(grad, own, near, core_bit, step ^ y_bit, chunk)

    @pl.when(step == 0)
    def _():
        wait_all(copies)

    quarter = slope.shape[-1]
    grad_hidden = jnp.dot(grad[...], whole_b[:, quarter:], preferred_element_type=F32)
    low_pre = (grad_hidden * slope[...]).astype(BF16)
    grad_pre[...] = low_pre
    normed = lax.dot_general(
        low_pre, whole_b[:, :quarter], CONTRACT_LAST, preferred_element_type=F32
    )
    grad_two[...] = normed * vec[2:3]
    add_up(sums, 0, normed * xhat[...].astype(F32))
    add_up(sums, 1, normed)
    add_up(sums, 2, low_pre)
    add_up(sums, 3, grad[...])
    kept = jnp.where(place[3 + sequence] > 0, grad[...], jnp.zeros_like(grad))
    product = lax.dot_general(att[...], kept, CONTRACT_FIRST, preferred_element_type=F32)

    @pl.when(step == 0)
    def _():
        outward[...] = product

    @pl.when(step != 0)
    def _():
        outward[...] += product


def attention_backward_kernel(count, place, *refs):
    refs = list(refs)

    def take(number):
        taken, refs[:] = refs[:number], refs[number:]
        return taken

    grad, vec = take(2)
    tables = take(3)
    w_out, xhat, qk, val, lse, grad_two = take(6)
    pieces = take(count)
    keep, send, grad_joined, sums, whole_a, dk_all, dv_all, dq_all, sems = refs[-9:]
    core_bit, y_bit, dp_place = place[0], place[1], place[2]
    step = 1 - pl.program_id(0)
    copies = weight_copies(dp_place, [(pieces, 0)], [whole_a], sems)

    @pl.when(step == 1)
    def _():
        start_all(copies)
        sums[...] = jnp.zeros_like(sums)

    block = grad.shape[0]
    chunk = block // 2
    heads = val.shape[-1] // HEAD_DIM
    grad_att = lax.dot_general(
        grad[...], w_out[...], CONTRACT_LAST, preferred_element_type=F32
    ).astype(BF16)
    row = lax.broadcasted_iota(jnp.int32, (block, block), 0)
    column = lax.broadcasted_iota(jnp.int32, (block, block), 1)
    for here in range(2):

        @pl.when(step == here)
        def _():
            for h in range(heads):
                at_q, at_k = 2 * HEAD_DIM * h, 2 * HEAD_DIM * h + HEAD_DIM
                query = qk[block * here : block * (here + 1), at_q:at_k]
                query = query * jnp.asarray(SCORE_SCALE, BF16)
                near_grad = grad_att[:, HEAD_DIM * h : HEAD_DIM * (h + 1)]
                log_row = lse[h : h + 1]
                probs, grad_probs, keys = [], [], []
                delta = 0.0
                for j in range(here + 1):
                    key = qk[block * j : block * (j + 1), at_k : at_k + HEAD_DIM]
                    value = val[block * j : block * (j + 1), HEAD_DIM * h : HEAD_DIM * (h + 1)]
                    scores = lax.dot_general(
                        key, query, CONTRACT_LAST, preferred_element_type=F32
                    )
                    prob = jnp.exp(scores - log_row)
                    if j == here:
                        prob = jnp.where(row <= column, prob, 0.0)
                    grad_prob = lax.dot_general(
                        value, near_grad, CONTRACT_LAST, preferred_element_type=F32
                    )
                    delta = delta + jnp.sum(prob * grad_prob, axis=0, keepdims=True)
                    probs.append(prob)
                    grad_probs.append(grad_prob)
                    keys.append(key)
                dq = 0.0
                for j in range(here + 1):
                    grad_score = (probs[j] * (grad_probs[j] - delta)).astype(BF16)
                    dk = jnp.dot(grad_score, query, preferred_element_type=F32)
                    dv = jnp.dot(probs[j].astype(BF16), near_grad, preferred_element_type=F32)
                    if here == 1:
                        dk_all[h, block * j : block * (j + 1)] = dk
                        dv_all[h, block * j : block * (j + 1)] = dv
                    else:
                        dk_all[h, block * j : block * (j + 1)] += dk
                        dv_all[h, block * j : block * (j + 1)] += dv
                    dq = dq + lax.dot_general(
                        grad_score, keys[j], CONTRACT_FIRST, preferred_element_type=F32
                    )
                dq_all[h] = dq * SCORE_SCALE

    for h in range(heads):
        pair = jnp.concatenate([dq_all[h], dk_all[h, pl.ds(step * block, block)]], axis=1)
        at_q = 2 * HEAD_DIM * h
        grad_joined[:, at_q : at_q + 2 * HEAD_DIM] = turn(pair, tables, -1.0).astype(BF16)
        first = 2 * HEAD_DIM * heads + HEAD_DIM * h
        grad_joined[:, first : first + HEAD_DIM] = dv_all[h, pl.ds(step * block, block)].astype(
            BF16
        )

    @pl.when(step == 1)
    def _():
        wait_all(copies)

    normed = lax.dot_general(
        grad_joined[...], whole_a[:, : grad_joined.shape[1]], CONTRACT_LAST, preferred_element_type=F32
    )
    spread_tokens(
        normed * vec[0:1] + grad_two[...], keep, send, core_bit, step ^ y_bit, chunk
    )
    add_up(sums, 0, normed * xhat[...].astype(F32))
    add_up(sums, 1, normed)
    add_up(sums, 2, grad_joined[...])


def outer_sum(flags, lefts, rights):
    total = 0.0
    for s, (left, right) in enumerate(zip(lefts, rights)):
        kept = jnp.where(flags[s] > 0, right, jnp.zeros_like(right))
        total = total + lax.dot_general(left, kept, CONTRACT_FIRST, preferred_element_type=F32)
    return total


def store_rows(value, outs, first, x_bit):
    columns = pl.ds(first, value.shape[1])
    if len(outs) == 1:
        outs[0][:, columns] = value.astype(BF16)
        return
    keep, send = outs
    rows = keep.shape[1]
    for bit in (0, 1):

        @pl.when(x_bit == bit)
        def _():
            for z in range(keep.shape[0]):
                at = rows * (2 * z + bit)
                to = rows * (2 * z + 1 - bit)
                keep[z, :, columns] = value[at : at + rows]
                send[z, :, columns] = value[to : to + rows].astype(BF16)


def mlp_outer_kernel(count, n_outs, scalars, vec, *refs):
    groups = [refs[count * n : count * (n + 1)] for n in range(4)]
    outs = refs[-n_outs:]
    xhat, grad, grad_pre, hid = ([ref[...] for ref in group] for group in groups)
    x_bit, flags = scalars[0], [scalars[2 + s] for s in range(count)]
    normed = [(x.astype(F32) * vec[2:3] + vec[3:4]).astype(BF16) for x in xhat]
    store_rows(outer_sum(flags, normed, grad_pre), outs, 0, x_bit)
    store_rows(outer_sum(flags, grad, hid), outs, hid[0].shape[1], x_bit)


def qkv_outer_kernel(count, n_outs, scalars, vec, *refs):
    groups = [refs[count * n : count * (n + 1)] for n in range(2)]
    outward, outs = refs[2 * count], refs[-n_outs:]
    xhat, grad_joined = ([ref[...] for ref in group] for group in groups)
    wide = grad_joined[0].shape[1]
    x_bit, flags = scalars[0], [scalars[2 + s] for s in range(count)]
    normed = [(x.astype(F32) * vec[0:1] + vec[1:2]).astype(BF16) for x in xhat]
    store_rows(outer_sum(flags, normed, grad_joined), outs, 0, x_bit)
    store_rows(outward[...].astype(F32), outs, wide, x_bit)


def natural_heads(values):
    heads = values.shape[1] // (3 * HEAD_DIM)
    parts = []
    for h in range(heads):
        parts.append(values[:, 2 * HEAD_DIM * h : 2 * HEAD_DIM * (h + 1)])
        at = 2 * HEAD_DIM * heads + HEAD_DIM * h
        parts.append(values[:, at : at + HEAD_DIM])
    return parts


def matrix_cuts(width):
    unit = width // 12
    return [0, 3 * unit, 4 * unit, 8 * unit, width]


def gradient_kernel(counts, cuts, *refs):
    refs = list(refs)
    grads, row_sums, col_sums = refs[-3:]
    parts = []
    for count in counts:
        taken, refs[:] = refs[:count], refs[count:]
        parts.append(sum(ref[...].astype(F32) for ref in taken))
    both, rest = parts
    at = 0
    for part in natural_heads(rest[:, : cuts[1]]):
        grads[0, :, at : at + part.shape[1]] = part
        at += part.shape[1]
    grads[0, :, cuts[1] : cuts[2]] = rest[:, cuts[1] :]
    grads[0, :, cuts[2] :] = both
    whole = grads[0]
    squares = whole * whole + EPS_SQUARE
    col_sums[0] = jnp.sum(squares, axis=0, keepdims=True)
    lane = lax.broadcasted_iota(jnp.int32, (whole.shape[0], 128), 1)
    by_row = jnp.zeros((whole.shape[0], 128), F32)
    for m in range(4):
        total = jnp.sum(squares[:, cuts[m] : cuts[m + 1]], axis=1, keepdims=True)
        by_row = jnp.where(lane == m, total, by_row)
    row_sums[0] = by_row


def scaled_update(grads, row_inverse, col_inverse, cuts, m):
    columns = slice(cuts[m], cuts[m + 1])
    return grads[0, :, columns] * row_inverse[0, :, m : m + 1] * col_inverse[0, :, columns]


def square_kernel(cuts, grads, master, row_inverse, col_inverse, sums):
    row = lax.broadcasted_iota(jnp.int32, (8, 128), 0)
    lane = lax.broadcasted_iota(jnp.int32, (8, 128), 1)
    result = jnp.zeros((8, 128), F32)
    for m in range(4):
        update = scaled_update(grads, row_inverse, col_inverse, cuts, m)
        old = master[0, :, cuts[m] : cuts[m + 1]]
        for at, values in ((0, update), (1, old)):
            total = jnp.sum(jnp.sum(values * values, axis=0, keepdims=True), axis=1, keepdims=True)
            result = jnp.where((row == at) & (lane == m), total, result)
    sums[0] = result


def update_kernel(cuts, grads, master, row_inverse, col_inverse, factor, new, new_low):
    for m in range(4):
        update = scaled_update(grads, row_inverse, col_inverse, cuts, m)
        columns = slice(cuts[m], cuts[m + 1])
        fresh = master[0, :, columns] - factor[0, :, m : m + 1] * update
        new[0, :, columns] = fresh
        new_low[0, :, columns] = fresh.astype(BF16)


def whole_spec(shape):
    return pl.BlockSpec(shape, lambda *_: (0,) * len(shape))


def in_any(count):
    return [pl.BlockSpec(memory_space=pl.ANY)] * count


def cost(micros):
    return pl.CostEstimate(
        flops=int(micros * 10**9), bytes_accessed=int(micros * 10**6), transcendentals=0
    )


def chunk_specs(chunks):
    specs = []
    for array, place in chunks:
        if place is None:
            specs.append(whole_spec(array.shape))
        else:
            specs.append(
                pl.BlockSpec((None, *array.shape[1:]), lambda *_, place=place: (place, 0, 0, 0))
            )
    return specs


def rows_spec(rows, width, block_of):
    return pl.BlockSpec((rows, width), lambda t, *_: (block_of(t), 0))


def run_forward(place, chunks, vec, tables, weight, riders=()):
    w_out, pieces = weight
    chunk = chunks[0][0].shape[-2]
    block, length = 2 * chunk, 4 * chunk
    count = len(pieces)
    out_wide = w_out.shape[0]
    heads = out_wide // HEAD_DIM
    wide = 3 * out_wide
    quarter = FF * out_wide // D

    def same(t):
        return t

    widths = [
        (D, BF16),
        (2 * out_wide, BF16),
        (out_wide, BF16),
        (out_wide, BF16),
        (quarter, BF16),
        (quarter, F32),
    ]
    shapes = [jax.ShapeDtypeStruct((length, width), kind) for width, kind in widths]
    specs = [rows_spec(block, width, same) for width, _ in widths]
    shapes.insert(4, jax.ShapeDtypeStruct((8, length), F32))
    specs.insert(4, pl.BlockSpec((8, block), lambda t, *_: (0, t)))
    return pl.pallas_call(
        functools.partial(forward_kernel, count),
        grid_spec=pltpu.PrefetchScalarGridSpec(
            num_scalar_prefetch=1,
            grid=(2,),
            in_specs=[
                *chunk_specs(chunks),
                whole_spec((8, D)),
                *[rows_spec(block, 2 * HEAD_DIM, same)] * 3,
                whole_spec(w_out.shape),
                *in_any(count + len(riders)),
            ],
            out_specs=[whole_spec((2, chunk, D))] * 2 + specs,
            scratch_shapes=[
                pltpu.VMEM((D, wide + out_wide), BF16),
                pltpu.VMEM((D, 2 * quarter), BF16),
                pltpu.VMEM((heads, length, HEAD_DIM), BF16),
                pltpu.VMEM((heads, length, HEAD_DIM), BF16),
                pltpu.SemaphoreType.DMA((2 * count,)),
            ],
        ),
        out_shape=[
            jax.ShapeDtypeStruct((2, chunk, D), F32),
            jax.ShapeDtypeStruct((2, chunk, D), BF16),
            *shapes,
        ],
        compiler_params=pltpu.CompilerParams(vmem_limit_bytes=VMEM_BYTES),
        cost_estimate=cost(13),
        name="layer_forward",
    )(place, *[array for array, _ in chunks], vec, *tables, w_out, *pieces, *riders)


def run_mlp_backward(place, sequence, chunks, vec, weight, xhat, slope, att, riders=()):
    _, pieces = weight
    chunk = chunks[0][0].shape[-2]
    block, length = 2 * chunk, 4 * chunk
    quarter = slope.shape[1]

    def same(t):
        return t

    return pl.pallas_call(
        functools.partial(mlp_backward_kernel, len(pieces), sequence),
        grid_spec=pltpu.PrefetchScalarGridSpec(
            num_scalar_prefetch=1,
            grid=(2,),
            in_specs=[
                *chunk_specs(chunks),
                whole_spec((8, D)),
                rows_spec(block, D, same),
                rows_spec(block, quarter, same),
                rows_spec(block, att.shape[1], same),
                *in_any(len(pieces) + len(riders)),
            ],
            out_specs=[
                rows_spec(block, D, same),
                rows_spec(block, quarter, same),
                rows_spec(block, D, same),
                whole_spec((8, D)),
                whole_spec((att.shape[1], D)),
            ],
            scratch_shapes=[
                pltpu.VMEM((D, 2 * quarter), BF16),
                pltpu.SemaphoreType.DMA((len(pieces),)),
            ],
        ),
        out_shape=[
            jax.ShapeDtypeStruct((length, D), BF16),
            jax.ShapeDtypeStruct((length, quarter), BF16),
            jax.ShapeDtypeStruct((length, D), F32),
            jax.ShapeDtypeStruct((8, D), F32),
            jax.ShapeDtypeStruct((att.shape[1], D), F32),
        ],
        compiler_params=pltpu.CompilerParams(vmem_limit_bytes=VMEM_BYTES),
        cost_estimate=cost(8),
        name="mlp_backward",
    )(place, *[array for array, _ in chunks], vec, xhat, slope, att, *pieces, *riders)


def run_attention_backward(
    place, grad, vec, tables, weight, xhat, qk, val, lse, grad_two, riders=()
):
    w_out, pieces = weight
    length = grad.shape[0]
    block, chunk = length // 2, length // 4
    out_wide = w_out.shape[0]
    heads = out_wide // HEAD_DIM
    wide = 3 * out_wide

    def turned(t):
        return 1 - t

    return pl.pallas_call(
        functools.partial(attention_backward_kernel, len(pieces)),
        grid_spec=pltpu.PrefetchScalarGridSpec(
            num_scalar_prefetch=1,
            grid=(2,),
            in_specs=[
                rows_spec(block, D, turned),
                whole_spec((8, D)),
                *[rows_spec(block, 2 * HEAD_DIM, turned)] * 3,
                whole_spec(w_out.shape),
                rows_spec(block, D, turned),
                whole_spec(qk.shape),
                whole_spec(val.shape),
                pl.BlockSpec((8, block), lambda t, *_: (0, 1 - t)),
                rows_spec(block, D, turned),
                *in_any(len(pieces) + len(riders)),
            ],
            out_specs=[
                *[whole_spec((2, chunk, D))] * 2,
                rows_spec(block, wide, turned),
                whole_spec((8, D)),
            ],
            scratch_shapes=[
                pltpu.VMEM((D, wide + out_wide), BF16),
                pltpu.VMEM((heads, length, HEAD_DIM), F32),
                pltpu.VMEM((heads, length, HEAD_DIM), F32),
                pltpu.VMEM((heads, block, HEAD_DIM), F32),
                pltpu.SemaphoreType.DMA((len(pieces),)),
            ],
        ),
        out_shape=[
            jax.ShapeDtypeStruct((2, chunk, D), F32),
            jax.ShapeDtypeStruct((2, chunk, D), BF16),
            jax.ShapeDtypeStruct((length, wide), BF16),
            jax.ShapeDtypeStruct((8, D), F32),
        ],
        compiler_params=pltpu.CompilerParams(vmem_limit_bytes=VMEM_BYTES),
        cost_estimate=cost(11),
        name="attention_backward",
    )(place, grad, vec, *tables, w_out, xhat, qk, val, lse, grad_two, *pieces, *riders)


def outer_outputs(split, columns):
    if split:
        shape = (4, D // 8, columns)
        kinds = [F32, BF16]
    else:
        shape, kinds = (D, columns), [BF16]
    return [jax.ShapeDtypeStruct(shape, kind) for kind in kinds], [whole_spec(shape)] * len(kinds)


def run_mlp_outer(scalars, vec, groups, split, riders=()):
    arrays = [array for group in groups for array in group]
    shapes, specs = outer_outputs(split, 2 * groups[3][0].shape[1])
    return pl.pallas_call(
        functools.partial(mlp_outer_kernel, len(groups[0]), len(shapes)),
        grid_spec=pltpu.PrefetchScalarGridSpec(
            num_scalar_prefetch=1,
            grid=(1,),
            in_specs=[
                whole_spec((8, D)),
                *[whole_spec(array.shape) for array in arrays],
                *in_any(len(riders)),
            ],
            out_specs=specs,
        ),
        out_shape=shapes,
        compiler_params=pltpu.CompilerParams(vmem_limit_bytes=VMEM_BYTES),
        cost_estimate=cost(10),
        name="mlp_outer",
    )(scalars, vec, *arrays, *riders)


def run_qkv_outer(scalars, vec, groups, outward, split, riders=()):
    arrays = [array for group in groups for array in group] + [outward]
    shapes, specs = outer_outputs(split, groups[1][0].shape[1] + outward.shape[1])
    return pl.pallas_call(
        functools.partial(qkv_outer_kernel, len(groups[0]), len(shapes)),
        grid_spec=pltpu.PrefetchScalarGridSpec(
            num_scalar_prefetch=1,
            grid=(1,),
            in_specs=[
                whole_spec((8, D)),
                *[whole_spec(array.shape) for array in arrays],
                *in_any(len(riders)),
            ],
            out_specs=specs,
        ),
        out_shape=shapes,
        compiler_params=pltpu.CompilerParams(vmem_limit_bytes=VMEM_BYTES),
        cost_estimate=cost(6),
        name="qkv_outer",
    )(scalars, vec, *arrays, *riders)


def run_gradient(sources, layer, shape, earlier=None):
    _, rows, width = shape
    arrays = [array for source in sources for array in source]
    riders = [] if earlier is None else [earlier]
    return pl.pallas_call(
        functools.partial(
            gradient_kernel, [len(source) for source in sources], matrix_cuts(width)
        ),
        grid=(1,),
        in_specs=[whole_spec(array.shape) for array in arrays] + in_any(len(riders)),
        out_specs=[
            pl.BlockSpec((1, rows, width), lambda *_: (layer, 0, 0)),
            whole_spec((1, rows, 128)),
            whole_spec((1, 1, width)),
        ],
        out_shape=[
            jax.ShapeDtypeStruct(shape, F32),
            jax.ShapeDtypeStruct((1, rows, 128), F32),
            jax.ShapeDtypeStruct((1, 1, width), F32),
        ],
        input_output_aliases={len(arrays): 0} if riders else {},
        compiler_params=pltpu.CompilerParams(vmem_limit_bytes=VMEM_BYTES),
        cost_estimate=cost(2),
        name="gradient",
    )(*arrays, *riders)


def layer_spec(*shape):
    return pl.BlockSpec((1, *shape), lambda i: (i, 0, 0))


def run_squares(grads, master, row_inverse, col_inverse):
    layers, rows, width = grads.shape
    return pl.pallas_call(
        functools.partial(square_kernel, matrix_cuts(width)),
        grid=(layers,),
        in_specs=[
            layer_spec(rows, width),
            layer_spec(rows, width),
            layer_spec(rows, 4),
            layer_spec(1, width),
        ],
        out_specs=layer_spec(8, 128),
        out_shape=jax.ShapeDtypeStruct((layers, 8, 128), F32),
        compiler_params=pltpu.CompilerParams(vmem_limit_bytes=VMEM_BYTES),
        cost_estimate=cost(2),
        name="squares",
    )(grads, master, row_inverse, col_inverse)


def run_update(grads, master, row_inverse, col_inverse, factor):
    layers, rows, width = grads.shape
    return pl.pallas_call(
        functools.partial(update_kernel, matrix_cuts(width)),
        grid=(layers,),
        in_specs=[
            layer_spec(rows, width),
            layer_spec(rows, width),
            layer_spec(rows, 4),
            layer_spec(1, width),
            layer_spec(1, 4),
        ],
        out_specs=[layer_spec(rows, width)] * 2,
        out_shape=[
            jax.ShapeDtypeStruct(grads.shape, F32),
            jax.ShapeDtypeStruct(grads.shape, BF16),
        ],
        compiler_params=pltpu.CompilerParams(vmem_limit_bytes=VMEM_BYTES),
        cost_estimate=cost(2),
        name="update",
    )(grads, master, row_inverse, col_inverse, factor)


def example_kernel(layers, sequences, scalars, *refs):
    out = refs[-1]
    out[...] = jnp.zeros_like(out)
    seq_place = scalars[0]
    for place in range(FF // D):

        @pl.when(seq_place == place)
        def _():
            for i in range(layers):
                for s in range(sequences):
                    of_mlp, of_attention = refs[2 * (i * sequences + s) : 2 * (i * sequences + s) + 2]
                    row = slice(s, s + 1)
                    at = SMALL * i

                    def put(first, values):
                        width = values.shape[1]
                        out[row, at + first : at + first + width] = values

                    put(0, of_attention[0:1])
                    put(D, of_attention[1:2])
                    put(2 * D, of_mlp[0:1])
                    put(3 * D, of_mlp[1:2])
                    if place == 0:
                        put(7 * D, of_mlp[3:4])
                        put(8 * D + FF, of_mlp[3:4])
                    wide = 3 * D // (FF // D)
                    first = 4 * D + wide * place
                    for part in natural_heads(of_attention[2:3, :wide]):
                        put(first, part)
                        first += part.shape[1]
                    put(8 * D + D * place, of_mlp[2:3])


def run_example(scalars, sums, sequences):
    arrays = [array for layer in sums for pair in layer for array in pair]
    return pl.pallas_call(
        functools.partial(example_kernel, len(sums), sequences),
        grid_spec=pltpu.PrefetchScalarGridSpec(
            num_scalar_prefetch=1,
            grid=(1,),
            in_specs=[whole_spec(array.shape) for array in arrays],
            out_specs=whole_spec((sequences, len(sums) * SMALL)),
        ),
        out_shape=jax.ShapeDtypeStruct((sequences, len(sums) * SMALL), F32),
        cost_estimate=cost(1),
        name="examples",
    )(scalars, *arrays)


def small_kernel(length, totals, examples, state, params, grads, moments, new, scores):
    layers = state.shape[0]
    lane = lax.broadcasted_iota(jnp.int32, scores.shape, 1)
    query, each = totals[1:2], examples[...]
    norm = jnp.sum(each * each, axis=1, keepdims=True) / (layers * SMALL * length)
    spread = length * layers * SMALL * (jnp.mean(query * query, axis=1, keepdims=True) + 1e-06)
    influence = jnp.sum(each * query, axis=1, keepdims=True) / jnp.sqrt(spread)
    scores[...] = jnp.where(lane == 0, norm, influence)
    edges = [0, D, 2 * D, 3 * D, 4 * D, 7 * D, 8 * D, 8 * D + FF, SMALL]
    for i in range(layers):
        row = slice(i, i + 1)
        gradient = totals[0:1, SMALL * i : SMALL * (i + 1)]
        grads[row] = gradient
        moment = DECAY * state[row] + (1.0 - DECAY) * (gradient * gradient + EPS_SQUARE)
        moments[row] = moment
        for first, end in zip(edges, edges[1:]):
            columns = slice(first, end)
            update = gradient[:, columns] * lax.rsqrt(moment[:, columns])
            old = params[row, columns]
            rms = jnp.sqrt(jnp.mean(update * update, axis=1, keepdims=True))
            old_rms = jnp.sqrt(jnp.mean(old * old, axis=1, keepdims=True))
            new[row, columns] = old - RATE * old_rms * (update / jnp.maximum(1.0, rms))


def run_small(length, totals, examples, state, params):
    arrays = [totals, examples, state, params]
    shapes = [state.shape] * 3 + [(examples.shape[0], 128)]
    return pl.pallas_call(
        functools.partial(small_kernel, length),
        grid=(1,),
        in_specs=[whole_spec(array.shape) for array in arrays],
        out_specs=[whole_spec(shape) for shape in shapes],
        out_shape=[jax.ShapeDtypeStruct(shape, F32) for shape in shapes],
        cost_estimate=cost(2),
        name="small_vectors",
    )(*arrays)


def pass_through_kernel(*refs):
    del refs


def after(values, *others):
    return pl.pallas_call(
        pass_through_kernel,
        in_specs=in_any(1 + len(others)),
        out_specs=pl.BlockSpec(memory_space=pl.ANY),
        out_shape=jax.ShapeDtypeStruct(values.shape, values.dtype),
        input_output_aliases={0: 0},
        name="after",
    )(values, *others)


def out_rows(columns, dp_place, seq_place):
    stacked = jnp.zeros((D, columns[0].shape[1]), BF16)
    for column, place in zip(columns, piece_places(len(columns), dp_place)):
        stacked = lax.dynamic_update_slice(stacked, column, (place * column.shape[0], 0))
    size = lax.axis_size("seq")
    blocks = stacked.reshape(size, D // size, -1)
    return jnp.concatenate(exchange_blocks(blocks, seq_place), axis=1)


def on_device(block_in, cotangent, labels, master, small_params, row_state, col_state, small_state):
    sequences, chunk = block_in.shape[:2]
    group_count = lax.axis_size("seq")
    seq_place, dp_place = lax.axis_index("seq"), lax.axis_index("dp")
    length = chunk * group_count
    flags = (labels == 0).astype(jnp.int32)
    place = jnp.concatenate(
        [jnp.stack([seq_place % 2, seq_place // 2, dp_place]).astype(jnp.int32), flags]
    )
    train_flag = flags.astype(F32)
    scalars = jnp.concatenate(
        [jnp.stack([dp_place % 2, seq_place]).astype(jnp.int32), flags]
    )
    query_flag = 1.0 - train_flag
    wide, out_wide, quarter = 3 * D // group_count, D // group_count, FF // group_count
    cuts = matrix_cuts(master.shape[2])
    split = lax.axis_size("dp") == 8
    x_bit, z_place = dp_place % 2, dp_place // 2
    tables = rotary_tables(length)

    def normalise(stream):
        scaled, inverse = apply_layer_norm(stream)
        low_scaled = scaled.astype(BF16)
        return (scaled, inverse), low_scaled

    stream = both_halves(block_in).astype(F32)
    norm, low_scaled = normalise(stream)
    near = swap(low_scaled, "seq", 1)
    chunks = [((low_scaled, s), (near, s)) for s in range(sequences)]

    low = master.astype(BF16)
    rows_of = [
        jnp.concatenate([heads_together(low[i, :, : cuts[1]]), low[i, :, cuts[1] :]], axis=1)
        for i in range(LAYERS)
    ]
    pieces = gather_rows(rows_of[0])
    whole_one = lax.all_gather(after(rows_of[1], *pieces[4:5]), "dp", axis=0, tiled=True)

    def weight_of(pieces):
        columns = [piece[:, wide : wide + out_wide] for piece in pieces]
        return out_rows(columns, dp_place, seq_place), pieces

    weights = [weight_of(pieces)]
    vectors, params = [], []
    for i in range(LAYERS):
        param = unpack(small_params[i])
        params.append(param)
        bias_qkv = heads_together(lax.dynamic_slice_in_dim(param[4], seq_place * wide, wide))
        bias_up = lax.dynamic_slice_in_dim(param[6], seq_place * quarter, quarter)
        vectors.append(
            jnp.stack(
                [
                    *param[:4],
                    jnp.pad(bias_up, (0, D - quarter)),
                    jnp.pad(bias_qkv, (0, D - wide)),
                    jnp.zeros((D,), F32),
                    jnp.zeros((D,), F32),
                ]
            )
        )

    streams = [stream[s] for s in range(sequences)]
    norms, saved_all = [[(norm[0][s], norm[1][s]) for s in range(sequences)]], []
    open_sum = None

    def close_sum(behind):
        nonlocal open_sum
        total, received, finish = open_sum
        open_sum = None
        finish(finish_sum(total, after(received, behind)))

    def open_exchange(keep, send, behind, finish):
        nonlocal open_sum
        if open_sum is not None:
            send = after(send, open_sum[1])
            close_sum(behind)
        total, low_total = core_sum(keep, send)
        open_sum = (total, swap(low_total, "seq", 2), finish)
        return [low_total]

    riders = []
    for i in range(LAYERS):
        last = i == LAYERS - 1
        saved_all.append([])
        next_chunks, next_norms = [], []
        bias = params[i][5] + params[i][7]

        def finish_stream(s, bias, next_chunks, next_norms, summed):
            streams[s] = streams[s] + summed + bias
            norm, low_scaled = normalise(streams[s])
            next_norms.append(norm)
            next_chunks.append(((low_scaled, None), (swap(low_scaled, "seq", 1), None)))

        for s in range(sequences):
            keep, send, *saved = run_forward(
                place, chunks[s], vectors[i], tables, weights[i], riders
            )
            saved_all[i].append(saved)
            if last:
                if open_sum is not None:
                    send = after(send, open_sum[1])
                    close_sum(saved[0])
                streams[s] = streams[s][0] + own_sum_over_seq(keep, send) + bias
                continue
            riders = open_exchange(
                keep,
                send,
                saved[0],
                functools.partial(finish_stream, s, bias, next_chunks, next_norms),
            )
        if i == 0:
            weights.append(weight_of([after(whole_one, saved_all[0][0][0])]))
        if last:
            break
        chunks = next_chunks
        norms.append(next_norms)
    block_out = jnp.stack(streams).astype(BF16)

    low_grad = both_halves(cotangent)
    near = swap(low_grad, "seq", 1)
    chunks = [((low_grad, s), (near, s)) for s in range(sequences)]
    grads = [low_grad[s].astype(F32) for s in range(sequences)]
    sources, sums = [None] * LAYERS, [None] * LAYERS
    riders, later, latest = [], [], []
    for i in reversed(range(LAYERS)):
        last = i == 0
        xhats, qks, vals, atts, lses, hids, slopes = zip(*saved_all[i])
        mlp, attention, next_chunks = [], [], []

        def finish_grad(s, norm, next_chunks, summed):
            grads[s] = grads[s] + norm_back(summed, *norm)
            low_grad = grads[s].astype(BF16)
            next_chunks.append(((low_grad, None), (swap(low_grad, "seq", 1), None)))

        for s in range(sequences):
            mlp.append(
                run_mlp_backward(
                    place, s, chunks[s], vectors[i], weights[i], xhats[s], slopes[s], atts[s], riders
                )
            )
            riders = [mlp[s][3]]
            if open_sum is not None:
                close_sum(mlp[s][3])
            if s == 0:
                riders += later
        outward = sum(out[4] for out in mlp).astype(BF16)
        blocks = outward.reshape(out_wide, group_count, out_wide).transpose(1, 0, 2)
        outward = jnp.concatenate(exchange_blocks(blocks, seq_place), axis=0)
        groups = [xhats, [out[0] for out in mlp], [out[1] for out in mlp], hids]
        both = run_mlp_outer(scalars, vectors[i], groups, split, [] if last else [block_out])
        if split:
            total_b = pair_total(*both)
            part_b = scatter_along_z(total_b)
        else:
            part_b = lax.psum_scatter(both[0], "dp", scatter_dimension=0, tiled=True)
        riders = both[-1:]
        for s in range(sequences):
            keep, send, grad_joined, sums_t = run_attention_backward(
                place,
                mlp[s][0],
                vectors[i],
                tables,
                weights[i],
                xhats[s],
                qks[s],
                vals[s],
                lses[s],
                mlp[s][2],
                riders,
            )
            attention.append((grad_joined, sums_t))
            if last:
                riders = latest
                norm = norms[i][s]
                grad_scaled = own_sum_over_seq(keep, send)
                grads[s] = grads[s][0] + norm_back(grad_scaled, norm[0][0], norm[1][0])
            else:
                riders = open_exchange(
                    keep,
                    send,
                    grad_joined,
                    functools.partial(finish_grad, s, norms[i][s], next_chunks),
                )
        if split:
            riders = ([] if last else riders) + [total_b]
        groups = [xhats, [out[0] for out in attention]]
        rest = run_qkv_outer(scalars, vectors[i], groups, outward, split, riders)
        if not split:
            part_a = [lax.psum_scatter(rest[0], "dp", scatter_dimension=0, tiled=True)]
        elif last:
            own_a, parts_a = pair_sum(*rest, z_place)
            part_a = [own_a, *exchange_parts(parts_a)]
        else:
            total_a = pair_total(*rest)
            part_a = [scatter_along_z(total_a)]
            later, latest = [part_b, total_a], part_a
        sources[i] = [[part_b], part_a]
        riders = rest[:1]
        chunks = next_chunks
        sums[i] = [(out[3], other[1]) for out, other in zip(mlp, attention)]
    grad_stream = jnp.stack(grads)

    reduced_all, row_sums, col_sums = None, [None] * LAYERS, [None] * LAYERS
    for i in reversed(range(LAYERS)):
        reduced_all, row_sums[i], col_sums[i] = run_gradient(
            sources[i], i, master.shape, reduced_all
        )
    matrix_width = jnp.array([3 * D, D, FF, FF], F32)
    row_part = jnp.concatenate(row_sums, axis=0)[:, :, :4].transpose(0, 2, 1)
    col_part = jnp.concatenate(
        [
            jnp.concatenate(col_sums, axis=0)[:, 0],
            jnp.sum(row_part, axis=2),
            jnp.sum(row_state, axis=2),
        ],
        axis=1,
    )
    examples = after(run_example(scalars[1:2], sums, sequences), row_sums[0])
    dp_bits, seq_bits = [], []
    for axis, bits in (("dp", dp_bits), ("seq", seq_bits)):
        bits += [(axis, 1 << k) for k in range(lax.axis_size(axis).bit_length() - 1)]
    first_steps = max(len(seq_bits), len(dp_bits))
    small = examples
    small_steps = [*seq_bits, None, *dp_bits]

    def small_step():
        nonlocal small, examples, small_steps
        step, *small_steps = small_steps
        if step is None:
            examples = small
            small = jnp.stack(
                [
                    jnp.sum(train_flag[:, None] * examples, axis=0),
                    jnp.sum(query_flag[:, None] * examples, axis=0),
                ]
            )
            step, *small_steps = small_steps
        sent = small.astype(BF16)
        return sent, swap(sent, *step)

    def together(values):
        nonlocal small
        received = [swap(value, *step) for value, step in values]
        sent = None
        if small_steps:
            sent, small_in = small_step()
            received.append(small_in)
        if len(received) > 1:
            received = [
                after(value, *[other for other in received if other is not value])
                for value in received
            ]
        if sent is not None:
            small = sent.astype(F32) + received.pop().astype(F32)
        return [value + other for (value, _), other in zip(values, received)]

    for k in range(first_steps):
        now = []
        if k < len(seq_bits):
            now.append((row_part, seq_bits[k]))
        if k < len(dp_bits):
            now.append((col_part, dp_bits[k]))
        *rest_sums, last_sum = together(now)
        if k < len(seq_bits) and k < len(dp_bits):
            (row_part,), col_part = rest_sums, last_sum
        elif k < len(dp_bits):
            col_part = last_sum
        else:
            row_part = last_sum
    fresh_row_moments = DECAY * row_state + (1.0 - DECAY) * (
        row_part / matrix_width[None, :, None]
    )
    col_stats = DECAY * col_state + (1.0 - DECAY) * (col_part[:, : cuts[4]] / D)
    square_part, state_sum = col_part[:, cuts[4] : cuts[4] + 4], col_part[:, cuts[4] + 4 :]
    row_inverse = lax.rsqrt(fresh_row_moments).transpose(0, 2, 1)
    col_inverse = lax.rsqrt(col_stats)[:, None]
    square_sums = run_squares(reduced_all, master, row_inverse, col_inverse)
    group_sums = jnp.concatenate([square_sums[:, :2, :4], square_part[:, None]], axis=1)
    for step in seq_bits:
        (group_sums,) = together([(group_sums, step)])
    square_totals = group_sums[:, :2]
    for step in dp_bits:
        (square_totals,) = together([(square_totals, step)])
    while small_steps:
        together([])
    small_grads, small_moments, small_new, scores = run_small(
        length, small, examples, small_state, small_params
    )
    example_norms, influence = scores[:, 0], scores[:, 1]
    row_mean = (
        DECAY * state_sum + (1.0 - DECAY) * (group_sums[:, 2] / matrix_width[None, :])
    ) / D
    entry_count = D * matrix_width
    update_rms = jnp.sqrt(row_mean * square_totals[:, 0] / entry_count[None, :])
    weight_rms = jnp.sqrt(square_totals[:, 1] / entry_count[None, :])
    factor = RATE * weight_rms * jnp.sqrt(row_mean) / jnp.maximum(1.0, update_rms)
    new_master, new_low = run_update(
        reduced_all, master, row_inverse, col_inverse, factor[:, None]
    )
    return (
        block_out,
        grad_stream,
        example_norms,
        influence,
        reduced_all,
        fresh_row_moments,
        col_stats,
        new_master,
        new_low,
        small_grads,
        small_moments,
        small_new,
    )


def solution(mesh):
    placed = (
        P("dp", "seq", None),
        P("dp", "seq", None),
        P("dp"),
        P(None, "dp", "seq"),
        P(),
        P(None, None, "dp"),
        P(None, "seq"),
        P(),
    )
    return jax.shard_map(
        on_device,
        mesh=mesh,
        in_specs=placed,
        out_specs=(
            P("dp", "seq", None),
            P("dp", "seq", None),
            P("dp"),
            P("dp"),
            P(None, "dp", "seq"),
            P(None, None, "dp"),
            P(None, "seq"),
            P(None, "dp", "seq"),
            P(None, "dp", "seq"),
            P(),
            P(),
            P(),
        ),
        check_vma=False,
    )
```

```python
import functools

import jax
import numpy as np
import jax.numpy as jnp
from jax import lax
from jax.experimental import pallas as pl
from jax.experimental.pallas import tpu as pltpu
from jax.sharding import PartitionSpec as P

D = 768
HEADS = 12
FF = 3072
LAYERS = 2
HEAD_DIM = 64
ROT = 16
SMALL = 9984

EPS_NORM = 1e-05
EPS_SQUARE = 1e-30
RATE = 0.5
DECAY = 0.5
NEG_LARGE = -1e30
SCORE_SCALE = HEAD_DIM ** (-0.5)
CONTRACT_LAST = (((1,), (1,)), ((), ()))
CONTRACT_FIRST = (((0,), (0,)), ((), ()))
VMEM_BYTES = 24 * 1024 * 1024
BF16 = jnp.bfloat16
F32 = jnp.float32


def unpack(vector):
    return jnp.split(vector, [D, 2 * D, 3 * D, 4 * D, 7 * D, 8 * D, 8 * D + FF], axis=-1)


def apply_layer_norm(inputs):
    centred = inputs - jnp.mean(inputs, axis=-1, keepdims=True)
    variance = jnp.mean(centred * centred, axis=-1, keepdims=True)
    inverse = lax.rsqrt(variance + EPS_NORM)
    return (centred * inverse, inverse)


def norm_back(grad_scaled, scaled, inverse):
    mean_grad = jnp.mean(grad_scaled, axis=-1, keepdims=True)
    mean_cross = jnp.mean(grad_scaled * scaled, axis=-1, keepdims=True)
    return (grad_scaled - mean_grad - scaled * mean_cross) * inverse


def rotary_tables(length):
    halfway = ROT // 2
    frequency = 10000.0 ** (-2.0 * np.arange(halfway) / ROT)
    angles = np.arange(length)[:, None] * frequency[None, :]
    cosine, sine = np.cos(angles), np.sin(angles)
    rest = np.ones((length, HEAD_DIM - ROT))
    none = np.zeros((length, halfway))
    keep = np.concatenate([cosine, cosine, rest], axis=1)
    ahead = np.concatenate([-sine, none, 0.0 * rest], axis=1)
    behind = np.concatenate([none, sine, 0.0 * rest], axis=1)
    return tuple(
        jnp.asarray(np.concatenate([table, table], axis=1), F32) for table in (keep, ahead, behind)
    )


def swap(values, axis, bits):
    size = lax.axis_size(axis)
    return lax.ppermute(values, axis, [(i, i ^ bits) for i in range(size)])


def sum_pairwise(values, axis, wire=F32):
    bits = 1
    while bits < lax.axis_size(axis):
        sent = values.astype(wire)
        values = sent.astype(F32) + swap(sent, axis, bits).astype(F32)
        bits *= 2
    return values


def both_halves(own):
    return jnp.stack([own, swap(own, "seq", 2)], axis=-3)


def core_sum(keep, send):
    received = swap(send, "seq", 1)
    return keep, received, (keep + received.astype(F32)).astype(BF16)


def gather_rows(rows):
    if lax.axis_size("dp") != 8:
        return [lax.all_gather(rows, "dp", axis=0, tiled=True)]
    pieces = []
    for k in range(4):
        pieces += [rows, swap(rows, "dp", 1)]
        if k < 3:
            rows = lax.ppermute(rows, "dp", [(i, (i + 2) % 8) for i in range(8)])
    return pieces


def piece_places(count, dp_place):
    if count == 1:
        return [0]
    return [(dp_place + 8 - 2 * (k // 2)) % 8 ^ (k % 2) for k in range(count)]


def pair_sum(keep, send, z_place):
    summed = keep + swap(send, "dp", 1).astype(F32)
    own = lax.dynamic_index_in_dim(summed, z_place, 0, keepdims=False)
    return own, [
        lax.dynamic_index_in_dim(summed, z_place ^ k, 0, keepdims=False).astype(BF16)
        for k in range(1, summed.shape[0])
    ]


def pair_total(keep, send):
    return (keep + swap(send, "dp", 1).astype(F32)).astype(BF16).reshape(-1, keep.shape[-1])


def scatter_along_z(total):
    groups = [[2 * z + x for z in range(4)] for x in range(2)]
    return lax.psum_scatter(
        total, "dp", scatter_dimension=0, tiled=True, axis_index_groups=groups
    )


def exchange_parts(parts):
    return [swap(part, "dp", 2 * (k + 1)) for k, part in enumerate(parts)]


def exchange_blocks(blocks, index):
    size = lax.axis_size("seq")
    received = []
    for k in range(size):
        block = lax.dynamic_index_in_dim(blocks, index ^ k, 0, keepdims=False)
        received.append(block if k == 0 else swap(block, "seq", k))
    return received


def heads_together(values):
    heads = values.shape[-1] // (3 * HEAD_DIM)
    lead = values.shape[:-1]
    by_head = values.reshape(*lead, heads, 3 * HEAD_DIM)
    return jnp.concatenate(
        [
            by_head[..., : 2 * HEAD_DIM].reshape(*lead, heads * 2 * HEAD_DIM),
            by_head[..., 2 * HEAD_DIM :].reshape(*lead, heads * HEAD_DIM),
        ],
        axis=-1,
    )


def heads_apart(values):
    heads = values.shape[-1] // (3 * HEAD_DIM)
    lead = values.shape[:-1]
    pairs, last = jnp.split(values, [heads * 2 * HEAD_DIM], axis=-1)
    return jnp.concatenate(
        [
            pairs.reshape(*lead, heads, 2 * HEAD_DIM),
            last.reshape(*lead, heads, HEAD_DIM),
        ],
        axis=-1,
    ).reshape(values.shape)


def halves(core_bit, chunk):
    own = pl.multiple_of(core_bit * chunk, chunk)
    return pl.ds(own, chunk), pl.ds(pl.multiple_of(chunk - own, chunk), chunk)


def place_tokens(dst, own, near, core_bit, y_here, chunk):
    at_own, at_near = halves(core_bit, chunk)
    dst[at_own] = own[y_here]
    dst[at_near] = near[y_here]


def spread_tokens(value, held, keep, send, core_bit, y_here, chunk):
    at_own, at_near = halves(core_bit, chunk)
    held[...] = value
    keep[pl.ds(y_here, 1)] = held[at_own][None]
    send[pl.ds(y_here, 1)] = held[at_near].astype(send.dtype)[None]


def gelu_and_slope(v):
    magnitude = jnp.abs(v) * 0.7071067811865476
    t = 1.0 / (1.0 + 0.3275911 * magnitude)
    falling = jnp.exp(-0.5 * v * v)
    poly = t * (
        0.254829592
        + t * (-0.284496736 + t * (1.421413741 + t * (-1.453152027 + t * 1.061405429)))
    )
    tail = 0.5 * poly * falling
    cdf = jnp.where(v >= 0.0, 1.0 - tail, tail)
    return v * cdf, cdf + v * falling * 0.3989422804014327


def weight_copies(dp_place, sources, targets, sems):
    copies = []
    for (pieces, first), target in zip(sources, targets):
        rows, width = pieces[0].shape[0], target.shape[1]
        for piece, place in zip(pieces, piece_places(len(pieces), dp_place)):
            offset = 0 if len(pieces) == 1 else pl.multiple_of(place * rows, 16)
            copies.append(
                pltpu.make_async_copy(
                    piece.at[:, pl.ds(first, width)],
                    target.at[pl.ds(offset, rows), :],
                    sems.at[len(copies)],
                )
            )
    return copies


def place_columns(whole, blocks, place):
    width = blocks[0].shape[1]
    seq_place = 2 * place[1] + place[0]
    for index in range(len(blocks)):

        @pl.when(seq_place == index)
        def _():
            for k, block in enumerate(blocks):
                at = width * (index ^ k)
                whole[:, at : at + width] = block[...]


def start_all(copies):
    for copy in copies:
        copy.start()


def wait_all(copies):
    for copy in copies:
        copy.wait()


def turn(pair, tables, sign):
    keep_tab, ahead_tab, behind_tab = tables
    ahead = pltpu.roll(pair, 2 * HEAD_DIM - ROT // 2, 1) * ahead_tab[...]
    behind = pltpu.roll(pair, ROT // 2, 1) * behind_tab[...]
    return pair * keep_tab[...] + sign * (ahead + behind)


def forward_kernel(counts, firsts, place, *refs):
    refs = list(refs)

    def take(count):
        taken, refs[:] = refs[:count], refs[count:]
        return taken

    own, near, vec = take(3)
    tables = take(3)
    blocks_out = take(4)
    pieces = [take(count) for count in counts]
    keep, send, xhat, qk, val, att, lse, hid, slope = refs[-16:-7]
    whole_a, whole_b, w_out, k_all, v_all, held, sems = refs[-7:]
    core_bit, y_bit, dp_place = place[0], place[1], place[2]
    step = pl.program_id(0)
    wide = 3 * val.shape[1]
    sources = list(zip(pieces, firsts))
    copies = weight_copies(dp_place, sources, [whole_a, whole_b], sems)

    @pl.when(step == 0)
    def _():
        start_all(copies)
        place_columns(w_out, blocks_out, place)

    chunk = own.shape[1]
    block = 2 * chunk
    y_here = step ^ y_bit
    place_tokens(xhat, own, near, core_bit, y_here, chunk)
    heads = val.shape[-1] // HEAD_DIM
    quarter = hid.shape[-1]
    row = lax.broadcasted_iota(jnp.int32, (block, block), 0)
    column = lax.broadcasted_iota(jnp.int32, (block, block), 1)
    lane = lax.broadcasted_iota(jnp.int32, (block, 128), 1)

    def attend(here, h, joined, log_sums):
        at_q, at_k = 2 * HEAD_DIM * h, 2 * HEAD_DIM * h + HEAD_DIM
        turned = turn(joined[:, at_q : at_k + HEAD_DIM], tables, 1.0)
        qk[:, at_q : at_k + HEAD_DIM] = turned.astype(BF16)
        k_all[h, block * here : block * (here + 1)] = turned[:, HEAD_DIM:].astype(BF16)
        first = 2 * HEAD_DIM * heads + HEAD_DIM * h
        v_all[h, block * here : block * (here + 1)] = joined[:, first : first + HEAD_DIM].astype(
            BF16
        )
        query = qk[:, at_q : at_q + HEAD_DIM] * jnp.asarray(SCORE_SCALE, BF16)
        scores = []
        for j in range(here + 1):
            part = lax.dot_general(
                query,
                k_all[h, block * j : block * (j + 1)],
                CONTRACT_LAST,
                preferred_element_type=F32,
            )
            if j == here:
                part = jnp.where(column <= row, part, NEG_LARGE)
            scores.append(part)
        largest = functools.reduce(
            jnp.maximum, [jnp.max(part, axis=-1, keepdims=True) for part in scores]
        )
        total = 0.0
        mixed = 0.0
        for j, part in enumerate(scores):
            exponent = jnp.exp(part - largest)
            total = total + jnp.sum(exponent, axis=-1, keepdims=True)
            mixed = mixed + jnp.dot(
                exponent.astype(BF16),
                v_all[h, block * j : block * (j + 1)],
                preferred_element_type=F32,
            )
        att[:, HEAD_DIM * h : HEAD_DIM * (h + 1)] = (mixed / total).astype(BF16)
        return jnp.where(lane == h, largest + jnp.log(total), log_sums)

    for here in range(2):

        @pl.when(step == here)
        def _():
            scaled = xhat[...].astype(F32)
            normed_one = (scaled * vec[0:1] + vec[1:2]).astype(BF16)
            normed_two = (scaled * vec[2:3] + vec[3:4]).astype(BF16)
            if here == 0:
                wait_all(copies)
            joined = (
                jnp.dot(normed_one, whole_a[:, :wide], preferred_element_type=F32) + vec[5:6, :wide]
            )
            val[...] = joined[:, 2 * HEAD_DIM * heads :].astype(BF16)
            hidden_pre = (
                jnp.dot(normed_two, whole_b[:, :quarter], preferred_element_type=F32)
                + vec[4:5, :quarter]
            )
            log_sums = jnp.zeros((block, 128), F32)
            for h in range(heads):
                log_sums = attend(here, h, joined, log_sums)
            lse[...] = log_sums.T[:8]
            hidden, gradient = gelu_and_slope(hidden_pre)
            hid[...] = hidden.astype(BF16)
            slope[...] = gradient.astype(BF16)
            partial = jnp.dot(att[...], w_out[...], preferred_element_type=F32) + lax.dot_general(
                hid[...], whole_b[:, quarter:], CONTRACT_LAST, preferred_element_type=F32
            )
            spread_tokens(partial, held, keep, send, core_bit, y_here, chunk)


def normalised(stream):
    centred = stream - jnp.mean(stream, axis=-1, keepdims=True)
    variance = jnp.mean(centred * centred, axis=-1, keepdims=True)
    inverse = lax.rsqrt(variance + EPS_NORM)
    return centred * inverse, inverse


def seq_sum(keep, near, across):
    return keep[...] + near[...].astype(F32) + across[...].astype(F32)


def finish_stream_kernel(keep, near, across, stream, bias, out, *low):
    value = stream[...].astype(F32) + seq_sum(keep, near, across) + bias[...]
    out[...] = value.astype(out.dtype)
    if low:
        low[0][...] = normalised(value)[0].astype(BF16)


def finish_grad_kernel(keep, near, across, grad, stream, out, *low):
    scaled, inverse = normalised(stream[...].astype(F32))
    back = norm_back(seq_sum(keep, near, across), scaled, inverse)
    value = grad[...].astype(F32) + back
    out[...] = value
    if low:
        low[0][...] = value.astype(BF16)


def add_up(sums, place_row, values):
    sums[place_row : place_row + 1, : values.shape[-1]] += jnp.sum(
        values.astype(F32), axis=0, keepdims=True
    )


def mlp_backward_kernel(count, first, sequence, n_before, n_outward, place, *refs):
    own, near, vec, xhat, slope, att = refs[:6]
    pieces = refs[6 : 6 + count]
    before = refs[6 + count : 6 + count + n_before]
    grad, grad_pre, grad_two, sums = refs[-7 - n_outward : -3 - n_outward]
    outward, (whole_b, product, sems) = refs[-3 - n_outward : -3], refs[-3:]
    core_bit, y_bit, dp_place = place[0], place[1], place[2]
    step = pl.program_id(0)
    copies = weight_copies(dp_place, [(pieces, first)], [whole_b], sems)

    @pl.when(step == 0)
    def _():
        start_all(copies)
        sums[...] = jnp.zeros_like(sums)

    chunk = own.shape[1]
    place_tokens(grad, own, near, core_bit, step ^ y_bit, chunk)

    @pl.when(step == 0)
    def _():
        wait_all(copies)

    quarter = slope.shape[-1]
    grad_hidden = jnp.dot(grad[...], whole_b[:, quarter:], preferred_element_type=F32)
    low_pre = (grad_hidden * slope[...].astype(F32)).astype(BF16)
    grad_pre[...] = low_pre
    normed = lax.dot_general(
        low_pre, whole_b[:, :quarter], CONTRACT_LAST, preferred_element_type=F32
    )
    grad_two[...] = (normed * vec[2:3]).astype(BF16)
    add_up(sums, 0, normed * xhat[...].astype(F32))
    add_up(sums, 1, normed)
    add_up(sums, 2, low_pre)
    add_up(sums, 3, grad[...])
    kept = jnp.where(place[3 + sequence] > 0, grad[...], jnp.zeros_like(grad))
    part = lax.dot_general(att[...], kept, CONTRACT_FIRST, preferred_element_type=F32)

    @pl.when(step == 0)
    def _():
        product[...] = part + before[0][...] if before else part

    @pl.when(step != 0)
    def _():
        product[...] += part
        if len(outward) == 1:
            outward[0][...] = product[...]
            return
        width = outward[0].shape[1]
        for index in range(len(outward)):

            @pl.when(2 * y_bit + core_bit == index)
            def _():
                for k, block in enumerate(outward):
                    at = width * (index ^ k)
                    block[...] = product[:, at : at + width].astype(BF16)


def attention_backward_kernel(count, first, place, *refs):
    refs = list(refs)

    def take(number):
        taken, refs[:] = refs[:number], refs[number:]
        return taken

    grad, vec = take(2)
    tables = take(3)
    blocks_out = take(4)
    xhat, qk, val, lse, grad_two = take(5)
    pieces = take(count)
    keep, send, grad_joined, sums = refs[-10:-6]
    whole_a, w_out, dk_all, dv_all, held, sems = refs[-6:]
    core_bit, y_bit, dp_place = place[0], place[1], place[2]
    step = 1 - pl.program_id(0)
    copies = weight_copies(dp_place, [(pieces, first)], [whole_a], sems)

    @pl.when(step == 1)
    def _():
        start_all(copies)
        sums[...] = jnp.zeros_like(sums)
        place_columns(w_out, blocks_out, place)

    block = grad.shape[0]
    chunk = block // 2
    heads = val.shape[-1] // HEAD_DIM
    row = lax.broadcasted_iota(jnp.int32, (block, block), 0)
    column = lax.broadcasted_iota(jnp.int32, (block, block), 1)

    def attend_back(here, h, near_grad):
        at_q, at_k = 2 * HEAD_DIM * h, 2 * HEAD_DIM * h + HEAD_DIM
        at_v = 2 * HEAD_DIM * heads + HEAD_DIM * h
        query = qk[block * here : block * (here + 1), at_q:at_k]
        query = query * jnp.asarray(SCORE_SCALE, BF16)
        log_row = lse[h : h + 1]
        probs, grad_probs, keys = [], [], []
        delta = 0.0
        for j in range(here + 1):
            key = qk[block * j : block * (j + 1), at_k : at_k + HEAD_DIM]
            value = val[block * j : block * (j + 1), HEAD_DIM * h : HEAD_DIM * (h + 1)]
            scores = lax.dot_general(key, query, CONTRACT_LAST, preferred_element_type=F32)
            prob = jnp.exp(scores - log_row)
            if j == here:
                prob = jnp.where(row <= column, prob, 0.0)
            grad_prob = lax.dot_general(
                value, near_grad, CONTRACT_LAST, preferred_element_type=F32
            )
            delta = delta + jnp.sum(prob * grad_prob, axis=0, keepdims=True)
            probs.append(prob)
            grad_probs.append(grad_prob)
            keys.append(key)
        dq = 0.0
        for j in range(here + 1):
            grad_score = (probs[j] * (grad_probs[j] - delta)).astype(BF16)
            dk = jnp.dot(grad_score, query, preferred_element_type=F32)
            dv = jnp.dot(probs[j].astype(BF16), near_grad, preferred_element_type=F32)
            dq = dq + lax.dot_general(
                grad_score, keys[j], CONTRACT_FIRST, preferred_element_type=F32
            )
            if j < here:
                dk_all[h], dv_all[h] = dk, dv
            elif here == 0:
                dk, dv = dk + dk_all[h], dv + dv_all[h]
        pair = jnp.concatenate([dq * SCORE_SCALE, dk], axis=1)
        grad_joined[:, at_q : at_q + 2 * HEAD_DIM] = turn(pair, tables, -1.0).astype(BF16)
        grad_joined[:, at_v : at_v + HEAD_DIM] = dv.astype(BF16)

    for here in (1, 0):

        @pl.when(step == here)
        def _():
            grad_att = lax.dot_general(
                grad[...], w_out[...], CONTRACT_LAST, preferred_element_type=F32
            ).astype(BF16)
            for h in range(heads):
                attend_back(here, h, grad_att[:, HEAD_DIM * h : HEAD_DIM * (h + 1)])
            if here == 1:
                wait_all(copies)
            normed = lax.dot_general(
                grad_joined[...],
                whole_a[:, : grad_joined.shape[1]],
                CONTRACT_LAST,
                preferred_element_type=F32,
            )
            spread_tokens(
                normed * vec[0:1] + grad_two[...].astype(F32),
                held,
                keep,
                send,
                core_bit,
                step ^ y_bit,
                chunk,
            )
            add_up(sums, 0, normed * xhat[...].astype(F32))
            add_up(sums, 1, normed)
            add_up(sums, 2, grad_joined[...])


def fetch(sources, targets, sems):
    copies = [
        pltpu.make_async_copy(source, target, sems.at[k])
        for k, (source, target) in enumerate(zip(sources, targets))
    ]
    start_all(copies)
    return copies


def outer_sum(flags, pairs):
    total = 0.0
    for flag, pair in zip(flags, pairs):
        left, right = pair()
        kept = jnp.where(flag > 0, right, jnp.zeros_like(right))
        total = total + lax.dot_general(left, kept, CONTRACT_FIRST, preferred_element_type=F32)
    return total


def store_rows(value, outs, first, x_bit):
    columns = pl.ds(first, value.shape[1])
    if len(outs) == 1:
        outs[0][:, columns] = value.astype(BF16)
        return
    keep, send = outs
    rows = keep.shape[1]
    for bit in (0, 1):

        @pl.when(x_bit == bit)
        def _():
            for z in range(keep.shape[0]):
                at = rows * (2 * z + bit)
                to = rows * (2 * z + 1 - bit)
                keep[z, :, columns] = value[at : at + rows]
                send[z, :, columns] = value[to : to + rows].astype(BF16)


def mlp_outer_kernel(count, n_outs, scalars, vec, *refs):
    sources, outs = refs[: 4 * count], refs[-n_outs - 4 * count - 1 : -4 * count - 1]
    held, sems = refs[-4 * count - 1 : -1], refs[-1]
    copies = fetch(sources, held, sems)
    x_bit, flags = scalars[0], [scalars[2 + s] for s in range(count)]

    def ready(k):
        copies[k].wait()
        return held[k][...]

    def up(s):
        def pair():
            xhat, grad_pre = ready(4 * s), ready(4 * s + 1)
            return (xhat.astype(F32) * vec[2:3] + vec[3:4]).astype(BF16), grad_pre

        return pair

    def down(s):
        return lambda: (ready(4 * s + 2), ready(4 * s + 3))

    store_rows(outer_sum(flags, [up(s) for s in range(count)]), outs, 0, x_bit)
    store_rows(
        outer_sum(flags, [down(s) for s in range(count)]), outs, held[3].shape[1], x_bit
    )


def qkv_outer_kernel(count, n_blocks, n_outs, scalars, vec, *refs):
    sources, blocks = refs[: 2 * count], refs[2 * count : 2 * count + n_blocks]
    held, outward, sems = refs[-2 * count - 2 : -2], refs[-2], refs[-1]
    outs = refs[-2 * count - 2 - n_outs : -2 * count - 2]
    copies = fetch(sources, held, sems)
    x_bit, flags = scalars[0], [scalars[2 + s] for s in range(count)]

    def pair_of(s):
        def pair():
            copies[2 * s].wait()
            copies[2 * s + 1].wait()
            normed = held[2 * s][...].astype(F32) * vec[0:1] + vec[1:2]
            return normed.astype(BF16), held[2 * s + 1][...]

        return pair

    rows = blocks[0].shape[0]
    for k, block in enumerate(blocks):
        outward[pl.ds(pl.multiple_of((scalars[1] ^ k) * rows, 16), rows)] = block[...]
    wide = held[1].shape[1]
    store_rows(outward[...].astype(F32), outs, wide, x_bit)
    store_rows(outer_sum(flags, [pair_of(s) for s in range(count)]), outs, 0, x_bit)


def natural_heads(values):
    heads = values.shape[1] // (3 * HEAD_DIM)
    parts = []
    for h in range(heads):
        parts.append(values[:, 2 * HEAD_DIM * h : 2 * HEAD_DIM * (h + 1)])
        at = 2 * HEAD_DIM * heads + HEAD_DIM * h
        parts.append(values[:, at : at + HEAD_DIM])
    return parts


def matrix_cuts(width):
    unit = width // 12
    return [0, 3 * unit, 4 * unit, 8 * unit, width]


def gradient_kernel(counts, cuts, *refs):
    refs = list(refs)
    row_state, (grads, row_sums, col_sums) = refs[sum(counts)], refs[-3:]
    parts = []
    for count in counts:
        taken, refs[:] = refs[:count], refs[count:]
        parts.append(sum(ref[...].astype(F32) for ref in taken))
    both, rest = parts
    at = 0
    for part in natural_heads(rest[:, : cuts[1]]):
        grads[0, :, at : at + part.shape[1]] = part
        at += part.shape[1]
    grads[0, :, cuts[1] : cuts[2]] = rest[:, cuts[1] :]
    grads[0, :, cuts[2] :] = both
    whole = grads[0]
    squares = whole * whole + EPS_SQUARE
    by_column = jnp.sum(squares, axis=0, keepdims=True)
    lanes = whole.shape[1] // 128
    row = lax.broadcasted_iota(jnp.int32, (whole.shape[0], 128), 1)
    lane = lax.broadcasted_iota(jnp.int32, (1, 128), 1)
    by_row = jnp.zeros((whole.shape[0], 128), F32)
    for m in range(4):
        total = jnp.sum(squares[:, cuts[m] : cuts[m + 1]], axis=1, keepdims=True)
        by_row = jnp.where(row == m, total, by_row)
    row_sums[0] = by_row.T[:8]
    totals = jnp.sum(by_row, axis=0, keepdims=True)
    states = jnp.sum(row_state[0], axis=1, keepdims=True)
    for m in range(4):
        totals = jnp.where(lane == 4 + m, states[m : m + 1], totals)
    col_sums[0] = jnp.zeros_like(col_sums[0])
    for k in range(lanes):
        col_sums[0, k : k + 1] = by_column[:, 128 * k : 128 * (k + 1)]
    col_sums[0, lanes : lanes + 1] = totals


def in_a_row(rows):
    return jnp.concatenate([rows[k : k + 1] for k in range(rows.shape[0])], axis=1)


def upright(rows):
    padded = jnp.concatenate([rows, jnp.zeros((4, rows.shape[1]), F32)], axis=0)
    spare = -rows.shape[1] % 128
    if spare:
        padded = jnp.concatenate([padded, jnp.zeros((8, spare), F32)], axis=1)
    return padded.T[: rows.shape[1]]


def scaled_update(grads, row_inverse, col_inverse, cuts, i, m):
    columns = slice(cuts[m], cuts[m + 1])
    return grads[i, :, columns] * row_inverse[:, m : m + 1] * col_inverse[:, columns]


def square_kernel(cuts, grads, master, rows, cols, row_state, col_state, fresh, stats, sums):
    layers = grads.shape[0]
    lanes = cuts[4] // 128
    lane = lax.broadcasted_iota(jnp.int32, (1, 128), 1)
    matrix = lax.broadcasted_iota(jnp.int32, (4, 1), 0)
    widths = jnp.where(matrix == 0, 3.0 * D, jnp.where(matrix == 1, 1.0 * D, 1.0 * FF))
    sums[...] = jnp.zeros_like(sums)
    for i in range(layers):
        fresh[i] = DECAY * row_state[i] + (1.0 - DECAY) * (rows[i, :4] / widths)
        stats[i : i + 1] = DECAY * col_state[i : i + 1] + (1.0 - DECAY) * (
            in_a_row(cols[i, :lanes]) / D
        )
        row_inverse = upright(lax.rsqrt(fresh[i]))
        col_inverse = lax.rsqrt(stats[i : i + 1])
        result = jnp.zeros((1, 128), F32)
        for m in range(4):
            update = scaled_update(grads, row_inverse, col_inverse, cuts, i, m)
            old = master[i, :, cuts[m] : cuts[m + 1]]
            for at, values in ((0, update), (4, old)):
                total = jnp.sum(
                    jnp.sum(values * values, axis=0, keepdims=True), axis=1, keepdims=True
                )
                result = jnp.where(lane == at + m, total, result)
        sums[i : i + 1] = result
        sums[layers + i : layers + i + 1] = cols[i, lanes : lanes + 1]


def update_kernel(cuts, grads, master, fresh, stats, sums, row_sums, new, new_low):
    layers = grads.shape[0]
    for i in range(layers):
        row_inverse = upright(lax.rsqrt(fresh[i]))
        col_inverse = lax.rsqrt(stats[i : i + 1])
        for m, width in enumerate((3.0 * D, 1.0 * D, 1.0 * FF, 1.0 * FF)):
            square_total = row_sums[layers + i : layers + i + 1, m : m + 1]
            state_total = row_sums[2 * layers + i : 2 * layers + i + 1, 4 + m : 5 + m]
            row_mean = (DECAY * state_total + (1.0 - DECAY) * (square_total / width)) / D
            update_rms = jnp.sqrt(row_mean * sums[i : i + 1, m : m + 1] / (D * width))
            weight_rms = jnp.sqrt(sums[i : i + 1, 4 + m : 5 + m] / (D * width))
            factor = RATE * weight_rms * jnp.sqrt(row_mean) / jnp.maximum(1.0, update_rms)
            columns = slice(cuts[m], cuts[m + 1])
            update = scaled_update(grads, row_inverse, col_inverse, cuts, i, m)
            value = master[i, :, columns] - factor * update
            new[i, :, columns] = value
            new_low[i, :, columns] = value.astype(BF16)


def whole_spec(shape):
    return pl.BlockSpec(shape, lambda *_: (0,) * len(shape))


def in_any(count):
    return [pl.BlockSpec(memory_space=pl.ANY)] * count


def far(arrays):
    return [pltpu.with_memory_space_constraint(array, pltpu.HBM) for array in arrays]


def cost(micros):
    return pl.CostEstimate(
        flops=int(micros * 10**9), bytes_accessed=int(micros * 10**6), transcendentals=0
    )


def chunk_specs(chunks):
    specs = []
    for array, place in chunks:
        if place is None:
            specs.append(whole_spec(array.shape))
        else:
            specs.append(
                pl.BlockSpec((None, *array.shape[1:]), lambda *_, place=place: (place, 0, 0, 0))
            )
    return specs


def rows_spec(rows, width, block_of):
    return pl.BlockSpec((rows, width), lambda t, *_: (block_of(t), 0))


def run_forward(place, chunks, vec, tables, weight, riders=()):
    blocks_out, sources = weight
    chunk = chunks[0][0].shape[-2]
    block, length = 2 * chunk, 4 * chunk
    counts = [len(pieces) for pieces, _ in sources]
    firsts = [first for _, first in sources]
    pieces = [piece for pieces, _ in sources for piece in pieces]
    count = len(pieces)
    out_wide = blocks_out[0].shape[0]
    heads = out_wide // HEAD_DIM
    wide = 3 * out_wide
    quarter = FF * out_wide // D

    def same(t):
        return t

    widths = [
        (D, BF16),
        (2 * out_wide, BF16),
        (out_wide, BF16),
        (out_wide, BF16),
        (quarter, BF16),
        (quarter, BF16),
    ]
    shapes = [pltpu.HBM((length, width), kind) for width, kind in widths]
    specs = [rows_spec(block, width, same) for width, _ in widths]
    shapes.insert(4, pltpu.HBM((8, length), F32))
    specs.insert(4, pl.BlockSpec((8, block), lambda t, *_: (0, t)))
    return pl.pallas_call(
        functools.partial(forward_kernel, counts, firsts),
        grid_spec=pltpu.PrefetchScalarGridSpec(
            num_scalar_prefetch=1,
            grid=(2,),
            in_specs=[
                *chunk_specs(chunks),
                whole_spec((8, D)),
                *[rows_spec(block, 2 * HEAD_DIM, same)] * 3,
                *[whole_spec((out_wide, out_wide))] * 4,
                *in_any(count + len(riders)),
            ],
            out_specs=[whole_spec((2, chunk, D))] * 2 + specs,
            scratch_shapes=[
                pltpu.VMEM((D, wide + out_wide), BF16),
                pltpu.VMEM((D, 2 * quarter), BF16),
                pltpu.VMEM((out_wide, D), BF16),
                pltpu.VMEM((heads, length, HEAD_DIM), BF16),
                pltpu.VMEM((heads, length, HEAD_DIM), BF16),
                pltpu.VMEM((block, D), F32),
                pltpu.SemaphoreType.DMA((count,)),
            ],
        ),
        out_shape=[
            pltpu.HBM((2, chunk, D), F32),
            jax.ShapeDtypeStruct((2, chunk, D), BF16),
            *shapes,
        ],
        compiler_params=pltpu.CompilerParams(vmem_limit_bytes=VMEM_BYTES),
        cost_estimate=cost(13),
        name="layer_forward",
    )(place, *[array for array, _ in chunks], vec, *far(tables), *blocks_out, *far(pieces), *far(riders))


def run_mlp_backward(place, sequence, last, chunks, vec, weight, xhat, slope, att, before, riders=()):
    pieces, first = weight[1][1]
    chunk = chunks[0][0].shape[-2]
    block, length = 2 * chunk, 4 * chunk
    quarter, out_wide = slope.shape[1], att.shape[1]

    def same(t):
        return t

    if last:
        outward = [jax.ShapeDtypeStruct((out_wide, out_wide), BF16)] * (D // out_wide)
    else:
        outward = [pltpu.HBM((out_wide, D), F32)]
    return pl.pallas_call(
        functools.partial(
            mlp_backward_kernel, len(pieces), first, sequence, len(before), len(outward)
        ),
        grid_spec=pltpu.PrefetchScalarGridSpec(
            num_scalar_prefetch=1,
            grid=(2,),
            in_specs=[
                *chunk_specs(chunks),
                whole_spec((8, D)),
                rows_spec(block, D, same),
                rows_spec(block, quarter, same),
                rows_spec(block, out_wide, same),
                *in_any(len(pieces)),
                *[whole_spec((out_wide, D))] * len(before),
                *in_any(len(riders)),
            ],
            out_specs=[
                rows_spec(block, D, same),
                rows_spec(block, quarter, same),
                rows_spec(block, D, same),
                whole_spec((8, D)),
                *[whole_spec(array.shape) for array in outward],
            ],
            scratch_shapes=[
                pltpu.VMEM((D, 2 * quarter), BF16),
                pltpu.VMEM((out_wide, D), F32),
                pltpu.SemaphoreType.DMA((len(pieces),)),
            ],
        ),
        out_shape=[
            pltpu.HBM((length, D), BF16),
            pltpu.HBM((length, quarter), BF16),
            pltpu.HBM((length, D), BF16),
            pltpu.HBM((8, D), F32),
            *outward,
        ],
        compiler_params=pltpu.CompilerParams(vmem_limit_bytes=VMEM_BYTES),
        cost_estimate=cost(8),
        name="mlp_backward",
    )(
        place,
        *[array for array, _ in chunks],
        vec,
        *far([xhat, slope, att, *pieces]),
        *before,
        *far(riders),
    )


def run_attention_backward(
    place, grad, vec, tables, weight, xhat, qk, val, lse, grad_two, riders=()
):
    blocks_out, ((pieces, first), _) = weight
    length = grad.shape[0]
    block, chunk = length // 2, length // 4
    out_wide = blocks_out[0].shape[0]
    heads = out_wide // HEAD_DIM
    wide = 3 * out_wide

    def turned(t):
        return 1 - t

    return pl.pallas_call(
        functools.partial(attention_backward_kernel, len(pieces), first),
        grid_spec=pltpu.PrefetchScalarGridSpec(
            num_scalar_prefetch=1,
            grid=(2,),
            in_specs=[
                rows_spec(block, D, turned),
                whole_spec((8, D)),
                *[rows_spec(block, 2 * HEAD_DIM, turned)] * 3,
                *[whole_spec((out_wide, out_wide))] * 4,
                rows_spec(block, D, turned),
                whole_spec(qk.shape),
                whole_spec(val.shape),
                pl.BlockSpec((8, block), lambda t, *_: (0, 1 - t)),
                rows_spec(block, D, turned),
                *in_any(len(pieces) + len(riders)),
            ],
            out_specs=[
                *[whole_spec((2, chunk, D))] * 2,
                rows_spec(block, wide, turned),
                whole_spec((8, D)),
            ],
            scratch_shapes=[
                pltpu.VMEM((D, wide + out_wide), BF16),
                pltpu.VMEM((out_wide, D), BF16),
                pltpu.VMEM((heads, block, HEAD_DIM), F32),
                pltpu.VMEM((heads, block, HEAD_DIM), F32),
                pltpu.VMEM((block, D), F32),
                pltpu.SemaphoreType.DMA((len(pieces),)),
            ],
        ),
        out_shape=[
            pltpu.HBM((2, chunk, D), F32),
            jax.ShapeDtypeStruct((2, chunk, D), BF16),
            pltpu.HBM((length, wide), BF16),
            pltpu.HBM((8, D), F32),
        ],
        compiler_params=pltpu.CompilerParams(vmem_limit_bytes=VMEM_BYTES),
        cost_estimate=cost(11),
        name="attention_backward",
    )(
        place,
        *far([grad]),
        vec,
        *far(tables),
        *blocks_out,
        *far([xhat, qk, val, lse, grad_two, *pieces, *riders]),
    )


def outer_outputs(split, columns):
    if split:
        shape = (4, D // 8, columns)
        kinds = [F32, BF16]
    else:
        shape, kinds = (D, columns), [BF16]
    return [jax.ShapeDtypeStruct(shape, kind) for kind in kinds], [whole_spec(shape)] * len(kinds)


def run_mlp_outer(scalars, vec, groups, split, riders=()):
    xhats, grads, pres, hids = groups
    arrays = [array for both in zip(xhats, pres, grads, hids) for array in both]
    shapes, specs = outer_outputs(split, 2 * hids[0].shape[1])
    return pl.pallas_call(
        functools.partial(mlp_outer_kernel, len(xhats), len(shapes)),
        grid_spec=pltpu.PrefetchScalarGridSpec(
            num_scalar_prefetch=1,
            grid=(1,),
            in_specs=[whole_spec((8, D)), *in_any(len(arrays) + len(riders))],
            out_specs=specs,
            scratch_shapes=[
                *[pltpu.VMEM(array.shape, BF16) for array in arrays],
                pltpu.SemaphoreType.DMA((len(arrays),)),
            ],
        ),
        out_shape=shapes,
        compiler_params=pltpu.CompilerParams(vmem_limit_bytes=VMEM_BYTES),
        cost_estimate=cost(10),
        name="mlp_outer",
    )(scalars, vec, *far(arrays), *far(riders))


def run_qkv_outer(scalars, vec, groups, outward, split, riders=()):
    arrays = [array for both in zip(*groups) for array in both]
    out_wide = outward[0].shape[1]
    shapes, specs = outer_outputs(split, groups[1][0].shape[1] + out_wide)
    return pl.pallas_call(
        functools.partial(qkv_outer_kernel, len(groups[0]), len(outward), len(shapes)),
        grid_spec=pltpu.PrefetchScalarGridSpec(
            num_scalar_prefetch=1,
            grid=(1,),
            in_specs=[
                whole_spec((8, D)),
                *in_any(len(arrays)),
                *[whole_spec(block.shape) for block in outward],
                *in_any(len(riders)),
            ],
            out_specs=specs,
            scratch_shapes=[
                *[pltpu.VMEM(array.shape, BF16) for array in arrays],
                pltpu.VMEM((D, out_wide), BF16),
                pltpu.SemaphoreType.DMA((len(arrays),)),
            ],
        ),
        out_shape=shapes,
        compiler_params=pltpu.CompilerParams(vmem_limit_bytes=VMEM_BYTES),
        cost_estimate=cost(6),
        name="qkv_outer",
    )(scalars, vec, *far(arrays), *outward, *far(riders))


def run_gradient(sources, row_state, layer, shape, earlier=(), riders=()):
    layers, rows, width = shape
    arrays = [array for source in sources for array in source]
    shapes = [shape, (layers, 8, rows), (layers, 8 * -(-(width // 128 + 1) // 8), 128)]

    def of_layer(shape):
        return pl.BlockSpec((1, *shape[1:]), lambda *_: (layer, 0, 0))

    return pl.pallas_call(
        functools.partial(
            gradient_kernel, [len(source) for source in sources], matrix_cuts(width)
        ),
        grid=(1,),
        in_specs=[
            *[whole_spec(array.shape) for array in arrays],
            of_layer(row_state.shape),
            *in_any(len(earlier) + len(riders)),
        ],
        out_specs=[of_layer(shape) for shape in shapes],
        out_shape=[jax.ShapeDtypeStruct(shape, F32) for shape in shapes],
        input_output_aliases={len(arrays) + 1 + k: k for k in range(len(earlier))},
        compiler_params=pltpu.CompilerParams(vmem_limit_bytes=VMEM_BYTES),
        cost_estimate=cost(2),
        name="gradient",
    )(*arrays, row_state, *earlier, *riders)


def run_whole(kernel, arrays, shapes, name):
    return pl.pallas_call(
        functools.partial(kernel, matrix_cuts(arrays[0].shape[2])),
        grid=(1,),
        in_specs=[whole_spec(array.shape) for array in arrays],
        out_specs=[whole_spec(shape) for shape, _ in shapes],
        out_shape=[jax.ShapeDtypeStruct(shape, kind) for shape, kind in shapes],
        compiler_params=pltpu.CompilerParams(vmem_limit_bytes=VMEM_BYTES),
        cost_estimate=cost(2),
        name=name,
    )(*arrays)


def example_kernel(layers, sequences, scalars, *refs):
    out = refs[-1]
    out[...] = jnp.zeros_like(out)
    seq_place = scalars[0]
    mine = jnp.where(seq_place == 0, 1.0, 0.0)
    for s in range(sequences):
        for i in range(layers):
            of_mlp, of_attention = refs[2 * (i * sequences + s) : 2 * (i * sequences + s) + 2]
            at = s * layers + i
            out[at, 0:2] = of_attention[0:2]
            out[at, 2:4] = of_mlp[0:2]
            out[at, 4:5] = of_mlp[3:4] * mine
            out[at, pl.ds(5 + seq_place, 1)] = of_mlp[2:3]
            wide = 3 * D * D // FF
            out[at, pl.ds(5 + FF // D + seq_place, 1), :wide] = of_attention[2:3, :wide]


def run_example(scalars, sums, sequences):
    arrays = [array for layer in sums for pair in layer for array in pair]
    shape = (sequences * len(sums), 16, D)
    return pl.pallas_call(
        functools.partial(example_kernel, len(sums), sequences),
        grid_spec=pltpu.PrefetchScalarGridSpec(
            num_scalar_prefetch=1,
            grid=(1,),
            in_specs=[whole_spec(array.shape) for array in arrays],
            out_specs=whole_spec(shape),
        ),
        out_shape=jax.ShapeDtypeStruct(shape, F32),
        cost_estimate=cost(1),
        name="examples",
    )(scalars, *arrays)


def example_vector(rows):
    groups = FF // D
    wide = 3 * D // groups
    qkv = [
        part for k in range(groups) for part in natural_heads(rows[5 + groups + k : 6 + groups + k, :wide])
    ]
    up = [rows[5 + k : 6 + k] for k in range(groups)]
    return jnp.concatenate(
        [*[rows[k : k + 1] for k in range(4)], *qkv, rows[4:5], *up, rows[4:5]], axis=1
    )


def small_kernel(length, totals, examples, state, params, grads, moments, new, scores):
    layers = state.shape[0]
    sequences = scores.shape[0]
    lane = lax.broadcasted_iota(jnp.int32, (1, scores.shape[1]), 1)
    row = lax.broadcasted_iota(jnp.int32, totals.shape[1:], 0)
    weight = jnp.where(row == 4, 2.0, 1.0)

    def product(left, right):
        value = jnp.sum(left * right * weight, axis=1, keepdims=True)
        return jnp.sum(value, axis=0, keepdims=True)

    query = [totals[layers + i] for i in range(layers)]
    mean = sum(product(rows, rows) for rows in query) / (layers * SMALL)
    spread = length * layers * SMALL * (mean + 1e-06)
    for s in range(sequences):
        each = [examples[s * layers + i] for i in range(layers)]
        norm = sum(product(rows, rows) for rows in each) / (layers * SMALL * length)
        influence = sum(product(*pair) for pair in zip(each, query)) / jnp.sqrt(spread)
        scores[s : s + 1] = jnp.where(lane == 0, norm, influence)
    edges = [0, D, 2 * D, 3 * D, 4 * D, 7 * D, 8 * D, 8 * D + FF, SMALL]
    for i in range(layers):
        place = slice(i, i + 1)
        gradient = example_vector(totals[i])
        grads[place] = gradient
        moment = DECAY * state[place] + (1.0 - DECAY) * (gradient * gradient + EPS_SQUARE)
        moments[place] = moment
        for first, end in zip(edges, edges[1:]):
            columns = slice(first, end)
            update = gradient[:, columns] * lax.rsqrt(moment[:, columns])
            old = params[place, columns]
            rms = jnp.sqrt(jnp.mean(update * update, axis=1, keepdims=True))
            old_rms = jnp.sqrt(jnp.mean(old * old, axis=1, keepdims=True))
            new[place, columns] = old - RATE * old_rms * (update / jnp.maximum(1.0, rms))


def run_small(length, totals, examples, state, params, sequences):
    arrays = [totals, examples, state, params]
    shapes = [state.shape] * 3 + [(sequences, 128)]
    return pl.pallas_call(
        functools.partial(small_kernel, length),
        grid=(1,),
        in_specs=[whole_spec(array.shape) for array in arrays],
        out_specs=[whole_spec(shape) for shape in shapes],
        out_shape=[jax.ShapeDtypeStruct(shape, F32) for shape in shapes],
        cost_estimate=cost(2),
        name="small_vectors",
    )(*arrays)


def half_spec(array, place, flipped=False):
    def index(h):
        half = 1 - h if flipped else h
        return (half, 0, 0) if place is None else (place, half, 0, 0)

    block = (None, *array.shape[-2:])
    return pl.BlockSpec(block if place is None else (None, *block), index)


def run_finish(kernel, sums, received, others, bias, name):
    keep, near, _ = sums
    shape = keep.shape
    arrays = [(keep, None), (near, None), (received, None), *others]
    specs = [half_spec(array, place, k == 2) for k, (array, place) in enumerate(arrays)]
    return pl.pallas_call(
        kernel,
        grid=(2,),
        in_specs=specs + ([] if bias is None else [whole_spec(bias.shape)]),
        out_specs=[half_spec(keep, None)] * 2,
        out_shape=[pltpu.HBM(shape, F32), jax.ShapeDtypeStruct(shape, BF16)],
        compiler_params=pltpu.CompilerParams(vmem_limit_bytes=VMEM_BYTES),
        cost_estimate=cost(2),
        name=name,
    )(*far([array for array, _ in arrays]), *([] if bias is None else [bias]))


def last_kernel(kernel, count, n_inputs, *refs):
    out = refs[-1]
    bias = refs[count * n_inputs : -1]
    for s in range(count):
        kernel(*refs[n_inputs * s : n_inputs * (s + 1)], *bias, out.at[s])


def run_last(kernel, sums, received, others, bias, kind, name):
    arrays, specs = [], []
    for (keep, near, _), across, more in zip(sums, received, others):
        chunk = keep.shape[-2]
        arrays += [keep, near, across]
        half = pl.BlockSpec((None, chunk, D), lambda i: (0, 0, 0))
        specs += [half, half, whole_spec(across.shape)]
        for array, place in more:
            arrays.append(array)
            if place is None:
                specs.append(half)
            else:
                specs.append(
                    pl.BlockSpec((None, None, chunk, D), lambda i, place=place: (place, 0, 0, 0))
                )
    count = len(sums)
    return pl.pallas_call(
        functools.partial(last_kernel, kernel, count, len(arrays) // count),
        grid=(1,),
        in_specs=specs + ([] if bias is None else [whole_spec(bias.shape)]),
        out_specs=whole_spec((count, chunk, D)),
        out_shape=jax.ShapeDtypeStruct((count, chunk, D), kind),
        compiler_params=pltpu.CompilerParams(vmem_limit_bytes=VMEM_BYTES),
        cost_estimate=cost(2),
        name=name,
    )(*far(arrays), *([] if bias is None else [bias]))


def pass_through_kernel(*refs):
    del refs


def after(values, *others):
    return pl.pallas_call(
        pass_through_kernel,
        in_specs=in_any(1 + len(others)),
        out_specs=pl.BlockSpec(memory_space=pl.ANY),
        out_shape=jax.ShapeDtypeStruct(values.shape, values.dtype),
        input_output_aliases={0: 0},
        name="after",
    )(values, *others)


def out_blocks(columns, dp_place, seq_place):
    stacked = jnp.zeros((D, columns[0].shape[1]), BF16)
    for column, place in zip(columns, piece_places(len(columns), dp_place)):
        stacked = lax.dynamic_update_slice(stacked, column, (place * column.shape[0], 0))
    size = lax.axis_size("seq")
    return exchange_blocks(stacked.reshape(size, D // size, -1), seq_place)


def on_device(block_in, cotangent, labels, master, small_params, row_state, col_state, small_state):
    sequences, chunk = block_in.shape[:2]
    group_count = lax.axis_size("seq")
    seq_place, dp_place = lax.axis_index("seq"), lax.axis_index("dp")
    length = chunk * group_count
    flags = (labels == 0).astype(jnp.int32)
    place = jnp.concatenate(
        [jnp.stack([seq_place % 2, seq_place // 2, dp_place]).astype(jnp.int32), flags]
    )
    train_flag = flags.astype(F32)
    scalars = jnp.concatenate(
        [jnp.stack([dp_place % 2, seq_place]).astype(jnp.int32), flags]
    )
    query_flag = 1.0 - train_flag
    wide, out_wide, quarter = 3 * D // group_count, D // group_count, FF // group_count
    cuts = matrix_cuts(master.shape[2])
    split = lax.axis_size("dp") == 8
    x_bit, z_place = dp_place % 2, dp_place // 2
    tables = rotary_tables(length)

    def normalise(stream):
        scaled, inverse = apply_layer_norm(stream)
        low_scaled = scaled.astype(BF16)
        return (scaled, inverse), low_scaled

    stream = both_halves(block_in)
    _, low_scaled = normalise(stream.astype(F32))
    near = swap(low_scaled, "seq", 1)
    chunks = [((low_scaled, s), (near, s)) for s in range(sequences)]

    low = master.astype(BF16)
    rows_of = [
        jnp.concatenate([heads_together(low[i, :, : cuts[1]]), low[i, :, cuts[1] :]], axis=1)
        for i in range(LAYERS)
    ]
    pieces = gather_rows(rows_of[0])
    whole_one = lax.all_gather(after(rows_of[1], *pieces[4:5]), "dp", axis=0, tiled=True)

    def weight_of(pieces):
        columns = [piece[:, wide : wide + out_wide] for piece in pieces]
        return out_blocks(columns, dp_place, seq_place), [(pieces, 0), (pieces, cuts[2])]

    weights = [weight_of(pieces)]
    vectors, params = [], []
    for i in range(LAYERS):
        param = unpack(small_params[i])
        params.append(param)
        bias_qkv = heads_together(lax.dynamic_slice_in_dim(param[4], seq_place * wide, wide))
        bias_up = lax.dynamic_slice_in_dim(param[6], seq_place * quarter, quarter)
        vectors.append(
            jnp.stack(
                [
                    *param[:4],
                    jnp.pad(bias_up, (0, D - quarter)),
                    jnp.pad(bias_qkv, (0, D - wide)),
                    jnp.zeros((D,), F32),
                    jnp.zeros((D,), F32),
                ]
            )
        )

    streams = [[(stream, s) for s in range(sequences)]]
    saved_all = []
    open_sum = None

    def close_sum(behind):
        nonlocal open_sum
        sums, received, finish = open_sum
        open_sum = None
        finish(sums, after(received, behind))

    def open_exchange(keep, send, behind, finish):
        nonlocal open_sum
        if open_sum is not None:
            send = after(send, open_sum[1])
            close_sum(behind)
        sums = core_sum(keep, send)
        open_sum = (sums, swap(sums[2], "seq", 2), finish)
        return [sums[2]]

    def own_exchange(keep, send):
        near = swap(send, "seq", 1)
        low = (keep[1] + near[1].astype(F32)).astype(BF16)
        return (keep, near, None), swap(low, "seq", 2)

    both_grads = both_halves(cotangent)
    near_grads = swap(both_grads, "seq", 1)
    riders = []
    for i in range(LAYERS):
        last = i == LAYERS - 1
        saved_all.append([])
        next_chunks, next_streams, ends = [], [], []
        bias = (params[i][5] + params[i][7])[None]

        def finish_stream(s, old, bias, next_chunks, next_streams, sums, received):
            fresh, low = run_finish(
                finish_stream_kernel, sums, received, [old], bias, "finish_stream"
            )
            next_streams.append((fresh, None))
            next_chunks.append(((low, None), (swap(low, "seq", 1), None)))

        for s in range(sequences):
            keep, send, *saved = run_forward(
                place, chunks[s], vectors[i], tables, weights[i], riders
            )
            saved_all[i].append(saved)
            if last:
                if open_sum is not None:
                    send = after(send, open_sum[1])
                    close_sum(saved[0])
                ends.append(own_exchange(keep, send))
                continue
            riders = open_exchange(
                keep,
                send,
                saved[0],
                functools.partial(
                    finish_stream, s, streams[i][s], bias, next_chunks, next_streams
                ),
            )
            if i == 0:
                riders = riders + [near_grads]
        if i == 0:
            whole_one = after(whole_one, saved_all[0][0][0])
            weights.append(weight_of([whole_one]))
        if last:
            break
        chunks = next_chunks
        streams.append(next_streams)
    block_out = run_last(
        finish_stream_kernel,
        [sums for sums, _ in ends],
        [received for _, received in ends],
        [[old] for old in streams[-1]],
        bias,
        BF16,
        "block_out",
    )

    grads = [(both_grads, s) for s in range(sequences)]
    chunks = [((both_grads, s), (near_grads, s)) for s in range(sequences)]
    sources, sums = [None] * LAYERS, [None] * LAYERS
    riders, later, latest = [], [], []
    for i in reversed(range(LAYERS)):
        last = i == 0
        xhats, qks, vals, atts, lses, hids, slopes = zip(*saved_all[i])
        mlp, attention, next_chunks, next_grads, ends = [], [], [], [], []

        def finish_grad(s, others, next_chunks, next_grads, sums, received):
            fresh, low = run_finish(
                finish_grad_kernel, sums, received, others, None, "finish_grad"
            )
            next_grads.append((fresh, None))
            next_chunks.append(((low, None), (swap(low, "seq", 1), None)))

        for s in range(sequences):
            mlp.append(
                run_mlp_backward(
                    place,
                    s,
                    s == sequences - 1,
                    chunks[s],
                    vectors[i],
                    weights[i],
                    xhats[s],
                    slopes[s],
                    atts[s],
                    mlp[s - 1][4:] if s else [],
                    riders,
                )
            )
            riders = [mlp[s][3]]
            if open_sum is not None:
                close_sum(mlp[s][3])
            if s == 0:
                riders += later
        outward = [
            block if k == 0 else swap(block, "seq", k) for k, block in enumerate(mlp[-1][4:])
        ]
        groups_b = [xhats, [out[0] for out in mlp], [out[1] for out in mlp], hids]
        both = run_mlp_outer(
            scalars, vectors[i], groups_b, split, [block_out, *latest] if last else []
        )
        riders = [both[-1], *outward]
        for s in range(sequences):
            keep, send, grad_joined, sums_t = run_attention_backward(
                place,
                mlp[s][0],
                vectors[i],
                tables,
                weights[i],
                xhats[s],
                qks[s],
                vals[s],
                lses[s],
                mlp[s][2],
                riders,
            )
            attention.append((grad_joined, sums_t))
            if last:
                riders = []
                ends.append(own_exchange(keep, send))
            else:
                riders = open_exchange(
                    keep,
                    send,
                    grad_joined,
                    functools.partial(
                        finish_grad, s, [grads[s], streams[i][s]], next_chunks, next_grads
                    ),
                )
        if split and not last:
            total_b = pair_total(*both)
            part_b = scatter_along_z(total_b)
        if split and last:
            total_b = pair_total(after(both[0], *[out[0] for out in attention]), both[1])
            part_b = scatter_along_z(total_b)
            riders = [total_b]
        elif not split:
            part_b = lax.psum_scatter(both[0], "dp", scatter_dimension=0, tiled=True)
        groups = [xhats, [out[0] for out in attention]]
        rest = run_qkv_outer(scalars, vectors[i], groups, outward, split, riders)
        if not split:
            part_a = [lax.psum_scatter(rest[0], "dp", scatter_dimension=0, tiled=True)]
        elif last:
            own_a, parts_a = pair_sum(after(rest[0], part_b), rest[1], z_place)
            part_a = [own_a, *exchange_parts(parts_a)]
        else:
            total_a = pair_total(*rest)
            part_a = [scatter_along_z(total_a)]
            later, latest = [total_b], [total_a]
        sources[i] = [[part_b], part_a]
        riders = rest[:1]
        chunks = next_chunks
        grads = next_grads or grads
        sums[i] = [(out[3], other[1]) for out, other in zip(mlp, attention)]
    behind_a = parts_a[:1] if split else rest
    grad_stream = run_last(
        finish_grad_kernel,
        [sums_of for sums_of, _ in ends],
        [after(received, *behind_a) for _, received in ends],
        [[grad, old] for grad, old in zip(grads, streams[0])],
        None,
        F32,
        "input_grad",
    )

    examples = after(run_example(scalars[1:2], sums, sequences), *behind_a)
    examples = sum_pairwise(examples, "seq", BF16)
    stacked = ()
    for i in reversed(range(LAYERS)):
        behind = [] if i else [examples, grad_stream]
        stacked = run_gradient(sources[i], row_state, i, master.shape, stacked, behind)
    reduced_all, row_part, col_part = stacked
    dp_bits, seq_bits = [], []
    for axis, bits in (("dp", dp_bits), ("seq", seq_bits)):
        bits += [(axis, 1 << k) for k in range(lax.axis_size(axis).bit_length() - 1)]
    first_steps = max(len(seq_bits), len(dp_bits))
    flat = examples.reshape(sequences, -1)
    small = jnp.stack(
        [
            jnp.sum(train_flag[:, None] * flat, axis=0),
            jnp.sum((1.0 - train_flag)[:, None] * flat, axis=0),
        ]
    ).reshape(2 * LAYERS, *examples.shape[1:])
    small_steps = list(dp_bits)

    def small_step():
        nonlocal small_steps
        step, *small_steps = small_steps
        sent = small.astype(BF16)
        return sent, swap(sent, *step)

    def together(values):
        nonlocal small
        received = [swap(value, *step) for value, step in values]
        sent = None
        if small_steps:
            sent, small_in = small_step()
            received.append(small_in)
        if len(received) > 1:
            received = [
                after(value, *[other for other in received if other is not value])
                for value in received
            ]
        if sent is not None:
            small = sent.astype(F32) + received.pop().astype(F32)
        return [value + other for (value, _), other in zip(values, received)]

    for k in range(first_steps):
        now = []
        if k < len(seq_bits):
            now.append((row_part, seq_bits[k]))
        if k < len(dp_bits):
            now.append((col_part, dp_bits[k]))
        *rest_sums, last_sum = together(now)
        if k < len(seq_bits) and k < len(dp_bits):
            (row_part,), col_part = rest_sums, last_sum
        elif k < len(dp_bits):
            col_part = last_sum
        else:
            row_part = last_sum
    layers = master.shape[0]
    fresh_row_moments, col_stats, local_sums = run_whole(
        square_kernel,
        [reduced_all, master, row_part, col_part, row_state, col_state],
        [(row_state.shape, F32), (col_state.shape, F32), ((8, 128), F32)],
        "squares",
    )
    state_sums = local_sums
    for step in seq_bits:
        (local_sums,) = together([(local_sums, step)])
    seq_sums = jnp.concatenate(
        [local_sums[: 2 * layers], state_sums[layers : 2 * layers], local_sums[3 * layers :]], axis=0
    )
    for step in dp_bits:
        (local_sums,) = together([(local_sums, step)])
    while small_steps:
        together([])
    small_grads, small_moments, small_new, scores = run_small(
        length, small, examples, small_state, small_params, sequences
    )
    example_norms, influence = scores[:, 0], scores[:, 1]
    new_master, new_low = run_whole(
        update_kernel,
        [reduced_all, master, fresh_row_moments, col_stats, local_sums, seq_sums],
        [(master.shape, F32), (master.shape, BF16)],
        "update",
    )
    return (
        block_out,
        grad_stream,
        example_norms,
        influence,
        reduced_all,
        fresh_row_moments,
        col_stats,
        new_master,
        new_low,
        small_grads,
        small_moments,
        small_new,
    )


def solution(mesh):
    placed = (
        P("dp", "seq", None),
        P("dp", "seq", None),
        P("dp"),
        P(None, "dp", "seq"),
        P(),
        P(None, None, "dp"),
        P(None, "seq"),
        P(),
    )
    return jax.shard_map(
        on_device,
        mesh=mesh,
        in_specs=placed,
        out_specs=(
            P("dp", "seq", None),
            P("dp", "seq", None),
            P("dp"),
            P("dp"),
            P(None, "dp", "seq"),
            P(None, None, "dp"),
            P(None, "seq"),
            P(None, "dp", "seq"),
            P(None, "dp", "seq"),
            P(),
            P(),
            P(),
        ),
        check_vma=False,
    )
```

```python
import functools

import jax
import numpy as np
import jax.numpy as jnp
from jax import lax
from jax.experimental import pallas as pl
from jax.experimental.pallas import tpu as pltpu
from jax.sharding import PartitionSpec as P

D = 768
HEADS = 12
FF = 3072
LAYERS = 2
HEAD_DIM = 64
ROT = 16
SMALL = 9984

EPS_NORM = 1e-05
EPS_SQUARE = 1e-30
RATE = 0.5
DECAY = 0.5
NEG_LARGE = -1e30
SCORE_SCALE = HEAD_DIM ** (-0.5)
CONTRACT_LAST = (((1,), (1,)), ((), ()))
CONTRACT_FIRST = (((0,), (0,)), ((), ()))
VMEM_BYTES = 24 * 1024 * 1024
BF16 = jnp.bfloat16
F32 = jnp.float32


def unpack(vector):
    return jnp.split(vector, [D, 2 * D, 3 * D, 4 * D, 7 * D, 8 * D, 8 * D + FF], axis=-1)


def apply_layer_norm(inputs):
    centred = inputs - jnp.mean(inputs, axis=-1, keepdims=True)
    variance = jnp.mean(centred * centred, axis=-1, keepdims=True)
    inverse = lax.rsqrt(variance + EPS_NORM)
    return (centred * inverse, inverse)


def norm_back(grad_scaled, scaled, inverse):
    mean_grad = jnp.mean(grad_scaled, axis=-1, keepdims=True)
    mean_cross = jnp.mean(grad_scaled * scaled, axis=-1, keepdims=True)
    return (grad_scaled - mean_grad - scaled * mean_cross) * inverse


def rotary_tables(length):
    halfway = ROT // 2
    frequency = 10000.0 ** (-2.0 * np.arange(halfway) / ROT)
    angles = np.arange(length)[:, None] * frequency[None, :]
    cosine, sine = np.cos(angles), np.sin(angles)
    rest = np.ones((length, HEAD_DIM - ROT))
    none = np.zeros((length, halfway))
    keep = np.concatenate([cosine, cosine, rest], axis=1)
    ahead = np.concatenate([-sine, none, 0.0 * rest], axis=1)
    behind = np.concatenate([none, sine, 0.0 * rest], axis=1)
    return tuple(
        jnp.asarray(np.concatenate([table, table], axis=1), F32) for table in (keep, ahead, behind)
    )


def swap(values, axis, bits):
    size = lax.axis_size(axis)
    return lax.ppermute(values, axis, [(i, i ^ bits) for i in range(size)])


def sum_pairwise(values, axis, wire=F32):
    bits = 1
    while bits < lax.axis_size(axis):
        sent = values.astype(wire)
        values = sent.astype(F32) + swap(sent, axis, bits).astype(F32)
        bits *= 2
    return values


def both_halves(own):
    return jnp.stack([own, swap(own, "seq", 2)], axis=-3)


def core_sum(keep, send):
    received = swap(send, "seq", 1)
    return keep, received, (keep.astype(F32) + received.astype(F32)).astype(BF16)


def gather_rows(rows):
    if lax.axis_size("dp") != 8:
        return [lax.all_gather(rows, "dp", axis=0, tiled=True)]
    pieces = []
    for k in range(4):
        pieces += [rows, swap(rows, "dp", 1)]
        if k < 3:
            rows = lax.ppermute(rows, "dp", [(i, (i + 2) % 8) for i in range(8)])
    return pieces


def piece_places(count, dp_place):
    if count == 1:
        return [0]
    return [(dp_place + 8 - 2 * (k // 2)) % 8 ^ (k % 2) for k in range(count)]


def pair_sum(keep, send, z_place):
    summed = keep.astype(F32) + swap(send, "dp", 1).astype(F32)
    own = lax.dynamic_index_in_dim(summed, z_place, 0, keepdims=False)
    return own, [
        lax.dynamic_index_in_dim(summed, z_place ^ k, 0, keepdims=False).astype(BF16)
        for k in range(1, summed.shape[0])
    ]


def pair_total(keep, send):
    total = keep.astype(F32) + swap(send, "dp", 1).astype(F32)
    return total.astype(BF16).reshape(-1, keep.shape[-1])


def scatter_along_z(total):
    groups = [[2 * z + x for z in range(4)] for x in range(2)]
    return lax.psum_scatter(
        total, "dp", scatter_dimension=0, tiled=True, axis_index_groups=groups
    )


def exchange_parts(parts):
    return [swap(part, "dp", 2 * (k + 1)) for k, part in enumerate(parts)]


def exchange_blocks(blocks, index):
    size = lax.axis_size("seq")
    received = []
    for k in range(size):
        block = lax.dynamic_index_in_dim(blocks, index ^ k, 0, keepdims=False)
        received.append(block if k == 0 else swap(block, "seq", k))
    return received


def heads_together(values):
    heads = values.shape[-1] // (3 * HEAD_DIM)
    lead = values.shape[:-1]
    by_head = values.reshape(*lead, heads, 3 * HEAD_DIM)
    return jnp.concatenate(
        [
            by_head[..., : 2 * HEAD_DIM].reshape(*lead, heads * 2 * HEAD_DIM),
            by_head[..., 2 * HEAD_DIM :].reshape(*lead, heads * HEAD_DIM),
        ],
        axis=-1,
    )


def heads_apart(values):
    heads = values.shape[-1] // (3 * HEAD_DIM)
    lead = values.shape[:-1]
    pairs, last = jnp.split(values, [heads * 2 * HEAD_DIM], axis=-1)
    return jnp.concatenate(
        [
            pairs.reshape(*lead, heads, 2 * HEAD_DIM),
            last.reshape(*lead, heads, HEAD_DIM),
        ],
        axis=-1,
    ).reshape(values.shape)


def halves(core_bit, chunk):
    own = pl.multiple_of(core_bit * chunk, chunk)
    return pl.ds(own, chunk), pl.ds(pl.multiple_of(chunk - own, chunk), chunk)


def place_tokens(dst, own, near, core_bit, y_here, chunk):
    at_own, at_near = halves(core_bit, chunk)
    dst[at_own] = own[y_here]
    dst[at_near] = near[y_here]


def spread_tokens(value, held, keep, send, core_bit, y_here, chunk):
    at_own, at_near = halves(core_bit, chunk)
    held[...] = value
    keep[pl.ds(y_here, 1)] = held[at_own].astype(keep.dtype)[None]
    send[pl.ds(y_here, 1)] = held[at_near].astype(send.dtype)[None]


def gelu_and_slope(v):
    magnitude = jnp.abs(v) * 0.7071067811865476
    bottom = 1.0 + 0.3275911 * magnitude
    t = pl.reciprocal(bottom, approx=True)
    t = t * (2.0 - bottom * t)
    t = t * (2.0 - bottom * t)
    falling = jnp.exp(-0.5 * v * v)
    poly = t * (
        0.254829592
        + t * (-0.284496736 + t * (1.421413741 + t * (-1.453152027 + t * 1.061405429)))
    )
    tail = 0.5 * poly * falling
    cdf = jnp.where(v >= 0.0, 1.0 - tail, tail)
    return v * cdf, cdf + v * falling * 0.3989422804014327


def weight_copies(dp_place, sources, targets, sems):
    copies = []
    for (pieces, first), target in zip(sources, targets):
        rows, width = pieces[0].shape[0], target.shape[1]
        for piece, place in zip(pieces, piece_places(len(pieces), dp_place)):
            offset = 0 if len(pieces) == 1 else pl.multiple_of(place * rows, 16)
            copies.append(
                pltpu.make_async_copy(
                    piece.at[:, pl.ds(first, width)],
                    target.at[pl.ds(offset, rows), :],
                    sems.at[len(copies)],
                )
            )
    return copies


def place_columns(whole, blocks, place):
    width = blocks[0].shape[1]
    seq_place = 2 * place[1] + place[0]
    for index in range(len(blocks)):

        @pl.when(seq_place == index)
        def _():
            for k, block in enumerate(blocks):
                at = width * (index ^ k)
                whole[:, at : at + width] = block[...]


def start_all(copies):
    for copy in copies:
        copy.start()


def wait_all(copies):
    for copy in copies:
        copy.wait()


def turn(pair, tables, sign):
    keep_tab, ahead_tab, behind_tab = tables
    ahead = pltpu.roll(pair, 2 * HEAD_DIM - ROT // 2, 1) * ahead_tab[...]
    behind = pltpu.roll(pair, ROT // 2, 1) * behind_tab[...]
    return pair * keep_tab[...] + sign * (ahead + behind)


def forward_kernel(counts, firsts, place, *refs):
    refs = list(refs)

    def take(count):
        taken, refs[:] = refs[:count], refs[count:]
        return taken

    own, near, vec = take(3)
    tables = take(3)
    blocks_out = take(4)
    pieces = [take(count) for count in counts]
    keep, send, xhat, qk, val, att, lse, hid, slope = refs[-16:-7]
    whole_a, whole_b, w_out, k_all, v_all, held, sems = refs[-7:]
    core_bit, y_bit, dp_place = place[0], place[1], place[2]
    step = pl.program_id(0)
    wide = 3 * val.shape[1]
    sources = list(zip(pieces, firsts))
    copies = weight_copies(dp_place, sources, [whole_a, whole_b], sems)

    @pl.when(step == 0)
    def _():
        start_all(copies)
        place_columns(w_out, blocks_out, place)

    chunk = own.shape[1]
    block = 2 * chunk
    y_here = step ^ y_bit
    place_tokens(xhat, own, near, core_bit, y_here, chunk)
    heads = val.shape[-1] // HEAD_DIM
    quarter = hid.shape[-1]
    row = lax.broadcasted_iota(jnp.int32, (block, block), 0)
    column = lax.broadcasted_iota(jnp.int32, (block, block), 1)
    lane = lax.broadcasted_iota(jnp.int32, (block, 128), 1)

    def attend(here, h, joined, log_sums):
        at_q, at_k = 2 * HEAD_DIM * h, 2 * HEAD_DIM * h + HEAD_DIM
        turned = turn(joined[:, at_q : at_k + HEAD_DIM], tables, 1.0)
        qk[:, at_q : at_k + HEAD_DIM] = turned.astype(BF16)
        k_all[h, block * here : block * (here + 1)] = turned[:, HEAD_DIM:].astype(BF16)
        first = 2 * HEAD_DIM * heads + HEAD_DIM * h
        v_all[h, block * here : block * (here + 1)] = joined[:, first : first + HEAD_DIM].astype(
            BF16
        )
        query = qk[:, at_q : at_q + HEAD_DIM] * jnp.asarray(SCORE_SCALE, BF16)
        scores = []
        for j in range(here + 1):
            part = lax.dot_general(
                query,
                k_all[h, block * j : block * (j + 1)],
                CONTRACT_LAST,
                preferred_element_type=F32,
            )
            if j == here:
                part = jnp.where(column <= row, part, NEG_LARGE)
            scores.append(part)
        largest = functools.reduce(
            jnp.maximum, [jnp.max(part, axis=-1, keepdims=True) for part in scores]
        )
        total = 0.0
        mixed = 0.0
        for j, part in enumerate(scores):
            exponent = jnp.exp(part - largest)
            total = total + jnp.sum(exponent, axis=-1, keepdims=True)
            mixed = mixed + jnp.dot(
                exponent.astype(BF16),
                v_all[h, block * j : block * (j + 1)],
                preferred_element_type=F32,
            )
        att[:, HEAD_DIM * h : HEAD_DIM * (h + 1)] = (mixed / total).astype(BF16)
        return jnp.where(lane == h, largest + jnp.log(total), log_sums)

    for here in range(2):

        @pl.when(step == here)
        def _():
            scaled = xhat[...].astype(F32)
            normed_one = (scaled * vec[0:1] + vec[1:2]).astype(BF16)
            normed_two = (scaled * vec[2:3] + vec[3:4]).astype(BF16)
            if here == 0:
                wait_all(copies)
            joined = (
                jnp.dot(normed_one, whole_a[:, :wide], preferred_element_type=F32) + vec[5:6, :wide]
            )
            val[...] = joined[:, 2 * HEAD_DIM * heads :].astype(BF16)
            hidden_pre = (
                jnp.dot(normed_two, whole_b[:, :quarter], preferred_element_type=F32)
                + vec[4:5, :quarter]
            )
            log_sums = jnp.zeros((block, 128), F32)
            for h in range(heads):
                log_sums = attend(here, h, joined, log_sums)
            lse[...] = log_sums.T[:8]
            hidden, gradient = gelu_and_slope(hidden_pre)
            hid[...] = hidden.astype(BF16)
            slope[...] = gradient.astype(BF16)
            partial = jnp.dot(att[...], w_out[...], preferred_element_type=F32) + lax.dot_general(
                hid[...], whole_b[:, quarter:], CONTRACT_LAST, preferred_element_type=F32
            )
            spread_tokens(partial, held, keep, send, core_bit, y_here, chunk)


def normalised(stream):
    centred = stream - jnp.mean(stream, axis=-1, keepdims=True)
    variance = jnp.mean(centred * centred, axis=-1, keepdims=True)
    inverse = lax.rsqrt(variance + EPS_NORM)
    return centred * inverse, inverse


def seq_sum(keep, near, across):
    return keep[...].astype(F32) + near[...].astype(F32) + across[...].astype(F32)


def finish_stream_kernel(keep, near, across, stream, bias, out, *low):
    value = stream[...].astype(F32) + seq_sum(keep, near, across) + bias[...]
    out[...] = value.astype(out.dtype)
    if low:
        low[0][...] = normalised(value)[0].astype(BF16)


def finish_grad_kernel(keep, near, across, grad, stream, out, *low):
    scaled, inverse = normalised(stream[...].astype(F32))
    back = norm_back(seq_sum(keep, near, across), scaled, inverse)
    value = grad[...].astype(F32) + back
    out[...] = value
    if low:
        low[0][...] = value.astype(BF16)


def add_up(sums, place_row, values):
    sums[place_row : place_row + 1, : values.shape[-1]] += jnp.sum(
        values.astype(F32), axis=0, keepdims=True
    )


def mlp_backward_kernel(count, first, sequences, n_outs, place, vec, *refs):
    refs = list(refs)

    def take(number):
        taken, refs[:] = refs[:number], refs[number:]
        return taken

    inputs = [take(6) for _ in range(sequences)]
    pieces = take(count)
    n_blocks = D // inputs[0][4].shape[1]
    whole_b, product, sum_up, sum_down, sems = refs[-5:]
    del refs[: -5 - 4 * sequences - n_blocks - n_outs]
    outputs = [take(4) for _ in range(sequences)]
    outward, outs = take(n_blocks), take(n_outs)
    core_bit, y_bit, dp_place = place[0], place[1], place[2]
    step = pl.program_id(0)
    copies = weight_copies(dp_place, [(pieces, first)], [whole_b], sems)
    quarter = sum_up.shape[1]

    @pl.when(step == 0)
    def _():
        start_all(copies)
        product[...] = jnp.zeros_like(product)
        sum_up[...] = jnp.zeros_like(sum_up)
        sum_down[...] = jnp.zeros_like(sum_down)

    def one_block(s):
        own, near, xhat, slope, att, hid = inputs[s]
        grad, grad_pre, grad_two, sums = outputs[s]
        chunk = own.shape[1]
        half = step - 2 * s
        place_tokens(grad, own, near, core_bit, half ^ y_bit, chunk)

        @pl.when(half == 0)
        def _():
            sums[...] = jnp.zeros_like(sums)
            if s == 0:
                wait_all(copies)

        flag = place[3 + s] > 0
        scaled = xhat[...].astype(F32)
        grad_hidden = jnp.dot(grad[...], whole_b[:, quarter:], preferred_element_type=F32)
        low_pre = (grad_hidden * slope[...].astype(F32)).astype(BF16)
        grad_pre[...] = low_pre
        normed = lax.dot_general(
            low_pre, whole_b[:, :quarter], CONTRACT_LAST, preferred_element_type=F32
        )
        grad_two[...] = (normed * vec[2:3]).astype(BF16)
        kept = jnp.where(flag, grad[...], jnp.zeros_like(grad))
        kept_pre = jnp.where(flag, low_pre, jnp.zeros_like(low_pre))
        forward_normed = (scaled * vec[2:3] + vec[3:4]).astype(BF16)
        product[...] += lax.dot_general(
            att[...], kept, CONTRACT_FIRST, preferred_element_type=F32
        )
        sum_up[...] += lax.dot_general(
            forward_normed, kept_pre, CONTRACT_FIRST, preferred_element_type=F32
        )
        sum_down[...] += lax.dot_general(
            kept, hid[...], CONTRACT_FIRST, preferred_element_type=F32
        )
        add_up(sums, 0, normed * scaled)
        add_up(sums, 1, normed)
        add_up(sums, 2, low_pre)
        add_up(sums, 3, grad[...])

    for s in range(sequences):

        @pl.when(step // 2 == s)
        def _():
            one_block(s)

    @pl.when(step == 2 * sequences - 1)
    def _():
        store_rows(sum_up, outs, 0, dp_place % 2)
        store_rows(sum_down, outs, quarter, dp_place % 2)
        width = outward[0].shape[1]
        for index in range(n_blocks):

            @pl.when(2 * y_bit + core_bit == index)
            def _():
                for k, block in enumerate(outward):
                    at = width * (index ^ k)
                    block[...] = product[:, at : at + width].astype(BF16)


def attention_backward_kernel(count, first, place, *refs):
    refs = list(refs)

    def take(number):
        taken, refs[:] = refs[:number], refs[number:]
        return taken

    grad, vec = take(2)
    tables = take(3)
    blocks_out = take(4)
    xhat, qk, val, lse, grad_two = take(5)
    pieces = take(count)
    keep, send, grad_joined, sums = refs[-10:-6]
    whole_a, w_out, dk_all, dv_all, held, sems = refs[-6:]
    core_bit, y_bit, dp_place = place[0], place[1], place[2]
    step = 1 - pl.program_id(0)
    copies = weight_copies(dp_place, [(pieces, first)], [whole_a], sems)

    @pl.when(step == 1)
    def _():
        start_all(copies)
        sums[...] = jnp.zeros_like(sums)
        place_columns(w_out, blocks_out, place)

    block = grad.shape[0]
    chunk = block // 2
    heads = val.shape[-1] // HEAD_DIM
    row = lax.broadcasted_iota(jnp.int32, (block, block), 0)
    column = lax.broadcasted_iota(jnp.int32, (block, block), 1)

    def attend_back(here, h, near_grad):
        at_q, at_k = 2 * HEAD_DIM * h, 2 * HEAD_DIM * h + HEAD_DIM
        at_v = 2 * HEAD_DIM * heads + HEAD_DIM * h
        query = qk[block * here : block * (here + 1), at_q:at_k]
        query = query * jnp.asarray(SCORE_SCALE, BF16)
        log_row = lse[h : h + 1]
        probs, grad_probs, keys = [], [], []
        delta = 0.0
        for j in range(here + 1):
            key = qk[block * j : block * (j + 1), at_k : at_k + HEAD_DIM]
            value = val[block * j : block * (j + 1), HEAD_DIM * h : HEAD_DIM * (h + 1)]
            scores = lax.dot_general(key, query, CONTRACT_LAST, preferred_element_type=F32)
            prob = jnp.exp(scores - log_row)
            if j == here:
                prob = jnp.where(row <= column, prob, 0.0)
            grad_prob = lax.dot_general(
                value, near_grad, CONTRACT_LAST, preferred_element_type=F32
            )
            delta = delta + jnp.sum(prob * grad_prob, axis=0, keepdims=True)
            probs.append(prob)
            grad_probs.append(grad_prob)
            keys.append(key)
        dq = 0.0
        for j in range(here + 1):
            grad_score = (probs[j] * (grad_probs[j] - delta)).astype(BF16)
            dk = jnp.dot(grad_score, query, preferred_element_type=F32)
            dv = jnp.dot(probs[j].astype(BF16), near_grad, preferred_element_type=F32)
            dq = dq + lax.dot_general(
                grad_score, keys[j], CONTRACT_FIRST, preferred_element_type=F32
            )
            if j < here:
                dk_all[h], dv_all[h] = dk, dv
            elif here == 0:
                dk, dv = dk + dk_all[h], dv + dv_all[h]
        pair = jnp.concatenate([dq * SCORE_SCALE, dk], axis=1)
        grad_joined[:, at_q : at_q + 2 * HEAD_DIM] = turn(pair, tables, -1.0).astype(BF16)
        grad_joined[:, at_v : at_v + HEAD_DIM] = dv.astype(BF16)

    for here in (1, 0):

        @pl.when(step == here)
        def _():
            grad_att = lax.dot_general(
                grad[...], w_out[...], CONTRACT_LAST, preferred_element_type=F32
            ).astype(BF16)
            for h in range(heads):
                attend_back(here, h, grad_att[:, HEAD_DIM * h : HEAD_DIM * (h + 1)])
            if here == 1:
                wait_all(copies)
            normed = lax.dot_general(
                grad_joined[...],
                whole_a[:, : grad_joined.shape[1]],
                CONTRACT_LAST,
                preferred_element_type=F32,
            )
            spread_tokens(
                normed * vec[0:1] + grad_two[...].astype(F32),
                held,
                keep,
                send,
                core_bit,
                step ^ y_bit,
                chunk,
            )
            add_up(sums, 0, normed * xhat[...].astype(F32))
            add_up(sums, 1, normed)
            add_up(sums, 2, grad_joined[...])


def fetch(sources, targets, sems):
    copies = [
        pltpu.make_async_copy(source, target, sems.at[k])
        for k, (source, target) in enumerate(zip(sources, targets))
    ]
    start_all(copies)
    return copies


def outer_sum(flags, pairs):
    total = 0.0
    for flag, pair in zip(flags, pairs):
        left, right = pair()
        kept = jnp.where(flag > 0, right, jnp.zeros_like(right))
        total = total + lax.dot_general(left, kept, CONTRACT_FIRST, preferred_element_type=F32)
    return total


def store_rows(value, outs, first, x_bit):
    columns = pl.ds(first, value.shape[1])
    if len(outs) == 1:
        outs[0][:, columns] = value[...].astype(BF16)
        return
    keep, send = outs
    rows = keep.shape[1]
    for bit in (0, 1):

        @pl.when(x_bit == bit)
        def _():
            for z in range(keep.shape[0]):
                at = rows * (2 * z + bit)
                to = rows * (2 * z + 1 - bit)
                keep[z, :, columns] = value[at : at + rows].astype(BF16)
                send[z, :, columns] = value[to : to + rows].astype(BF16)


def qkv_outer_kernel(count, n_blocks, n_outs, scalars, vec, *refs):
    sources, blocks = refs[: 2 * count], refs[2 * count : 2 * count + n_blocks]
    held, outward, sems = refs[-2 * count - 2 : -2], refs[-2], refs[-1]
    outs = refs[-2 * count - 2 - n_outs : -2 * count - 2]
    copies = fetch(sources, held, sems)
    x_bit, flags = scalars[0], [scalars[2 + s] for s in range(count)]

    def pair_of(s):
        def pair():
            copies[2 * s].wait()
            copies[2 * s + 1].wait()
            normed = held[2 * s][...].astype(F32) * vec[0:1] + vec[1:2]
            return normed.astype(BF16), held[2 * s + 1][...]

        return pair

    rows = blocks[0].shape[0]
    for k, block in enumerate(blocks):
        outward[pl.ds(pl.multiple_of((scalars[1] ^ k) * rows, 16), rows)] = block[...]
    wide = held[1].shape[1]
    store_rows(outward[...].astype(F32), outs, wide, x_bit)
    store_rows(outer_sum(flags, [pair_of(s) for s in range(count)]), outs, 0, x_bit)


def natural_heads(values):
    heads = values.shape[1] // (3 * HEAD_DIM)
    parts = []
    for h in range(heads):
        parts.append(values[:, 2 * HEAD_DIM * h : 2 * HEAD_DIM * (h + 1)])
        at = 2 * HEAD_DIM * heads + HEAD_DIM * h
        parts.append(values[:, at : at + HEAD_DIM])
    return parts


def matrix_cuts(width):
    unit = width // 12
    return [0, 3 * unit, 4 * unit, 8 * unit, width]


def gradient_kernel(counts, cuts, *refs):
    refs = list(refs)
    row_state, (grads, row_sums, col_sums) = refs[sum(counts)], refs[-3:]
    parts = []
    for count in counts:
        taken, refs[:] = refs[:count], refs[count:]
        parts.append(sum(ref[...].astype(F32) for ref in taken))
    both, rest = parts
    at = 0
    for part in natural_heads(rest[:, : cuts[1]]):
        grads[0, :, at : at + part.shape[1]] = part
        at += part.shape[1]
    grads[0, :, cuts[1] : cuts[2]] = rest[:, cuts[1] :]
    grads[0, :, cuts[2] :] = both
    whole = grads[0]
    squares = whole * whole + EPS_SQUARE
    by_column = jnp.sum(squares, axis=0, keepdims=True)
    lanes = whole.shape[1] // 128
    row = lax.broadcasted_iota(jnp.int32, (whole.shape[0], 128), 1)
    lane = lax.broadcasted_iota(jnp.int32, (1, 128), 1)
    by_row = jnp.zeros((whole.shape[0], 128), F32)
    for m in range(4):
        total = jnp.sum(squares[:, cuts[m] : cuts[m + 1]], axis=1, keepdims=True)
        by_row = jnp.where(row == m, total, by_row)
    row_sums[0] = by_row.T[:8]
    totals = jnp.sum(by_row, axis=0, keepdims=True)
    states = jnp.sum(row_state[0], axis=1, keepdims=True)
    for m in range(4):
        totals = jnp.where(lane == 4 + m, states[m : m + 1], totals)
    col_sums[0] = jnp.zeros_like(col_sums[0])
    for k in range(lanes):
        col_sums[0, k : k + 1] = by_column[:, 128 * k : 128 * (k + 1)]
    col_sums[0, lanes : lanes + 1] = totals


def in_a_row(rows):
    return jnp.concatenate([rows[k : k + 1] for k in range(rows.shape[0])], axis=1)


def upright(rows):
    padded = jnp.concatenate([rows, jnp.zeros((4, rows.shape[1]), F32)], axis=0)
    spare = -rows.shape[1] % 128
    if spare:
        padded = jnp.concatenate([padded, jnp.zeros((8, spare), F32)], axis=1)
    return padded.T[: rows.shape[1]]


def scaled_update(grads, row_inverse, col_inverse, cuts, i, m):
    columns = slice(cuts[m], cuts[m + 1])
    return grads[i, :, columns] * row_inverse[:, m : m + 1] * col_inverse[:, columns]


def square_kernel(cuts, grads, master, rows, cols, row_state, col_state, fresh, stats, sums):
    layers = grads.shape[0]
    lanes = cuts[4] // 128
    lane = lax.broadcasted_iota(jnp.int32, (1, 128), 1)
    matrix = lax.broadcasted_iota(jnp.int32, (4, 1), 0)
    widths = jnp.where(matrix == 0, 3.0 * D, jnp.where(matrix == 1, 1.0 * D, 1.0 * FF))
    sums[...] = jnp.zeros_like(sums)
    for i in range(layers):
        fresh[i] = DECAY * row_state[i] + (1.0 - DECAY) * (rows[i, :4] / widths)
        stats[i : i + 1] = DECAY * col_state[i : i + 1] + (1.0 - DECAY) * (
            in_a_row(cols[i, :lanes]) / D
        )
        row_inverse = upright(lax.rsqrt(fresh[i]))
        col_inverse = lax.rsqrt(stats[i : i + 1])
        result = jnp.zeros((1, 128), F32)
        for m in range(4):
            update = scaled_update(grads, row_inverse, col_inverse, cuts, i, m)
            old = master[i, :, cuts[m] : cuts[m + 1]]
            for at, values in ((0, update), (4, old)):
                total = jnp.sum(
                    jnp.sum(values * values, axis=0, keepdims=True), axis=1, keepdims=True
                )
                result = jnp.where(lane == at + m, total, result)
        sums[i : i + 1] = result
        sums[layers + i : layers + i + 1] = cols[i, lanes : lanes + 1]


def update_kernel(cuts, grads, master, fresh, stats, sums, row_sums, new, new_low):
    layers = grads.shape[0]
    for i in range(layers):
        row_inverse = upright(lax.rsqrt(fresh[i]))
        col_inverse = lax.rsqrt(stats[i : i + 1])
        for m, width in enumerate((3.0 * D, 1.0 * D, 1.0 * FF, 1.0 * FF)):
            square_total = row_sums[layers + i : layers + i + 1, m : m + 1]
            state_total = row_sums[2 * layers + i : 2 * layers + i + 1, 4 + m : 5 + m]
            row_mean = (DECAY * state_total + (1.0 - DECAY) * (square_total / width)) / D
            update_rms = jnp.sqrt(row_mean * sums[i : i + 1, m : m + 1] / (D * width))
            weight_rms = jnp.sqrt(sums[i : i + 1, 4 + m : 5 + m] / (D * width))
            factor = RATE * weight_rms * jnp.sqrt(row_mean) / jnp.maximum(1.0, update_rms)
            columns = slice(cuts[m], cuts[m + 1])
            update = scaled_update(grads, row_inverse, col_inverse, cuts, i, m)
            value = master[i, :, columns] - factor * update
            new[i, :, columns] = value
            new_low[i, :, columns] = value.astype(BF16)


def whole_spec(shape):
    return pl.BlockSpec(shape, lambda *_: (0,) * len(shape))


def in_any(count):
    return [pl.BlockSpec(memory_space=pl.ANY)] * count


def far(arrays):
    return [pltpu.with_memory_space_constraint(array, pltpu.HBM) for array in arrays]


def cost(micros):
    return pl.CostEstimate(
        flops=int(micros * 10**9), bytes_accessed=int(micros * 10**6), transcendentals=0
    )


def chunk_specs(chunks):
    specs = []
    for array, place in chunks:
        if place is None:
            specs.append(whole_spec(array.shape))
        else:
            specs.append(
                pl.BlockSpec((None, *array.shape[1:]), lambda *_, place=place: (place, 0, 0, 0))
            )
    return specs


def rows_spec(rows, width, block_of):
    return pl.BlockSpec((rows, width), lambda t, *_: (block_of(t), 0))


def run_forward(place, chunks, vec, tables, weight, riders=()):
    blocks_out, sources = weight
    chunk = chunks[0][0].shape[-2]
    block, length = 2 * chunk, 4 * chunk
    counts = [len(pieces) for pieces, _ in sources]
    firsts = [first for _, first in sources]
    pieces = [piece for pieces, _ in sources for piece in pieces]
    count = len(pieces)
    out_wide = blocks_out[0].shape[0]
    heads = out_wide // HEAD_DIM
    wide = 3 * out_wide
    quarter = FF * out_wide // D

    def same(t):
        return t

    widths = [
        (D, BF16),
        (2 * out_wide, BF16),
        (out_wide, BF16),
        (out_wide, BF16),
        (quarter, BF16),
        (quarter, BF16),
    ]
    shapes = [pltpu.HBM((length, width), kind) for width, kind in widths]
    specs = [rows_spec(block, width, same) for width, _ in widths]
    shapes.insert(4, pltpu.HBM((8, length), F32))
    specs.insert(4, pl.BlockSpec((8, block), lambda t, *_: (0, t)))
    return pl.pallas_call(
        functools.partial(forward_kernel, counts, firsts),
        grid_spec=pltpu.PrefetchScalarGridSpec(
            num_scalar_prefetch=1,
            grid=(2,),
            in_specs=[
                *chunk_specs(chunks),
                whole_spec((8, D)),
                *[rows_spec(block, 2 * HEAD_DIM, same)] * 3,
                *[whole_spec((out_wide, out_wide))] * 4,
                *in_any(count + len(riders)),
            ],
            out_specs=[whole_spec((2, chunk, D))] * 2 + specs,
            scratch_shapes=[
                pltpu.VMEM((D, wide + out_wide), BF16),
                pltpu.VMEM((D, 2 * quarter), BF16),
                pltpu.VMEM((out_wide, D), BF16),
                pltpu.VMEM((heads, length, HEAD_DIM), BF16),
                pltpu.VMEM((heads, length, HEAD_DIM), BF16),
                pltpu.VMEM((block, D), F32),
                pltpu.SemaphoreType.DMA((count,)),
            ],
        ),
        out_shape=[
            pltpu.HBM((2, chunk, D), BF16),
            jax.ShapeDtypeStruct((2, chunk, D), BF16),
            *shapes,
        ],
        compiler_params=pltpu.CompilerParams(vmem_limit_bytes=VMEM_BYTES),
        cost_estimate=cost(13),
        name="layer_forward",
    )(place, *[array for array, _ in chunks], vec, *far(tables), *blocks_out, *far(pieces), *far(riders))


def run_mlp_backward(place, chunks, vec, weight, saved, split, riders=()):
    pieces, first = weight[1][1]
    sequences = len(chunks)
    chunk = chunks[0][0][0].shape[-2]
    block, length = 2 * chunk, 4 * chunk
    xhat, slope, att, hid = saved[0]
    quarter, out_wide = slope.shape[1], att.shape[1]
    n_blocks = D // out_wide

    def block_of(s):
        return lambda t: jnp.clip(t - 2 * s, 0, 1)

    def once(spec):
        return pl.BlockSpec(spec.block_shape, spec.index_map, pipeline_mode=pl.Buffered(1))

    arrays, in_specs = [], []
    for s in range(sequences):
        arrays += [array for array, _ in chunks[s]] + far(saved[s])
        in_specs += [once(spec) for spec in chunk_specs(chunks[s])]
        in_specs += [rows_spec(block, array.shape[1], block_of(s)) for array in saved[s]]
    shapes, specs = outer_outputs(split, 2 * quarter)
    out_shape, out_specs = [], []
    for s in range(sequences):
        out_shape += [
            pltpu.HBM((length, D), BF16),
            pltpu.HBM((length, quarter), BF16),
            pltpu.HBM((length, D), BF16),
            pltpu.HBM((8, D), F32),
        ]
        out_specs += [
            rows_spec(block, D, block_of(s)),
            rows_spec(block, quarter, block_of(s)),
            rows_spec(block, D, block_of(s)),
            whole_spec((8, D)),
        ]
    out_shape += [jax.ShapeDtypeStruct((out_wide, out_wide), BF16)] * n_blocks + shapes
    out_specs += [whole_spec((out_wide, out_wide))] * n_blocks + [once(spec) for spec in specs]
    results = pl.pallas_call(
        functools.partial(mlp_backward_kernel, len(pieces), first, sequences, len(shapes)),
        grid_spec=pltpu.PrefetchScalarGridSpec(
            num_scalar_prefetch=1,
            grid=(2 * sequences,),
            in_specs=[
                whole_spec((8, D)),
                *in_specs,
                *in_any(len(pieces) + len(riders)),
            ],
            out_specs=out_specs,
            scratch_shapes=[
                pltpu.VMEM((D, 2 * quarter), BF16),
                pltpu.VMEM((out_wide, D), F32),
                pltpu.VMEM((D, quarter), F32),
                pltpu.VMEM((D, quarter), F32),
                pltpu.SemaphoreType.DMA((len(pieces),)),
            ],
        ),
        out_shape=out_shape,
        compiler_params=pltpu.CompilerParams(vmem_limit_bytes=2 * VMEM_BYTES),
        cost_estimate=cost(20),
        name="mlp_backward",
    )(place, vec, *arrays, *far(pieces), *far(riders))
    each = [results[4 * s : 4 * s + 4] for s in range(sequences)]
    rest = results[4 * sequences :]
    return each, rest[:n_blocks], rest[n_blocks:]


def run_attention_backward(
    place, grad, vec, tables, weight, xhat, qk, val, lse, grad_two, riders=()
):
    blocks_out, ((pieces, first), _) = weight
    length = grad.shape[0]
    block, chunk = length // 2, length // 4
    out_wide = blocks_out[0].shape[0]
    heads = out_wide // HEAD_DIM
    wide = 3 * out_wide

    def turned(t):
        return 1 - t

    return pl.pallas_call(
        functools.partial(attention_backward_kernel, len(pieces), first),
        grid_spec=pltpu.PrefetchScalarGridSpec(
            num_scalar_prefetch=1,
            grid=(2,),
            in_specs=[
                rows_spec(block, D, turned),
                whole_spec((8, D)),
                *[rows_spec(block, 2 * HEAD_DIM, turned)] * 3,
                *[whole_spec((out_wide, out_wide))] * 4,
                rows_spec(block, D, turned),
                whole_spec(qk.shape),
                whole_spec(val.shape),
                pl.BlockSpec((8, block), lambda t, *_: (0, 1 - t)),
                rows_spec(block, D, turned),
                *in_any(len(pieces) + len(riders)),
            ],
            out_specs=[
                *[whole_spec((2, chunk, D))] * 2,
                rows_spec(block, wide, turned),
                whole_spec((8, D)),
            ],
            scratch_shapes=[
                pltpu.VMEM((D, wide + out_wide), BF16),
                pltpu.VMEM((out_wide, D), BF16),
                pltpu.VMEM((heads, block, HEAD_DIM), F32),
                pltpu.VMEM((heads, block, HEAD_DIM), F32),
                pltpu.VMEM((block, D), F32),
                pltpu.SemaphoreType.DMA((len(pieces),)),
            ],
        ),
        out_shape=[
            pltpu.HBM((2, chunk, D), BF16),
            jax.ShapeDtypeStruct((2, chunk, D), BF16),
            pltpu.HBM((length, wide), BF16),
            pltpu.HBM((8, D), F32),
        ],
        compiler_params=pltpu.CompilerParams(vmem_limit_bytes=VMEM_BYTES),
        cost_estimate=cost(11),
        name="attention_backward",
    )(
        place,
        *far([grad]),
        vec,
        *far(tables),
        *blocks_out,
        *far([xhat, qk, val, lse, grad_two, *pieces, *riders]),
    )


def outer_outputs(split, columns):
    if split:
        shape = (4, D // 8, columns)
        kinds = [BF16, BF16]
    else:
        shape, kinds = (D, columns), [BF16]
    return [jax.ShapeDtypeStruct(shape, kind) for kind in kinds], [whole_spec(shape)] * len(kinds)


def run_qkv_outer(scalars, vec, groups, outward, split, riders=()):
    arrays = [array for both in zip(*groups) for array in both]
    out_wide = outward[0].shape[1]
    shapes, specs = outer_outputs(split, groups[1][0].shape[1] + out_wide)
    return pl.pallas_call(
        functools.partial(qkv_outer_kernel, len(groups[0]), len(outward), len(shapes)),
        grid_spec=pltpu.PrefetchScalarGridSpec(
            num_scalar_prefetch=1,
            grid=(1,),
            in_specs=[
                whole_spec((8, D)),
                *in_any(len(arrays)),
                *[whole_spec(block.shape) for block in outward],
                *in_any(len(riders)),
            ],
            out_specs=specs,
            scratch_shapes=[
                *[pltpu.VMEM(array.shape, BF16) for array in arrays],
                pltpu.VMEM((D, out_wide), BF16),
                pltpu.SemaphoreType.DMA((len(arrays),)),
            ],
        ),
        out_shape=shapes,
        compiler_params=pltpu.CompilerParams(vmem_limit_bytes=VMEM_BYTES),
        cost_estimate=cost(6),
        name="qkv_outer",
    )(scalars, vec, *far(arrays), *outward, *far(riders))


def run_gradient(sources, row_state, layer, shape, earlier=(), riders=()):
    layers, rows, width = shape
    arrays = [array for source in sources for array in source]
    shapes = [shape, (layers, 8, rows), (layers, 8 * -(-(width // 128 + 1) // 8), 128)]

    def of_layer(shape):
        return pl.BlockSpec((1, *shape[1:]), lambda *_: (layer, 0, 0))

    return pl.pallas_call(
        functools.partial(
            gradient_kernel, [len(source) for source in sources], matrix_cuts(width)
        ),
        grid=(1,),
        in_specs=[
            *[whole_spec(array.shape) for array in arrays],
            of_layer(row_state.shape),
            *in_any(len(earlier) + len(riders)),
        ],
        out_specs=[of_layer(shape) for shape in shapes],
        out_shape=[jax.ShapeDtypeStruct(shape, F32) for shape in shapes],
        input_output_aliases={len(arrays) + 1 + k: k for k in range(len(earlier))},
        compiler_params=pltpu.CompilerParams(vmem_limit_bytes=VMEM_BYTES),
        cost_estimate=cost(2),
        name="gradient",
    )(*arrays, row_state, *earlier, *riders)


def run_whole(kernel, arrays, shapes, name):
    return pl.pallas_call(
        functools.partial(kernel, matrix_cuts(arrays[0].shape[2])),
        grid=(1,),
        in_specs=[whole_spec(array.shape) for array in arrays],
        out_specs=[whole_spec(shape) for shape, _ in shapes],
        out_shape=[jax.ShapeDtypeStruct(shape, kind) for shape, kind in shapes],
        compiler_params=pltpu.CompilerParams(vmem_limit_bytes=VMEM_BYTES),
        cost_estimate=cost(2),
        name=name,
    )(*arrays)


def example_kernel(layers, sequences, scalars, *refs):
    out = refs[-1]
    out[...] = jnp.zeros_like(out)
    seq_place = scalars[0]
    mine = jnp.where(seq_place == 0, 1.0, 0.0)
    for s in range(sequences):
        for i in range(layers):
            of_mlp, of_attention = refs[2 * (i * sequences + s) : 2 * (i * sequences + s) + 2]
            at = s * layers + i
            out[at, 0:2] = of_attention[0:2]
            out[at, 2:4] = of_mlp[0:2]
            out[at, 4:5] = of_mlp[3:4] * mine
            out[at, pl.ds(5 + seq_place, 1)] = of_mlp[2:3]
            wide = 3 * D * D // FF
            out[at, pl.ds(5 + FF // D + seq_place, 1), :wide] = of_attention[2:3, :wide]


def run_example(scalars, sums, sequences):
    arrays = [array for layer in sums for pair in layer for array in pair]
    shape = (sequences * len(sums), 16, D)
    return pl.pallas_call(
        functools.partial(example_kernel, len(sums), sequences),
        grid_spec=pltpu.PrefetchScalarGridSpec(
            num_scalar_prefetch=1,
            grid=(1,),
            in_specs=[whole_spec(array.shape) for array in arrays],
            out_specs=whole_spec(shape),
        ),
        out_shape=jax.ShapeDtypeStruct(shape, F32),
        cost_estimate=cost(1),
        name="examples",
    )(scalars, *arrays)


def example_vector(rows):
    groups = FF // D
    wide = 3 * D // groups
    qkv = [
        part for k in range(groups) for part in natural_heads(rows[5 + groups + k : 6 + groups + k, :wide])
    ]
    up = [rows[5 + k : 6 + k] for k in range(groups)]
    return jnp.concatenate(
        [*[rows[k : k + 1] for k in range(4)], *qkv, rows[4:5], *up, rows[4:5]], axis=1
    )


def small_kernel(length, totals, examples, state, params, grads, moments, new, scores):
    layers = state.shape[0]
    sequences = scores.shape[0]
    lane = lax.broadcasted_iota(jnp.int32, (1, scores.shape[1]), 1)
    row = lax.broadcasted_iota(jnp.int32, totals.shape[1:], 0)
    weight = jnp.where(row == 4, 2.0, 1.0)

    def product(left, right):
        value = jnp.sum(left * right * weight, axis=1, keepdims=True)
        return jnp.sum(value, axis=0, keepdims=True)

    query = [totals[layers + i] for i in range(layers)]
    mean = sum(product(rows, rows) for rows in query) / (layers * SMALL)
    spread = length * layers * SMALL * (mean + 1e-06)
    for s in range(sequences):
        each = [examples[s * layers + i] for i in range(layers)]
        norm = sum(product(rows, rows) for rows in each) / (layers * SMALL * length)
        influence = sum(product(*pair) for pair in zip(each, query)) / jnp.sqrt(spread)
        scores[s : s + 1] = jnp.where(lane == 0, norm, influence)
    edges = [0, D, 2 * D, 3 * D, 4 * D, 7 * D, 8 * D, 8 * D + FF, SMALL]
    for i in range(layers):
        place = slice(i, i + 1)
        gradient = example_vector(totals[i])
        grads[place] = gradient
        moment = DECAY * state[place] + (1.0 - DECAY) * (gradient * gradient + EPS_SQUARE)
        moments[place] = moment
        for first, end in zip(edges, edges[1:]):
            columns = slice(first, end)
            update = gradient[:, columns] * lax.rsqrt(moment[:, columns])
            old = params[place, columns]
            rms = jnp.sqrt(jnp.mean(update * update, axis=1, keepdims=True))
            old_rms = jnp.sqrt(jnp.mean(old * old, axis=1, keepdims=True))
            new[place, columns] = old - RATE * old_rms * (update / jnp.maximum(1.0, rms))


def run_small(length, totals, examples, state, params, sequences):
    arrays = [totals, examples, state, params]
    shapes = [state.shape] * 3 + [(sequences, 128)]
    return pl.pallas_call(
        functools.partial(small_kernel, length),
        grid=(1,),
        in_specs=[whole_spec(array.shape) for array in arrays],
        out_specs=[whole_spec(shape) for shape in shapes],
        out_shape=[jax.ShapeDtypeStruct(shape, F32) for shape in shapes],
        cost_estimate=cost(2),
        name="small_vectors",
    )(*arrays)


def half_spec(array, place, flipped=False):
    def index(h):
        half = 1 - h if flipped else h
        return (half, 0, 0) if place is None else (place, half, 0, 0)

    block = (None, *array.shape[-2:])
    return pl.BlockSpec(block if place is None else (None, *block), index)


def run_finish(kernel, sums, received, others, bias, name):
    keep, near, _ = sums
    shape = keep.shape
    arrays = [(keep, None), (near, None), (received, None), *others]
    specs = [half_spec(array, place, k == 2) for k, (array, place) in enumerate(arrays)]
    return pl.pallas_call(
        kernel,
        grid=(2,),
        in_specs=specs + ([] if bias is None else [whole_spec(bias.shape)]),
        out_specs=[half_spec(keep, None)] * 2,
        out_shape=[pltpu.HBM(shape, F32), jax.ShapeDtypeStruct(shape, BF16)],
        compiler_params=pltpu.CompilerParams(vmem_limit_bytes=VMEM_BYTES),
        cost_estimate=cost(2),
        name=name,
    )(*far([array for array, _ in arrays]), *([] if bias is None else [bias]))


def last_kernel(kernel, count, n_inputs, *refs):
    out = refs[-1]
    bias = refs[count * n_inputs : -1]
    for s in range(count):
        kernel(*refs[n_inputs * s : n_inputs * (s + 1)], *bias, out.at[s])


def run_last(kernel, sums, received, others, bias, kind, name):
    arrays, specs = [], []
    for (keep, near, _), across, more in zip(sums, received, others):
        chunk = keep.shape[-2]
        arrays += [keep, near, across]
        half = pl.BlockSpec((None, chunk, D), lambda i: (0, 0, 0))
        specs += [half, half, whole_spec(across.shape)]
        for array, place in more:
            arrays.append(array)
            if place is None:
                specs.append(half)
            else:
                specs.append(
                    pl.BlockSpec((None, None, chunk, D), lambda i, place=place: (place, 0, 0, 0))
                )
    count = len(sums)
    return pl.pallas_call(
        functools.partial(last_kernel, kernel, count, len(arrays) // count),
        grid=(1,),
        in_specs=specs + ([] if bias is None else [whole_spec(bias.shape)]),
        out_specs=whole_spec((count, chunk, D)),
        out_shape=jax.ShapeDtypeStruct((count, chunk, D), kind),
        compiler_params=pltpu.CompilerParams(vmem_limit_bytes=VMEM_BYTES),
        cost_estimate=cost(2),
        name=name,
    )(*far(arrays), *([] if bias is None else [bias]))


def pass_through_kernel(*refs):
    del refs


def after(values, *others):
    return pl.pallas_call(
        pass_through_kernel,
        in_specs=in_any(1 + len(others)),
        out_specs=pl.BlockSpec(memory_space=pl.ANY),
        out_shape=jax.ShapeDtypeStruct(values.shape, values.dtype),
        input_output_aliases={0: 0},
        name="after",
    )(values, *others)


def out_blocks(columns, dp_place, seq_place):
    stacked = jnp.zeros((D, columns[0].shape[1]), BF16)
    for column, place in zip(columns, piece_places(len(columns), dp_place)):
        stacked = lax.dynamic_update_slice(stacked, column, (place * column.shape[0], 0))
    size = lax.axis_size("seq")
    return exchange_blocks(stacked.reshape(size, D // size, -1), seq_place)


def on_device(block_in, cotangent, labels, master, small_params, row_state, col_state, small_state):
    sequences, chunk = block_in.shape[:2]
    group_count = lax.axis_size("seq")
    seq_place, dp_place = lax.axis_index("seq"), lax.axis_index("dp")
    length = chunk * group_count
    flags = (labels == 0).astype(jnp.int32)
    place = jnp.concatenate(
        [jnp.stack([seq_place % 2, seq_place // 2, dp_place]).astype(jnp.int32), flags]
    )
    train_flag = flags.astype(F32)
    scalars = jnp.concatenate(
        [jnp.stack([dp_place % 2, seq_place]).astype(jnp.int32), flags]
    )
    query_flag = 1.0 - train_flag
    wide, out_wide, quarter = 3 * D // group_count, D // group_count, FF // group_count
    cuts = matrix_cuts(master.shape[2])
    split = lax.axis_size("dp") == 8
    x_bit, z_place = dp_place % 2, dp_place // 2
    tables = rotary_tables(length)

    def normalise(stream):
        scaled, inverse = apply_layer_norm(stream)
        low_scaled = scaled.astype(BF16)
        return (scaled, inverse), low_scaled

    stream = both_halves(block_in)
    _, low_scaled = normalise(stream.astype(F32))
    near = swap(low_scaled, "seq", 1)
    chunks = [((low_scaled, s), (near, s)) for s in range(sequences)]

    low = master.astype(BF16)
    rows_of = [
        jnp.concatenate([heads_together(low[i, :, : cuts[1]]), low[i, :, cuts[1] :]], axis=1)
        for i in range(LAYERS)
    ]
    pieces = gather_rows(rows_of[0])
    whole_one = lax.all_gather(after(rows_of[1], *pieces[4:5]), "dp", axis=0, tiled=True)

    def weight_of(pieces):
        columns = [piece[:, wide : wide + out_wide] for piece in pieces]
        return out_blocks(columns, dp_place, seq_place), [(pieces, 0), (pieces, cuts[2])]

    weights = [weight_of(pieces)]
    vectors, params = [], []
    for i in range(LAYERS):
        param = unpack(small_params[i])
        params.append(param)
        bias_qkv = heads_together(lax.dynamic_slice_in_dim(param[4], seq_place * wide, wide))
        bias_up = lax.dynamic_slice_in_dim(param[6], seq_place * quarter, quarter)
        vectors.append(
            jnp.stack(
                [
                    *param[:4],
                    jnp.pad(bias_up, (0, D - quarter)),
                    jnp.pad(bias_qkv, (0, D - wide)),
                    jnp.zeros((D,), F32),
                    jnp.zeros((D,), F32),
                ]
            )
        )

    streams = [[(stream, s) for s in range(sequences)]]
    saved_all = []
    open_sum = None

    def close_sum(behind):
        nonlocal open_sum
        sums, received, finish = open_sum
        open_sum = None
        finish(sums, after(received, behind))

    def open_exchange(keep, send, behind, finish):
        nonlocal open_sum
        if open_sum is not None:
            send = after(send, open_sum[1])
            close_sum(behind)
        sums = core_sum(keep, send)
        open_sum = (sums, swap(sums[2], "seq", 2), finish)
        return [sums[2]]

    def own_exchange(keep, send):
        near = swap(send, "seq", 1)
        low = (keep[1].astype(F32) + near[1].astype(F32)).astype(BF16)
        return (keep, near, None), swap(low, "seq", 2)

    both_grads = both_halves(cotangent)
    near_grads = swap(both_grads, "seq", 1)
    riders = []
    for i in range(LAYERS):
        last = i == LAYERS - 1
        saved_all.append([])
        next_chunks, next_streams, ends = [], [], []
        bias = (params[i][5] + params[i][7])[None]

        def finish_stream(s, old, bias, next_chunks, next_streams, sums, received):
            fresh, low = run_finish(
                finish_stream_kernel, sums, received, [old], bias, "finish_stream"
            )
            next_streams.append((fresh, None))
            next_chunks.append(((low, None), (swap(low, "seq", 1), None)))

        for s in range(sequences):
            keep, send, *saved = run_forward(
                place, chunks[s], vectors[i], tables, weights[i], riders
            )
            saved_all[i].append(saved)
            if last:
                if open_sum is not None:
                    send = after(send, open_sum[1])
                    close_sum(saved[0])
                ends.append(own_exchange(keep, send))
                continue
            riders = open_exchange(
                keep,
                send,
                saved[0],
                functools.partial(
                    finish_stream, s, streams[i][s], bias, next_chunks, next_streams
                ),
            )
            if i == 0:
                riders = riders + [near_grads]
        if i == 0:
            whole_one = after(whole_one, saved_all[0][0][0])
            weights.append(weight_of([whole_one]))
        if last:
            break
        chunks = next_chunks
        streams.append(next_streams)
    block_out = run_last(
        finish_stream_kernel,
        [sums for sums, _ in ends],
        [received for _, received in ends],
        [[old] for old in streams[-1]],
        bias,
        BF16,
        "block_out",
    )

    grads = [(both_grads, s) for s in range(sequences)]
    chunks = [((both_grads, s), (near_grads, s)) for s in range(sequences)]
    sources, sums = [None] * LAYERS, [None] * LAYERS
    riders, later, latest = [], [], []
    for i in reversed(range(LAYERS)):
        last = i == 0
        xhats, qks, vals, atts, lses, hids, slopes = zip(*saved_all[i])
        mlp, attention, next_chunks, next_grads, ends = [], [], [], [], []

        def finish_grad(s, others, next_chunks, next_grads, sums, received):
            fresh, low = run_finish(
                finish_grad_kernel, sums, received, others, None, "finish_grad"
            )
            next_grads.append((fresh, None))
            next_chunks.append(((low, None), (swap(low, "seq", 1), None)))

        if open_sum is not None:
            close_sum(riders[0])
        mlp, outward, both = run_mlp_backward(
            place,
            chunks,
            vectors[i],
            weights[i],
            list(zip(xhats, slopes, atts, hids)),
            split,
            [*riders, *later],
        )
        outward = [
            block if k == 0 else swap(block, "seq", k) for k, block in enumerate(outward)
        ]
        riders = [both[-1], *latest] if last else [both[-1], block_out]
        for s in range(sequences):
            keep, send, grad_joined, sums_t = run_attention_backward(
                place,
                mlp[s][0],
                vectors[i],
                tables,
                weights[i],
                xhats[s],
                qks[s],
                vals[s],
                lses[s],
                mlp[s][2],
                riders,
            )
            attention.append((grad_joined, sums_t))
            if last:
                riders = []
                ends.append(own_exchange(keep, send))
            else:
                riders = open_exchange(
                    keep,
                    send,
                    grad_joined,
                    functools.partial(
                        finish_grad, s, [grads[s], streams[i][s]], next_chunks, next_grads
                    ),
                )
                if s == 0:
                    riders = riders + outward
        if split and not last:
            total_b = pair_total(*both)
            part_b = scatter_along_z(total_b)
        if split and last:
            total_b = pair_total(after(both[0], *[out[0] for out in attention]), both[1])
            part_b = scatter_along_z(total_b)
            riders = [total_b]
        elif not split:
            part_b = lax.psum_scatter(both[0], "dp", scatter_dimension=0, tiled=True)
        groups = [xhats, [out[0] for out in attention]]
        rest = run_qkv_outer(scalars, vectors[i], groups, outward, split, riders)
        if not split:
            part_a = [lax.psum_scatter(rest[0], "dp", scatter_dimension=0, tiled=True)]
        elif last:
            own_a, parts_a = pair_sum(after(rest[0], part_b), rest[1], z_place)
            part_a = [own_a, *exchange_parts(parts_a)]
        else:
            total_a = pair_total(*rest)
            part_a = [scatter_along_z(total_a)]
            later, latest = [total_b], [total_a]
        sources[i] = [[part_b], part_a]
        riders = rest[:1]
        chunks = next_chunks
        grads = next_grads or grads
        sums[i] = [(out[3], other[1]) for out, other in zip(mlp, attention)]
    behind_a = parts_a[:1] if split else rest
    grad_stream = run_last(
        finish_grad_kernel,
        [sums_of for sums_of, _ in ends],
        [after(received, *behind_a) for _, received in ends],
        [[grad, old] for grad, old in zip(grads, streams[0])],
        None,
        F32,
        "input_grad",
    )

    examples = after(run_example(scalars[1:2], sums, sequences), *behind_a)
    examples = sum_pairwise(examples, "seq", BF16)
    stacked = ()
    for i in reversed(range(LAYERS)):
        behind = [] if i else [examples, grad_stream]
        stacked = run_gradient(sources[i], row_state, i, master.shape, stacked, behind)
    reduced_all, row_part, col_part = stacked
    dp_bits, seq_bits = [], []
    for axis, bits in (("dp", dp_bits), ("seq", seq_bits)):
        bits += [(axis, 1 << k) for k in range(lax.axis_size(axis).bit_length() - 1)]
    first_steps = max(len(seq_bits), len(dp_bits))
    flat = examples.reshape(sequences, -1)
    small = jnp.stack(
        [
            jnp.sum(train_flag[:, None] * flat, axis=0),
            jnp.sum((1.0 - train_flag)[:, None] * flat, axis=0),
        ]
    ).reshape(2 * LAYERS, *examples.shape[1:])
    small_steps = list(dp_bits)

    def small_step():
        nonlocal small_steps
        step, *small_steps = small_steps
        sent = small.astype(BF16)
        return sent, swap(sent, *step)

    def together(values):
        nonlocal small
        received = [swap(value, *step) for value, step in values]
        sent = None
        if small_steps:
            sent, small_in = small_step()
            received.append(small_in)
        if len(received) > 1:
            received = [
                after(value, *[other for other in received if other is not value])
                for value in received
            ]
        if sent is not None:
            small = sent.astype(F32) + received.pop().astype(F32)
        return [value + other for (value, _), other in zip(values, received)]

    for k in range(first_steps):
        now = []
        if k < len(seq_bits):
            now.append((row_part, seq_bits[k]))
        if k < len(dp_bits):
            now.append((col_part, dp_bits[k]))
        *rest_sums, last_sum = together(now)
        if k < len(seq_bits) and k < len(dp_bits):
            (row_part,), col_part = rest_sums, last_sum
        elif k < len(dp_bits):
            col_part = last_sum
        else:
            row_part = last_sum
    layers = master.shape[0]
    fresh_row_moments, col_stats, local_sums = run_whole(
        square_kernel,
        [reduced_all, master, row_part, col_part, row_state, col_state],
        [(row_state.shape, F32), (col_state.shape, F32), ((8, 128), F32)],
        "squares",
    )
    state_sums = local_sums
    for step in seq_bits:
        (local_sums,) = together([(local_sums, step)])
    seq_sums = jnp.concatenate(
        [local_sums[: 2 * layers], state_sums[layers : 2 * layers], local_sums[3 * layers :]], axis=0
    )
    for step in dp_bits:
        (local_sums,) = together([(local_sums, step)])
    while small_steps:
        together([])
    small_grads, small_moments, small_new, scores = run_small(
        length, small, examples, small_state, small_params, sequences
    )
    example_norms, influence = scores[:, 0], scores[:, 1]
    new_master, new_low = run_whole(
        update_kernel,
        [reduced_all, master, fresh_row_moments, col_stats, local_sums, seq_sums],
        [(master.shape, F32), (master.shape, BF16)],
        "update",
    )
    return (
        block_out,
        grad_stream,
        example_norms,
        influence,
        reduced_all,
        fresh_row_moments,
        col_stats,
        new_master,
        new_low,
        small_grads,
        small_moments,
        small_new,
    )


def solution(mesh):
    placed = (
        P("dp", "seq", None),
        P("dp", "seq", None),
        P("dp"),
        P(None, "dp", "seq"),
        P(),
        P(None, None, "dp"),
        P(None, "seq"),
        P(),
    )
    return jax.shard_map(
        on_device,
        mesh=mesh,
        in_specs=placed,
        out_specs=(
            P("dp", "seq", None),
            P("dp", "seq", None),
            P("dp"),
            P("dp"),
            P(None, "dp", "seq"),
            P(None, None, "dp"),
            P(None, "seq"),
            P(None, "dp", "seq"),
            P(None, "dp", "seq"),
            P(),
            P(),
            P(),
        ),
        check_vma=False,
    )
```

```python
import functools

import jax
import numpy as np
import jax.numpy as jnp
from jax import lax
from jax.experimental import pallas as pl
from jax.experimental.pallas import tpu as pltpu
from jax.sharding import PartitionSpec as P

D = 768
HEADS = 12
FF = 3072
LAYERS = 2
HEAD_DIM = 64
ROT = 16
SMALL = 9984

EPS_NORM = 1e-05
EPS_SQUARE = 1e-30
RATE = 0.5
DECAY = 0.5
NEG_LARGE = -1e30
SCORE_SCALE = HEAD_DIM ** (-0.5)
CONTRACT_LAST = (((1,), (1,)), ((), ()))
CONTRACT_FIRST = (((0,), (0,)), ((), ()))
VMEM_BYTES = 24 * 1024 * 1024
BF16 = jnp.bfloat16
F32 = jnp.float32


def unpack(vector):
    return jnp.split(vector, [D, 2 * D, 3 * D, 4 * D, 7 * D, 8 * D, 8 * D + FF], axis=-1)


def apply_layer_norm(inputs):
    centred = inputs - jnp.mean(inputs, axis=-1, keepdims=True)
    variance = jnp.mean(centred * centred, axis=-1, keepdims=True)
    inverse = lax.rsqrt(variance + EPS_NORM)
    return (centred * inverse, inverse)


def norm_back(grad_scaled, scaled, inverse):
    mean_grad = jnp.mean(grad_scaled, axis=-1, keepdims=True)
    mean_cross = jnp.mean(grad_scaled * scaled, axis=-1, keepdims=True)
    return (grad_scaled - mean_grad - scaled * mean_cross) * inverse


def rotary_tables(length):
    halfway = ROT // 2
    frequency = 10000.0 ** (-2.0 * np.arange(halfway) / ROT)
    angles = np.arange(length)[:, None] * frequency[None, :]
    cosine, sine = np.cos(angles), np.sin(angles)
    rest = np.ones((length, HEAD_DIM - ROT))
    none = np.zeros((length, halfway))
    keep = np.concatenate([cosine, cosine, rest], axis=1)
    ahead = np.concatenate([-sine, none, 0.0 * rest], axis=1)
    behind = np.concatenate([none, sine, 0.0 * rest], axis=1)
    return tuple(
        jnp.asarray(np.concatenate([table, table], axis=1), F32) for table in (keep, ahead, behind)
    )


def swap(values, axis, bits):
    size = lax.axis_size(axis)
    return lax.ppermute(values, axis, [(i, i ^ bits) for i in range(size)])


def sum_pairwise(values, axis, wire=F32):
    bits = 1
    while bits < lax.axis_size(axis):
        sent = values.astype(wire)
        values = sent.astype(F32) + swap(sent, axis, bits).astype(F32)
        bits *= 2
    return values


def both_halves(own):
    return jnp.stack([own, swap(own, "seq", 2)], axis=-3)


def core_sum(keep, send):
    received = swap(send, "seq", 1)
    return keep, received, (keep.astype(F32) + received.astype(F32)).astype(BF16)


def gather_rows(rows):
    if lax.axis_size("dp") != 8:
        return [lax.all_gather(rows, "dp", axis=0, tiled=True)]
    pieces = []
    for k in range(4):
        pieces += [rows, swap(rows, "dp", 1)]
        if k < 3:
            rows = lax.ppermute(rows, "dp", [(i, (i + 2) % 8) for i in range(8)])
    return pieces


def piece_places(count, dp_place):
    if count == 1:
        return [0]
    return [(dp_place + 8 - 2 * (k // 2)) % 8 ^ (k % 2) for k in range(count)]


def pair_sum(keep, send, z_place):
    summed = keep.astype(F32) + swap(send, "dp", 1).astype(F32)
    own = lax.dynamic_index_in_dim(summed, z_place, 0, keepdims=False)
    return own, [
        lax.dynamic_index_in_dim(summed, z_place ^ k, 0, keepdims=False).astype(BF16)
        for k in range(1, summed.shape[0])
    ]


def pair_total(keep, send):
    total = keep.astype(F32) + swap(send, "dp", 1).astype(F32)
    return total.astype(BF16).reshape(-1, keep.shape[-1])


def scatter_along_z(total):
    groups = [[2 * z + x for z in range(4)] for x in range(2)]
    return lax.psum_scatter(
        total, "dp", scatter_dimension=0, tiled=True, axis_index_groups=groups
    )


def exchange_parts(parts):
    return [swap(part, "dp", 2 * (k + 1)) for k, part in enumerate(parts)]


def exchange_blocks(blocks, index):
    size = lax.axis_size("seq")
    received = []
    for k in range(size):
        block = lax.dynamic_index_in_dim(blocks, index ^ k, 0, keepdims=False)
        received.append(block if k == 0 else swap(block, "seq", k))
    return received


def heads_together(values):
    heads = values.shape[-1] // (3 * HEAD_DIM)
    lead = values.shape[:-1]
    by_head = values.reshape(*lead, heads, 3 * HEAD_DIM)
    return jnp.concatenate(
        [
            by_head[..., : 2 * HEAD_DIM].reshape(*lead, heads * 2 * HEAD_DIM),
            by_head[..., 2 * HEAD_DIM :].reshape(*lead, heads * HEAD_DIM),
        ],
        axis=-1,
    )


def heads_apart(values):
    heads = values.shape[-1] // (3 * HEAD_DIM)
    lead = values.shape[:-1]
    pairs, last = jnp.split(values, [heads * 2 * HEAD_DIM], axis=-1)
    return jnp.concatenate(
        [
            pairs.reshape(*lead, heads, 2 * HEAD_DIM),
            last.reshape(*lead, heads, HEAD_DIM),
        ],
        axis=-1,
    ).reshape(values.shape)


def halves(core_bit, chunk):
    own = pl.multiple_of(core_bit * chunk, chunk)
    return pl.ds(own, chunk), pl.ds(pl.multiple_of(chunk - own, chunk), chunk)


def place_tokens(dst, own, near, core_bit, y_here, chunk):
    at_own, at_near = halves(core_bit, chunk)
    dst[at_own] = own[y_here]
    dst[at_near] = near[y_here]


def spread_tokens(value, held, keep, send, core_bit, y_here, chunk):
    at_own, at_near = halves(core_bit, chunk)
    held[...] = value
    keep[pl.ds(y_here, 1)] = held[at_own].astype(keep.dtype)[None]
    send[pl.ds(y_here, 1)] = held[at_near].astype(send.dtype)[None]


def gelu_and_slope(v):
    magnitude = jnp.abs(v) * 0.7071067811865476
    bottom = 1.0 + 0.3275911 * magnitude
    t = pl.reciprocal(bottom, approx=True)
    t = t * (2.0 - bottom * t)
    t = t * (2.0 - bottom * t)
    falling = jnp.exp(-0.5 * v * v)
    poly = t * (
        0.254829592
        + t * (-0.284496736 + t * (1.421413741 + t * (-1.453152027 + t * 1.061405429)))
    )
    tail = 0.5 * poly * falling
    cdf = jnp.where(v >= 0.0, 1.0 - tail, tail)
    return v * cdf, cdf + v * falling * 0.3989422804014327


def weight_copies(dp_place, sources, targets, sems):
    copies = []
    for (pieces, first), target in zip(sources, targets):
        rows, width = pieces[0].shape[0], target.shape[1]
        for piece, place in zip(pieces, piece_places(len(pieces), dp_place)):
            offset = 0 if len(pieces) == 1 else pl.multiple_of(place * rows, 16)
            copies.append(
                pltpu.make_async_copy(
                    piece.at[:, pl.ds(first, width)],
                    target.at[pl.ds(offset, rows), :],
                    sems.at[len(copies)],
                )
            )
    return copies


def place_columns(whole, blocks, place):
    width = blocks[0].shape[1]
    seq_place = 2 * place[1] + place[0]
    for index in range(len(blocks)):

        @pl.when(seq_place == index)
        def _():
            for k, block in enumerate(blocks):
                at = width * (index ^ k)
                whole[:, at : at + width] = block[...]


def start_all(copies):
    for copy in copies:
        copy.start()


def wait_all(copies):
    for copy in copies:
        copy.wait()


def turn(pair, tables, sign):
    keep_tab, ahead_tab, behind_tab = tables
    ahead = pltpu.roll(pair, 2 * HEAD_DIM - ROT // 2, 1) * ahead_tab[...]
    behind = pltpu.roll(pair, ROT // 2, 1) * behind_tab[...]
    return pair * keep_tab[...] + sign * (ahead + behind)


def forward_kernel(counts, firsts, place, *refs):
    refs = list(refs)

    def take(count):
        taken, refs[:] = refs[:count], refs[count:]
        return taken

    own, near, vec = take(3)
    tables = take(3)
    blocks_out = take(4)
    pieces = [take(count) for count in counts]
    keep, send, xhat, qk, val, att, lse, hid, slope = refs[-16:-7]
    whole_a, whole_b, w_out, k_all, v_all, held, sems = refs[-7:]
    core_bit, y_bit, dp_place = place[0], place[1], place[2]
    step = pl.program_id(0)
    wide = 3 * val.shape[1]
    sources = list(zip(pieces, firsts))
    copies = weight_copies(dp_place, sources, [whole_a, whole_b], sems)

    @pl.when(step == 0)
    def _():
        start_all(copies)
        place_columns(w_out, blocks_out, place)

    chunk = own.shape[1]
    block = 2 * chunk
    y_here = step ^ y_bit
    place_tokens(xhat, own, near, core_bit, y_here, chunk)
    heads = val.shape[-1] // HEAD_DIM
    quarter = hid.shape[-1]
    row = lax.broadcasted_iota(jnp.int32, (block, block), 0)
    column = lax.broadcasted_iota(jnp.int32, (block, block), 1)
    lane = lax.broadcasted_iota(jnp.int32, (block, 128), 1)

    def attend(here, h, joined, log_sums):
        at_q, at_k = 2 * HEAD_DIM * h, 2 * HEAD_DIM * h + HEAD_DIM
        turned = turn(joined[:, at_q : at_k + HEAD_DIM], tables, 1.0)
        qk[:, at_q : at_k + HEAD_DIM] = turned.astype(BF16)
        k_all[h, block * here : block * (here + 1)] = turned[:, HEAD_DIM:].astype(BF16)
        first = 2 * HEAD_DIM * heads + HEAD_DIM * h
        v_all[h, block * here : block * (here + 1)] = joined[:, first : first + HEAD_DIM].astype(
            BF16
        )
        query = qk[:, at_q : at_q + HEAD_DIM] * jnp.asarray(SCORE_SCALE, BF16)
        scores = []
        for j in range(here + 1):
            part = lax.dot_general(
                query,
                k_all[h, block * j : block * (j + 1)],
                CONTRACT_LAST,
                preferred_element_type=F32,
            )
            if j == here:
                part = jnp.where(column <= row, part, NEG_LARGE)
            scores.append(part)
        largest = functools.reduce(
            jnp.maximum, [jnp.max(part, axis=-1, keepdims=True) for part in scores]
        )
        total = 0.0
        mixed = 0.0
        for j, part in enumerate(scores):
            exponent = jnp.exp(part - largest)
            total = total + jnp.sum(exponent, axis=-1, keepdims=True)
            mixed = mixed + jnp.dot(
                exponent.astype(BF16),
                v_all[h, block * j : block * (j + 1)],
                preferred_element_type=F32,
            )
        att[:, HEAD_DIM * h : HEAD_DIM * (h + 1)] = (mixed / total).astype(BF16)
        return jnp.where(lane == h, largest + jnp.log(total), log_sums)

    for here in range(2):

        @pl.when(step == here)
        def _():
            scaled = xhat[...].astype(F32)
            normed_one = (scaled * vec[0:1] + vec[1:2]).astype(BF16)
            normed_two = (scaled * vec[2:3] + vec[3:4]).astype(BF16)
            if here == 0:
                wait_all(copies)
            joined = (
                jnp.dot(normed_one, whole_a[:, :wide], preferred_element_type=F32) + vec[5:6, :wide]
            )
            val[...] = joined[:, 2 * HEAD_DIM * heads :].astype(BF16)
            hidden_pre = (
                jnp.dot(normed_two, whole_b[:, :quarter], preferred_element_type=F32)
                + vec[4:5, :quarter]
            )
            log_sums = jnp.zeros((block, 128), F32)
            for h in range(heads):
                log_sums = attend(here, h, joined, log_sums)
            lse[...] = log_sums.T[:8]
            hidden, gradient = gelu_and_slope(hidden_pre)
            hid[...] = hidden.astype(BF16)
            slope[...] = gradient.astype(BF16)
            partial = jnp.dot(att[...], w_out[...], preferred_element_type=F32) + lax.dot_general(
                hid[...], whole_b[:, quarter:], CONTRACT_LAST, preferred_element_type=F32
            )
            spread_tokens(partial, held, keep, send, core_bit, y_here, chunk)


def normalised(stream):
    centred = stream - jnp.mean(stream, axis=-1, keepdims=True)
    variance = jnp.mean(centred * centred, axis=-1, keepdims=True)
    inverse = lax.rsqrt(variance + EPS_NORM)
    return centred * inverse, inverse


def seq_sum(keep, near, across):
    return keep[...].astype(F32) + near[...].astype(F32) + across[...].astype(F32)


def finish_stream_kernel(keep, near, across, stream, bias, out, *low):
    value = stream[...].astype(F32) + seq_sum(keep, near, across) + bias[...]
    out[...] = value.astype(out.dtype)
    if low:
        low[0][...] = normalised(value)[0].astype(BF16)


def finish_grad_kernel(keep, near, across, grad, stream, out, *low):
    scaled, inverse = normalised(stream[...].astype(F32))
    back = norm_back(seq_sum(keep, near, across), scaled, inverse)
    value = grad[...].astype(F32) + back
    out[...] = value
    if low:
        low[0][...] = value.astype(BF16)


def add_up(sums, place_row, values):
    sums[place_row : place_row + 1, : values.shape[-1]] += jnp.sum(
        values.astype(F32), axis=0, keepdims=True
    )


def mlp_backward_kernel(count, first, sequences, n_outs, place, vec, *refs):
    refs = list(refs)

    def take(number):
        taken, refs[:] = refs[:number], refs[number:]
        return taken

    inputs = [take(6) for _ in range(sequences)]
    pieces = take(count)
    n_blocks = D // inputs[0][4].shape[1]
    whole_b, product, sum_up, sum_down, sems = refs[-5:]
    del refs[: -5 - 4 * sequences - n_blocks - n_outs]
    outputs = [take(4) for _ in range(sequences)]
    outward, outs = take(n_blocks), take(n_outs)
    core_bit, y_bit, dp_place = place[0], place[1], place[2]
    step = pl.program_id(0)
    copies = weight_copies(dp_place, [(pieces, first)], [whole_b], sems)
    quarter = sum_up.shape[1]

    @pl.when(step == 0)
    def _():
        start_all(copies)
        product[...] = jnp.zeros_like(product)
        sum_up[...] = jnp.zeros_like(sum_up)
        sum_down[...] = jnp.zeros_like(sum_down)

    def one_block(s):
        own, near, xhat, slope, att, hid = inputs[s]
        grad, grad_pre, grad_two, sums = outputs[s]
        chunk = own.shape[1]
        half = step - 2 * s
        place_tokens(grad, own, near, core_bit, half ^ y_bit, chunk)

        @pl.when(half == 0)
        def _():
            sums[...] = jnp.zeros_like(sums)
            if s == 0:
                wait_all(copies)

        flag = place[3 + s] > 0
        scaled = xhat[...].astype(F32)
        grad_hidden = jnp.dot(grad[...], whole_b[:, quarter:], preferred_element_type=F32)
        low_pre = (grad_hidden * slope[...].astype(F32)).astype(BF16)
        grad_pre[...] = low_pre
        normed = lax.dot_general(
            low_pre, whole_b[:, :quarter], CONTRACT_LAST, preferred_element_type=F32
        )
        grad_two[...] = (normed * vec[2:3]).astype(BF16)
        kept = jnp.where(flag, grad[...], jnp.zeros_like(grad))
        kept_pre = jnp.where(flag, low_pre, jnp.zeros_like(low_pre))
        forward_normed = (scaled * vec[2:3] + vec[3:4]).astype(BF16)
        product[...] += lax.dot_general(
            att[...], kept, CONTRACT_FIRST, preferred_element_type=F32
        )
        sum_up[...] += lax.dot_general(
            forward_normed, kept_pre, CONTRACT_FIRST, preferred_element_type=F32
        )
        sum_down[...] += lax.dot_general(
            kept, hid[...], CONTRACT_FIRST, preferred_element_type=F32
        )
        add_up(sums, 0, normed * scaled)
        add_up(sums, 1, normed)
        add_up(sums, 2, low_pre)
        add_up(sums, 3, grad[...])

    for s in range(sequences):

        @pl.when(step // 2 == s)
        def _():
            one_block(s)

    @pl.when(step == 2 * sequences - 1)
    def _():
        store_rows(sum_up, outs, 0, dp_place % 2)
        store_rows(sum_down, outs, quarter, dp_place % 2)
        width = outward[0].shape[1]
        for index in range(n_blocks):

            @pl.when(2 * y_bit + core_bit == index)
            def _():
                for k, block in enumerate(outward):
                    at = width * (index ^ k)
                    block[...] = product[:, at : at + width].astype(BF16)


def attention_backward_kernel(count, first, place, *refs):
    refs = list(refs)

    def take(number):
        taken, refs[:] = refs[:number], refs[number:]
        return taken

    grad, vec = take(2)
    tables = take(3)
    blocks_out = take(4)
    xhat, qk, val, lse, grad_two = take(5)
    pieces = take(count)
    keep, send, grad_joined, sums = refs[-10:-6]
    whole_a, w_out, dk_all, dv_all, held, sems = refs[-6:]
    core_bit, y_bit, dp_place = place[0], place[1], place[2]
    step = 1 - pl.program_id(0)
    copies = weight_copies(dp_place, [(pieces, first)], [whole_a], sems)

    @pl.when(step == 1)
    def _():
        start_all(copies)
        sums[...] = jnp.zeros_like(sums)
        place_columns(w_out, blocks_out, place)

    block = grad.shape[0]
    chunk = block // 2
    heads = val.shape[-1] // HEAD_DIM
    row = lax.broadcasted_iota(jnp.int32, (block, block), 0)
    column = lax.broadcasted_iota(jnp.int32, (block, block), 1)

    def attend_back(here, h, near_grad):
        at_q, at_k = 2 * HEAD_DIM * h, 2 * HEAD_DIM * h + HEAD_DIM
        at_v = 2 * HEAD_DIM * heads + HEAD_DIM * h
        query = qk[block * here : block * (here + 1), at_q:at_k]
        query = query * jnp.asarray(SCORE_SCALE, BF16)
        log_row = lse[h : h + 1]
        probs, grad_probs, keys = [], [], []
        delta = 0.0
        for j in range(here + 1):
            key = qk[block * j : block * (j + 1), at_k : at_k + HEAD_DIM]
            value = val[block * j : block * (j + 1), HEAD_DIM * h : HEAD_DIM * (h + 1)]
            scores = lax.dot_general(key, query, CONTRACT_LAST, preferred_element_type=F32)
            prob = jnp.exp(scores - log_row)
            if j == here:
                prob = jnp.where(row <= column, prob, 0.0)
            grad_prob = lax.dot_general(
                value, near_grad, CONTRACT_LAST, preferred_element_type=F32
            )
            delta = delta + jnp.sum(prob * grad_prob, axis=0, keepdims=True)
            probs.append(prob)
            grad_probs.append(grad_prob)
            keys.append(key)
        dq = 0.0
        for j in range(here + 1):
            grad_score = (probs[j] * (grad_probs[j] - delta)).astype(BF16)
            dk = jnp.dot(grad_score, query, preferred_element_type=F32)
            dv = jnp.dot(probs[j].astype(BF16), near_grad, preferred_element_type=F32)
            dq = dq + lax.dot_general(
                grad_score, keys[j], CONTRACT_FIRST, preferred_element_type=F32
            )
            if j < here:
                dk_all[h], dv_all[h] = dk, dv
            elif here == 0:
                dk, dv = dk + dk_all[h], dv + dv_all[h]
        pair = jnp.concatenate([dq * SCORE_SCALE, dk], axis=1)
        grad_joined[:, at_q : at_q + 2 * HEAD_DIM] = turn(pair, tables, -1.0).astype(BF16)
        grad_joined[:, at_v : at_v + HEAD_DIM] = dv.astype(BF16)

    for here in (1, 0):

        @pl.when(step == here)
        def _():
            grad_att = lax.dot_general(
                grad[...], w_out[...], CONTRACT_LAST, preferred_element_type=F32
            ).astype(BF16)
            for h in range(heads):
                attend_back(here, h, grad_att[:, HEAD_DIM * h : HEAD_DIM * (h + 1)])
            if here == 1:
                wait_all(copies)
            normed = lax.dot_general(
                grad_joined[...],
                whole_a[:, : grad_joined.shape[1]],
                CONTRACT_LAST,
                preferred_element_type=F32,
            )
            spread_tokens(
                normed * vec[0:1] + grad_two[...].astype(F32),
                held,
                keep,
                send,
                core_bit,
                step ^ y_bit,
                chunk,
            )
            add_up(sums, 0, normed * xhat[...].astype(F32))
            add_up(sums, 1, normed)
            add_up(sums, 2, grad_joined[...])


def fetch(sources, targets, sems):
    copies = [
        pltpu.make_async_copy(source, target, sems.at[k])
        for k, (source, target) in enumerate(zip(sources, targets))
    ]
    start_all(copies)
    return copies


def outer_sum(flags, pairs):
    total = 0.0
    for flag, pair in zip(flags, pairs):
        left, right = pair()
        kept = jnp.where(flag > 0, right, jnp.zeros_like(right))
        total = total + lax.dot_general(left, kept, CONTRACT_FIRST, preferred_element_type=F32)
    return total


def store_rows(value, outs, first, x_bit):
    columns = pl.ds(first, value.shape[1])
    if len(outs) == 1:
        outs[0][:, columns] = value[...].astype(BF16)
        return
    keep, send = outs
    rows = keep.shape[1]
    for bit in (0, 1):

        @pl.when(x_bit == bit)
        def _():
            for z in range(keep.shape[0]):
                at = rows * (2 * z + bit)
                to = rows * (2 * z + 1 - bit)
                keep[z, :, columns] = value[at : at + rows].astype(BF16)
                send[z, :, columns] = value[to : to + rows].astype(BF16)


def qkv_outer_kernel(count, n_blocks, n_outs, scalars, vec, *refs):
    sources, blocks = refs[: 2 * count], refs[2 * count : 2 * count + n_blocks]
    held, outward, sems = refs[-2 * count - 2 : -2], refs[-2], refs[-1]
    outs = refs[-2 * count - 2 - n_outs : -2 * count - 2]
    copies = fetch(sources, held, sems)
    x_bit, flags = scalars[0], [scalars[2 + s] for s in range(count)]

    def pair_of(s):
        def pair():
            copies[2 * s].wait()
            copies[2 * s + 1].wait()
            normed = held[2 * s][...].astype(F32) * vec[0:1] + vec[1:2]
            return normed.astype(BF16), held[2 * s + 1][...]

        return pair

    rows = blocks[0].shape[0]
    for k, block in enumerate(blocks):
        outward[pl.ds(pl.multiple_of((scalars[1] ^ k) * rows, 16), rows)] = block[...]
    wide = held[1].shape[1]
    store_rows(outward[...].astype(F32), outs, wide, x_bit)
    store_rows(outer_sum(flags, [pair_of(s) for s in range(count)]), outs, 0, x_bit)


def natural_heads(values):
    heads = values.shape[1] // (3 * HEAD_DIM)
    parts = []
    for h in range(heads):
        parts.append(values[:, 2 * HEAD_DIM * h : 2 * HEAD_DIM * (h + 1)])
        at = 2 * HEAD_DIM * heads + HEAD_DIM * h
        parts.append(values[:, at : at + HEAD_DIM])
    return parts


def matrix_cuts(width):
    unit = width // 12
    return [0, 3 * unit, 4 * unit, 8 * unit, width]


def gradient_kernel(counts, cuts, *refs):
    refs = list(refs)
    row_state, (grads, row_sums, col_sums) = refs[sum(counts)], refs[-3:]
    parts = []
    for count in counts:
        taken, refs[:] = refs[:count], refs[count:]
        parts.append(sum(ref[...].astype(F32) for ref in taken))
    both, rest = parts
    at = 0
    for part in natural_heads(rest[:, : cuts[1]]):
        grads[0, :, at : at + part.shape[1]] = part
        at += part.shape[1]
    grads[0, :, cuts[1] : cuts[2]] = rest[:, cuts[1] :]
    grads[0, :, cuts[2] :] = both
    whole = grads[0]
    squares = whole * whole + EPS_SQUARE
    by_column = jnp.sum(squares, axis=0, keepdims=True)
    lanes = whole.shape[1] // 128
    row = lax.broadcasted_iota(jnp.int32, (whole.shape[0], 128), 1)
    lane = lax.broadcasted_iota(jnp.int32, (1, 128), 1)
    by_row = jnp.zeros((whole.shape[0], 128), F32)
    for m in range(4):
        total = jnp.sum(squares[:, cuts[m] : cuts[m + 1]], axis=1, keepdims=True)
        by_row = jnp.where(row == m, total, by_row)
    row_sums[0] = by_row.T[:8]
    totals = jnp.sum(by_row, axis=0, keepdims=True)
    states = jnp.sum(row_state[0], axis=1, keepdims=True)
    for m in range(4):
        totals = jnp.where(lane == 4 + m, states[m : m + 1], totals)
    col_sums[0] = jnp.zeros_like(col_sums[0])
    for k in range(lanes):
        col_sums[0, k : k + 1] = by_column[:, 128 * k : 128 * (k + 1)]
    col_sums[0, lanes : lanes + 1] = totals


def in_a_row(rows):
    return jnp.concatenate([rows[k : k + 1] for k in range(rows.shape[0])], axis=1)


def upright(rows):
    padded = jnp.concatenate([rows, jnp.zeros((4, rows.shape[1]), F32)], axis=0)
    spare = -rows.shape[1] % 128
    if spare:
        padded = jnp.concatenate([padded, jnp.zeros((8, spare), F32)], axis=1)
    return padded.T[: rows.shape[1]]


def scaled_update(grads, row_inverse, col_inverse, cuts, i, m):
    columns = slice(cuts[m], cuts[m + 1])
    return grads[i, :, columns] * row_inverse[:, m : m + 1] * col_inverse[:, columns]


def square_kernel(cuts, grads, master, rows, cols, row_state, col_state, fresh, stats, sums):
    layers = grads.shape[0]
    lanes = cuts[4] // 128
    lane = lax.broadcasted_iota(jnp.int32, (1, 128), 1)
    matrix = lax.broadcasted_iota(jnp.int32, (4, 1), 0)
    widths = jnp.where(matrix == 0, 3.0 * D, jnp.where(matrix == 1, 1.0 * D, 1.0 * FF))
    sums[...] = jnp.zeros_like(sums)
    for i in range(layers):
        fresh[i] = DECAY * row_state[i] + (1.0 - DECAY) * (rows[i, :4] / widths)
        stats[i : i + 1] = DECAY * col_state[i : i + 1] + (1.0 - DECAY) * (
            in_a_row(cols[i, :lanes]) / D
        )
        row_inverse = upright(lax.rsqrt(fresh[i]))
        col_inverse = lax.rsqrt(stats[i : i + 1])
        result = jnp.zeros((1, 128), F32)
        for m in range(4):
            update = scaled_update(grads, row_inverse, col_inverse, cuts, i, m)
            old = master[i, :, cuts[m] : cuts[m + 1]]
            for at, values in ((0, update), (4, old)):
                total = jnp.sum(
                    jnp.sum(values * values, axis=0, keepdims=True), axis=1, keepdims=True
                )
                result = jnp.where(lane == at + m, total, result)
        sums[i : i + 1] = result
        sums[layers + i : layers + i + 1] = cols[i, lanes : lanes + 1]


def update_kernel(cuts, grads, master, fresh, stats, sums, row_sums, new, new_low):
    layers = grads.shape[0]
    for i in range(layers):
        row_inverse = upright(lax.rsqrt(fresh[i]))
        col_inverse = lax.rsqrt(stats[i : i + 1])
        for m, width in enumerate((3.0 * D, 1.0 * D, 1.0 * FF, 1.0 * FF)):
            square_total = row_sums[layers + i : layers + i + 1, m : m + 1]
            state_total = row_sums[2 * layers + i : 2 * layers + i + 1, 4 + m : 5 + m]
            row_mean = (DECAY * state_total + (1.0 - DECAY) * (square_total / width)) / D
            update_rms = jnp.sqrt(row_mean * sums[i : i + 1, m : m + 1] / (D * width))
            weight_rms = jnp.sqrt(sums[i : i + 1, 4 + m : 5 + m] / (D * width))
            factor = RATE * weight_rms * jnp.sqrt(row_mean) / jnp.maximum(1.0, update_rms)
            columns = slice(cuts[m], cuts[m + 1])
            update = scaled_update(grads, row_inverse, col_inverse, cuts, i, m)
            value = master[i, :, columns] - factor * update
            new[i, :, columns] = value
            new_low[i, :, columns] = value.astype(BF16)


def whole_spec(shape):
    return pl.BlockSpec(shape, lambda *_: (0,) * len(shape))


def in_any(count):
    return [pl.BlockSpec(memory_space=pl.ANY)] * count


def far(arrays):
    return [pltpu.with_memory_space_constraint(array, pltpu.HBM) for array in arrays]


def cost(micros):
    return pl.CostEstimate(
        flops=int(micros * 10**9), bytes_accessed=int(micros * 10**6), transcendentals=0
    )


def chunk_specs(chunks):
    specs = []
    for array, place in chunks:
        if place is None:
            specs.append(whole_spec(array.shape))
        else:
            specs.append(
                pl.BlockSpec((None, *array.shape[1:]), lambda *_, place=place: (place, 0, 0, 0))
            )
    return specs


def rows_spec(rows, width, block_of):
    return pl.BlockSpec((rows, width), lambda t, *_: (block_of(t), 0))


def run_forward(place, chunks, vec, tables, weight, riders=()):
    blocks_out, sources = weight
    chunk = chunks[0][0].shape[-2]
    block, length = 2 * chunk, 4 * chunk
    counts = [len(pieces) for pieces, _ in sources]
    firsts = [first for _, first in sources]
    pieces = [piece for pieces, _ in sources for piece in pieces]
    count = len(pieces)
    out_wide = blocks_out[0].shape[0]
    heads = out_wide // HEAD_DIM
    wide = 3 * out_wide
    quarter = FF * out_wide // D

    def same(t):
        return t

    widths = [
        (D, BF16),
        (2 * out_wide, BF16),
        (out_wide, BF16),
        (out_wide, BF16),
        (quarter, BF16),
        (quarter, BF16),
    ]
    shapes = [pltpu.HBM((length, width), kind) for width, kind in widths]
    specs = [rows_spec(block, width, same) for width, _ in widths]
    shapes.insert(4, pltpu.HBM((8, length), F32))
    specs.insert(4, pl.BlockSpec((8, block), lambda t, *_: (0, t)))
    return pl.pallas_call(
        functools.partial(forward_kernel, counts, firsts),
        grid_spec=pltpu.PrefetchScalarGridSpec(
            num_scalar_prefetch=1,
            grid=(2,),
            in_specs=[
                *chunk_specs(chunks),
                whole_spec((8, D)),
                *[rows_spec(block, 2 * HEAD_DIM, same)] * 3,
                *[whole_spec((out_wide, out_wide))] * 4,
                *in_any(count + len(riders)),
            ],
            out_specs=[whole_spec((2, chunk, D))] * 2 + specs,
            scratch_shapes=[
                pltpu.VMEM((D, wide + out_wide), BF16),
                pltpu.VMEM((D, 2 * quarter), BF16),
                pltpu.VMEM((out_wide, D), BF16),
                pltpu.VMEM((heads, length, HEAD_DIM), BF16),
                pltpu.VMEM((heads, length, HEAD_DIM), BF16),
                pltpu.VMEM((block, D), F32),
                pltpu.SemaphoreType.DMA((count,)),
            ],
        ),
        out_shape=[
            pltpu.HBM((2, chunk, D), BF16),
            pltpu.HBM((2, chunk, D), BF16),
            *shapes,
        ],
        compiler_params=pltpu.CompilerParams(vmem_limit_bytes=VMEM_BYTES),
        cost_estimate=cost(13),
        name="layer_forward",
    )(place, *[array for array, _ in chunks], vec, *far(tables), *blocks_out, *far(pieces), *far(riders))


def run_mlp_backward(place, chunks, vec, weight, saved, split, riders=()):
    pieces, first = weight[1][1]
    sequences = len(chunks)
    chunk = chunks[0][0][0].shape[-2]
    block, length = 2 * chunk, 4 * chunk
    xhat, slope, att, hid = saved[0]
    quarter, out_wide = slope.shape[1], att.shape[1]
    n_blocks = D // out_wide

    def block_of(s):
        return lambda t: jnp.clip(t - 2 * s, 0, 1)

    def once(spec):
        return pl.BlockSpec(spec.block_shape, spec.index_map, pipeline_mode=pl.Buffered(1))

    arrays, in_specs = [], []
    for s in range(sequences):
        arrays += [array for array, _ in chunks[s]] + far(saved[s])
        in_specs += [once(spec) for spec in chunk_specs(chunks[s])]
        in_specs += [rows_spec(block, array.shape[1], block_of(s)) for array in saved[s]]
    shapes, specs = outer_outputs(split, 2 * quarter)
    out_shape, out_specs = [], []
    for s in range(sequences):
        out_shape += [
            pltpu.HBM((length, D), BF16),
            pltpu.HBM((length, quarter), BF16),
            pltpu.HBM((length, D), BF16),
            pltpu.HBM((8, D), F32),
        ]
        out_specs += [
            rows_spec(block, D, block_of(s)),
            rows_spec(block, quarter, block_of(s)),
            rows_spec(block, D, block_of(s)),
            whole_spec((8, D)),
        ]
    out_shape += [jax.ShapeDtypeStruct((out_wide, out_wide), BF16)] * n_blocks + shapes
    out_specs += [whole_spec((out_wide, out_wide))] * n_blocks + [once(spec) for spec in specs]
    results = pl.pallas_call(
        functools.partial(mlp_backward_kernel, len(pieces), first, sequences, len(shapes)),
        grid_spec=pltpu.PrefetchScalarGridSpec(
            num_scalar_prefetch=1,
            grid=(2 * sequences,),
            in_specs=[
                whole_spec((8, D)),
                *in_specs,
                *in_any(len(pieces) + len(riders)),
            ],
            out_specs=out_specs,
            scratch_shapes=[
                pltpu.VMEM((D, 2 * quarter), BF16),
                pltpu.VMEM((out_wide, D), F32),
                pltpu.VMEM((D, quarter), F32),
                pltpu.VMEM((D, quarter), F32),
                pltpu.SemaphoreType.DMA((len(pieces),)),
            ],
        ),
        out_shape=out_shape,
        compiler_params=pltpu.CompilerParams(vmem_limit_bytes=2 * VMEM_BYTES),
        cost_estimate=cost(20),
        name="mlp_backward",
    )(place, vec, *arrays, *far(pieces), *far(riders))
    each = [results[4 * s : 4 * s + 4] for s in range(sequences)]
    rest = results[4 * sequences :]
    return each, rest[:n_blocks], rest[n_blocks:]


def run_attention_backward(
    place, grad, vec, tables, weight, xhat, qk, val, lse, grad_two, riders=()
):
    blocks_out, ((pieces, first), _) = weight
    length = grad.shape[0]
    block, chunk = length // 2, length // 4
    out_wide = blocks_out[0].shape[0]
    heads = out_wide // HEAD_DIM
    wide = 3 * out_wide

    def turned(t):
        return 1 - t

    return pl.pallas_call(
        functools.partial(attention_backward_kernel, len(pieces), first),
        grid_spec=pltpu.PrefetchScalarGridSpec(
            num_scalar_prefetch=1,
            grid=(2,),
            in_specs=[
                rows_spec(block, D, turned),
                whole_spec((8, D)),
                *[rows_spec(block, 2 * HEAD_DIM, turned)] * 3,
                *[whole_spec((out_wide, out_wide))] * 4,
                rows_spec(block, D, turned),
                whole_spec(qk.shape),
                whole_spec(val.shape),
                pl.BlockSpec((8, block), lambda t, *_: (0, 1 - t)),
                rows_spec(block, D, turned),
                *in_any(len(pieces) + len(riders)),
            ],
            out_specs=[
                *[whole_spec((2, chunk, D))] * 2,
                rows_spec(block, wide, turned),
                whole_spec((8, D)),
            ],
            scratch_shapes=[
                pltpu.VMEM((D, wide + out_wide), BF16),
                pltpu.VMEM((out_wide, D), BF16),
                pltpu.VMEM((heads, block, HEAD_DIM), F32),
                pltpu.VMEM((heads, block, HEAD_DIM), F32),
                pltpu.VMEM((block, D), F32),
                pltpu.SemaphoreType.DMA((len(pieces),)),
            ],
        ),
        out_shape=[
            pltpu.HBM((2, chunk, D), BF16),
            pltpu.HBM((2, chunk, D), BF16),
            pltpu.HBM((length, wide), BF16),
            pltpu.HBM((8, D), F32),
        ],
        compiler_params=pltpu.CompilerParams(vmem_limit_bytes=VMEM_BYTES),
        cost_estimate=cost(11),
        name="attention_backward",
    )(
        place,
        *far([grad]),
        vec,
        *far(tables),
        *blocks_out,
        *far([xhat, qk, val, lse, grad_two, *pieces, *riders]),
    )


def outer_outputs(split, columns):
    if split:
        shape = (4, D // 8, columns)
        kinds = [BF16, BF16]
    else:
        shape, kinds = (D, columns), [BF16]
    return [pltpu.HBM(shape, kind) for kind in kinds], [whole_spec(shape)] * len(kinds)


def run_qkv_outer(scalars, vec, groups, outward, split, riders=()):
    arrays = [array for both in zip(*groups) for array in both]
    out_wide = outward[0].shape[1]
    shapes, specs = outer_outputs(split, groups[1][0].shape[1] + out_wide)
    return pl.pallas_call(
        functools.partial(qkv_outer_kernel, len(groups[0]), len(outward), len(shapes)),
        grid_spec=pltpu.PrefetchScalarGridSpec(
            num_scalar_prefetch=1,
            grid=(1,),
            in_specs=[
                whole_spec((8, D)),
                *in_any(len(arrays)),
                *[whole_spec(block.shape) for block in outward],
                *in_any(len(riders)),
            ],
            out_specs=specs,
            scratch_shapes=[
                *[pltpu.VMEM(array.shape, BF16) for array in arrays],
                pltpu.VMEM((D, out_wide), BF16),
                pltpu.SemaphoreType.DMA((len(arrays),)),
            ],
        ),
        out_shape=shapes,
        compiler_params=pltpu.CompilerParams(vmem_limit_bytes=VMEM_BYTES),
        cost_estimate=cost(6),
        name="qkv_outer",
    )(scalars, vec, *far(arrays), *outward, *far(riders))


def run_gradient(sources, row_state, layer, shape, earlier=(), riders=()):
    layers, rows, width = shape
    arrays = [array for source in sources for array in source]
    shapes = [shape, (layers, 8, rows), (layers, 8 * -(-(width // 128 + 1) // 8), 128)]

    def of_layer(shape):
        return pl.BlockSpec((1, *shape[1:]), lambda *_: (layer, 0, 0))

    return pl.pallas_call(
        functools.partial(
            gradient_kernel, [len(source) for source in sources], matrix_cuts(width)
        ),
        grid=(1,),
        in_specs=[
            *[whole_spec(array.shape) for array in arrays],
            of_layer(row_state.shape),
            *in_any(len(earlier) + len(riders)),
        ],
        out_specs=[of_layer(shape) for shape in shapes],
        out_shape=[jax.ShapeDtypeStruct(shape, F32) for shape in shapes],
        input_output_aliases={len(arrays) + 1 + k: k for k in range(len(earlier))},
        compiler_params=pltpu.CompilerParams(vmem_limit_bytes=VMEM_BYTES),
        cost_estimate=cost(2),
        name="gradient",
    )(*arrays, row_state, *earlier, *riders)


def run_whole(kernel, arrays, shapes, name):
    return pl.pallas_call(
        functools.partial(kernel, matrix_cuts(arrays[0].shape[2])),
        grid=(1,),
        in_specs=[whole_spec(array.shape) for array in arrays],
        out_specs=[whole_spec(shape) for shape, _ in shapes],
        out_shape=[jax.ShapeDtypeStruct(shape, kind) for shape, kind in shapes],
        compiler_params=pltpu.CompilerParams(vmem_limit_bytes=VMEM_BYTES),
        cost_estimate=cost(2),
        name=name,
    )(*arrays)


def example_kernel(layers, sequences, scalars, *refs):
    out = refs[-1]
    out[...] = jnp.zeros_like(out)
    seq_place = scalars[0]
    mine = jnp.where(seq_place == 0, 1.0, 0.0)
    for s in range(sequences):
        for i in range(layers):
            of_mlp, of_attention = refs[2 * (i * sequences + s) : 2 * (i * sequences + s) + 2]
            at = s * layers + i
            out[at, 0:2] = of_attention[0:2]
            out[at, 2:4] = of_mlp[0:2]
            out[at, 4:5] = of_mlp[3:4] * mine
            out[at, pl.ds(5 + seq_place, 1)] = of_mlp[2:3]
            wide = 3 * D * D // FF
            out[at, pl.ds(5 + FF // D + seq_place, 1), :wide] = of_attention[2:3, :wide]


def run_example(scalars, sums, sequences):
    arrays = [array for layer in sums for pair in layer for array in pair]
    shape = (sequences * len(sums), 16, D)
    return pl.pallas_call(
        functools.partial(example_kernel, len(sums), sequences),
        grid_spec=pltpu.PrefetchScalarGridSpec(
            num_scalar_prefetch=1,
            grid=(1,),
            in_specs=[whole_spec(array.shape) for array in arrays],
            out_specs=whole_spec(shape),
        ),
        out_shape=jax.ShapeDtypeStruct(shape, F32),
        cost_estimate=cost(1),
        name="examples",
    )(scalars, *arrays)


def example_vector(rows):
    groups = FF // D
    wide = 3 * D // groups
    qkv = [
        part for k in range(groups) for part in natural_heads(rows[5 + groups + k : 6 + groups + k, :wide])
    ]
    up = [rows[5 + k : 6 + k] for k in range(groups)]
    return jnp.concatenate(
        [*[rows[k : k + 1] for k in range(4)], *qkv, rows[4:5], *up, rows[4:5]], axis=1
    )


def small_kernel(length, totals, examples, state, params, grads, moments, new, scores):
    layers = state.shape[0]
    sequences = scores.shape[0]
    lane = lax.broadcasted_iota(jnp.int32, (1, scores.shape[1]), 1)
    row = lax.broadcasted_iota(jnp.int32, totals.shape[1:], 0)
    weight = jnp.where(row == 4, 2.0, 1.0)

    def product(left, right):
        value = jnp.sum(left * right * weight, axis=1, keepdims=True)
        return jnp.sum(value, axis=0, keepdims=True)

    query = [totals[layers + i] for i in range(layers)]
    mean = sum(product(rows, rows) for rows in query) / (layers * SMALL)
    spread = length * layers * SMALL * (mean + 1e-06)
    for s in range(sequences):
        each = [examples[s * layers + i] for i in range(layers)]
        norm = sum(product(rows, rows) for rows in each) / (layers * SMALL * length)
        influence = sum(product(*pair) for pair in zip(each, query)) / jnp.sqrt(spread)
        scores[s : s + 1] = jnp.where(lane == 0, norm, influence)
    edges = [0, D, 2 * D, 3 * D, 4 * D, 7 * D, 8 * D, 8 * D + FF, SMALL]
    for i in range(layers):
        place = slice(i, i + 1)
        gradient = example_vector(totals[i])
        grads[place] = gradient
        moment = DECAY * state[place] + (1.0 - DECAY) * (gradient * gradient + EPS_SQUARE)
        moments[place] = moment
        for first, end in zip(edges, edges[1:]):
            columns = slice(first, end)
            update = gradient[:, columns] * lax.rsqrt(moment[:, columns])
            old = params[place, columns]
            rms = jnp.sqrt(jnp.mean(update * update, axis=1, keepdims=True))
            old_rms = jnp.sqrt(jnp.mean(old * old, axis=1, keepdims=True))
            new[place, columns] = old - RATE * old_rms * (update / jnp.maximum(1.0, rms))


def run_small(length, totals, examples, state, params, sequences):
    arrays = [totals, examples, state, params]
    shapes = [state.shape] * 3 + [(sequences, 128)]
    return pl.pallas_call(
        functools.partial(small_kernel, length),
        grid=(1,),
        in_specs=[whole_spec(array.shape) for array in arrays],
        out_specs=[whole_spec(shape) for shape in shapes],
        out_shape=[jax.ShapeDtypeStruct(shape, F32) for shape in shapes],
        cost_estimate=cost(2),
        name="small_vectors",
    )(*arrays)


def half_spec(array, place, flipped=False):
    def index(h):
        half = 1 - h if flipped else h
        return (half, 0, 0) if place is None else (place, half, 0, 0)

    block = (None, *array.shape[-2:])
    return pl.BlockSpec(block if place is None else (None, *block), index)


def run_finish(kernel, sums, received, others, bias, name):
    keep, near, _ = sums
    shape = keep.shape
    arrays = [(keep, None), (near, None), (received, None), *others]
    specs = [half_spec(array, place, k == 2) for k, (array, place) in enumerate(arrays)]
    return pl.pallas_call(
        kernel,
        grid=(2,),
        in_specs=specs + ([] if bias is None else [whole_spec(bias.shape)]),
        out_specs=[half_spec(keep, None)] * 2,
        out_shape=[pltpu.HBM(shape, F32), jax.ShapeDtypeStruct(shape, BF16)],
        compiler_params=pltpu.CompilerParams(vmem_limit_bytes=VMEM_BYTES),
        cost_estimate=cost(2),
        name=name,
    )(*far([array for array, _ in arrays]), *([] if bias is None else [bias]))


def last_kernel(kernel, count, n_inputs, *refs):
    out = refs[-1]
    bias = refs[count * n_inputs : -1]
    for s in range(count):
        kernel(*refs[n_inputs * s : n_inputs * (s + 1)], *bias, out.at[s])


def run_last(kernel, sums, received, others, bias, kind, name):
    arrays, specs = [], []
    for (keep, near, _), across, more in zip(sums, received, others):
        chunk = keep.shape[-2]
        arrays += [keep, near, across]
        half = pl.BlockSpec((None, chunk, D), lambda i: (0, 0, 0))
        specs += [half, half, whole_spec(across.shape)]
        for array, place in more:
            arrays.append(array)
            if place is None:
                specs.append(half)
            else:
                specs.append(
                    pl.BlockSpec((None, None, chunk, D), lambda i, place=place: (place, 0, 0, 0))
                )
    count = len(sums)
    return pl.pallas_call(
        functools.partial(last_kernel, kernel, count, len(arrays) // count),
        grid=(1,),
        in_specs=specs + ([] if bias is None else [whole_spec(bias.shape)]),
        out_specs=whole_spec((count, chunk, D)),
        out_shape=jax.ShapeDtypeStruct((count, chunk, D), kind),
        compiler_params=pltpu.CompilerParams(vmem_limit_bytes=VMEM_BYTES),
        cost_estimate=cost(2),
        name=name,
    )(*far(arrays), *([] if bias is None else [bias]))


def pass_through_kernel(*refs):
    del refs


def after(values, *others):
    return pl.pallas_call(
        pass_through_kernel,
        in_specs=in_any(1 + len(others)),
        out_specs=pl.BlockSpec(memory_space=pl.ANY),
        out_shape=jax.ShapeDtypeStruct(values.shape, values.dtype),
        input_output_aliases={0: 0},
        name="after",
    )(values, *others)


def out_blocks(columns, dp_place, seq_place):
    stacked = jnp.zeros((D, columns[0].shape[1]), BF16)
    for column, place in zip(columns, piece_places(len(columns), dp_place)):
        stacked = lax.dynamic_update_slice(stacked, column, (place * column.shape[0], 0))
    size = lax.axis_size("seq")
    return exchange_blocks(stacked.reshape(size, D // size, -1), seq_place)


def on_device(block_in, cotangent, labels, master, small_params, row_state, col_state, small_state):
    sequences, chunk = block_in.shape[:2]
    group_count = lax.axis_size("seq")
    seq_place, dp_place = lax.axis_index("seq"), lax.axis_index("dp")
    length = chunk * group_count
    flags = (labels == 0).astype(jnp.int32)
    place = jnp.concatenate(
        [jnp.stack([seq_place % 2, seq_place // 2, dp_place]).astype(jnp.int32), flags]
    )
    train_flag = flags.astype(F32)
    scalars = jnp.concatenate(
        [jnp.stack([dp_place % 2, seq_place]).astype(jnp.int32), flags]
    )
    query_flag = 1.0 - train_flag
    wide, out_wide, quarter = 3 * D // group_count, D // group_count, FF // group_count
    cuts = matrix_cuts(master.shape[2])
    split = lax.axis_size("dp") == 8
    x_bit, z_place = dp_place % 2, dp_place // 2
    tables = rotary_tables(length)

    def normalise(stream):
        scaled, inverse = apply_layer_norm(stream)
        low_scaled = scaled.astype(BF16)
        return (scaled, inverse), low_scaled

    stream = both_halves(block_in)
    _, low_scaled = normalise(stream.astype(F32))
    near = swap(low_scaled, "seq", 1)
    chunks = [((low_scaled, s), (near, s)) for s in range(sequences)]

    low = master.astype(BF16)
    rows_of = [
        jnp.concatenate([heads_together(low[i, :, : cuts[1]]), low[i, :, cuts[1] :]], axis=1)
        for i in range(LAYERS)
    ]
    pieces = gather_rows(rows_of[0])
    whole_one = lax.all_gather(after(rows_of[1], *pieces[4:5]), "dp", axis=0, tiled=True)

    def weight_of(pieces):
        columns = [piece[:, wide : wide + out_wide] for piece in pieces]
        return out_blocks(columns, dp_place, seq_place), [(pieces, 0), (pieces, cuts[2])]

    weights = [weight_of(pieces)]
    vectors, params = [], []
    for i in range(LAYERS):
        param = unpack(small_params[i])
        params.append(param)
        bias_qkv = heads_together(lax.dynamic_slice_in_dim(param[4], seq_place * wide, wide))
        bias_up = lax.dynamic_slice_in_dim(param[6], seq_place * quarter, quarter)
        vectors.append(
            jnp.stack(
                [
                    *param[:4],
                    jnp.pad(bias_up, (0, D - quarter)),
                    jnp.pad(bias_qkv, (0, D - wide)),
                    jnp.zeros((D,), F32),
                    jnp.zeros((D,), F32),
                ]
            )
        )

    streams = [[(stream, s) for s in range(sequences)]]
    saved_all = []
    open_sum = None

    def close_sum(behind):
        nonlocal open_sum
        sums, received, finish = open_sum
        open_sum = None
        finish(sums, after(received, behind))

    def open_exchange(keep, send, behind, finish):
        nonlocal open_sum
        if open_sum is not None:
            send = after(send, open_sum[1])
            close_sum(behind)
        sums = core_sum(keep, send)
        open_sum = (sums, swap(sums[2], "seq", 2), finish)
        return [sums[2]]

    def own_exchange(keep, send):
        near = swap(send, "seq", 1)
        low = (keep[1].astype(F32) + near[1].astype(F32)).astype(BF16)
        return (keep, near, None), swap(low, "seq", 2)

    both_grads = both_halves(cotangent)
    near_grads = swap(both_grads, "seq", 1)
    riders = []
    for i in range(LAYERS):
        last = i == LAYERS - 1
        saved_all.append([])
        next_chunks, next_streams, ends = [], [], []
        bias = (params[i][5] + params[i][7])[None]

        def finish_stream(s, old, bias, next_chunks, next_streams, sums, received):
            fresh, low = run_finish(
                finish_stream_kernel, sums, received, [old], bias, "finish_stream"
            )
            next_streams.append((fresh, None))
            next_chunks.append(((low, None), (swap(low, "seq", 1), None)))

        for s in range(sequences):
            keep, send, *saved = run_forward(
                place, chunks[s], vectors[i], tables, weights[i], riders
            )
            saved_all[i].append(saved)
            if last:
                if open_sum is not None:
                    send = after(send, open_sum[1])
                    close_sum(saved[0])
                ends.append(own_exchange(keep, send))
                continue
            riders = open_exchange(
                keep,
                send,
                saved[0],
                functools.partial(
                    finish_stream, s, streams[i][s], bias, next_chunks, next_streams
                ),
            )
            if i == 0:
                riders = riders + [near_grads]
        if i == 0:
            whole_one = after(whole_one, saved_all[0][0][0])
            weights.append(weight_of([whole_one]))
        if last:
            break
        chunks = next_chunks
        streams.append(next_streams)
    block_out = run_last(
        finish_stream_kernel,
        [sums for sums, _ in ends],
        [received for _, received in ends],
        [[old] for old in streams[-1]],
        bias,
        BF16,
        "block_out",
    )

    grads = [(both_grads, s) for s in range(sequences)]
    chunks = [((both_grads, s), (near_grads, s)) for s in range(sequences)]
    sources, sums = [None] * LAYERS, [None] * LAYERS
    riders, later, latest = [], [], []
    for i in reversed(range(LAYERS)):
        last = i == 0
        xhats, qks, vals, atts, lses, hids, slopes = zip(*saved_all[i])
        mlp, attention, next_chunks, next_grads, ends = [], [], [], [], []

        def finish_grad(s, others, next_chunks, next_grads, sums, received):
            fresh, low = run_finish(
                finish_grad_kernel, sums, received, others, None, "finish_grad"
            )
            next_grads.append((fresh, None))
            next_chunks.append(((low, None), (swap(low, "seq", 1), None)))

        if open_sum is not None:
            close_sum(riders[0])
        mlp, outward, both = run_mlp_backward(
            place,
            chunks,
            vectors[i],
            weights[i],
            list(zip(xhats, slopes, atts, hids)),
            split,
            [*riders, *later],
        )
        outward = [
            block if k == 0 else swap(block, "seq", k) for k, block in enumerate(outward)
        ]
        riders = [both[-1], *latest] if last else [both[-1], block_out]
        for s in range(sequences):
            keep, send, grad_joined, sums_t = run_attention_backward(
                place,
                mlp[s][0],
                vectors[i],
                tables,
                weights[i],
                xhats[s],
                qks[s],
                vals[s],
                lses[s],
                mlp[s][2],
                riders,
            )
            attention.append((grad_joined, sums_t))
            if last:
                riders = []
                ends.append(own_exchange(keep, send))
            else:
                riders = open_exchange(
                    keep,
                    send,
                    grad_joined,
                    functools.partial(
                        finish_grad, s, [grads[s], streams[i][s]], next_chunks, next_grads
                    ),
                )
                if s == 0:
                    riders = riders + outward
        if split and not last:
            total_b = pair_total(*both)
            part_b = scatter_along_z(total_b)
        if split and last:
            total_b = pair_total(after(both[0], *[out[0] for out in attention]), both[1])
            part_b = scatter_along_z(total_b)
            riders = [total_b]
        elif not split:
            part_b = lax.psum_scatter(both[0], "dp", scatter_dimension=0, tiled=True)
        groups = [xhats, [out[0] for out in attention]]
        rest = run_qkv_outer(scalars, vectors[i], groups, outward, split, riders)
        if not split:
            part_a = [lax.psum_scatter(rest[0], "dp", scatter_dimension=0, tiled=True)]
        elif last:
            own_a, parts_a = pair_sum(after(rest[0], part_b), rest[1], z_place)
            part_a = [own_a, *exchange_parts(parts_a)]
        else:
            total_a = pair_total(*rest)
            part_a = [scatter_along_z(total_a)]
            later, latest = [total_b], [total_a]
        sources[i] = [[part_b], part_a]
        riders = rest[:1]
        chunks = next_chunks
        grads = next_grads or grads
        sums[i] = [(out[3], other[1]) for out, other in zip(mlp, attention)]
    behind_a = parts_a[:1] if split else rest
    grad_stream = run_last(
        finish_grad_kernel,
        [sums_of for sums_of, _ in ends],
        [after(received, *behind_a) for _, received in ends],
        [[grad, old] for grad, old in zip(grads, streams[0])],
        None,
        F32,
        "input_grad",
    )

    examples = after(run_example(scalars[1:2], sums, sequences), *behind_a)
    examples = sum_pairwise(examples, "seq", BF16)
    stacked = ()
    for i in reversed(range(LAYERS)):
        behind = [] if i else [examples, grad_stream]
        stacked = run_gradient(sources[i], row_state, i, master.shape, stacked, behind)
    reduced_all, row_part, col_part = stacked
    dp_bits, seq_bits = [], []
    for axis, bits in (("dp", dp_bits), ("seq", seq_bits)):
        bits += [(axis, 1 << k) for k in range(lax.axis_size(axis).bit_length() - 1)]
    first_steps = max(len(seq_bits), len(dp_bits))
    flat = examples.reshape(sequences, -1)
    small = jnp.stack(
        [
            jnp.sum(train_flag[:, None] * flat, axis=0),
            jnp.sum((1.0 - train_flag)[:, None] * flat, axis=0),
        ]
    ).reshape(2 * LAYERS, *examples.shape[1:])
    small_steps = list(dp_bits)

    def small_step():
        nonlocal small_steps
        step, *small_steps = small_steps
        sent = small.astype(BF16)
        return sent, swap(sent, *step)

    def together(values):
        nonlocal small
        received = [swap(value, *step) for value, step in values]
        sent = None
        if small_steps:
            sent, small_in = small_step()
            received.append(small_in)
        if len(received) > 1:
            received = [
                after(value, *[other for other in received if other is not value])
                for value in received
            ]
        if sent is not None:
            small = sent.astype(F32) + received.pop().astype(F32)
        return [value + other for (value, _), other in zip(values, received)]

    for k in range(first_steps):
        now = []
        if k < len(seq_bits):
            now.append((row_part, seq_bits[k]))
        if k < len(dp_bits):
            now.append((col_part, dp_bits[k]))
        *rest_sums, last_sum = together(now)
        if k < len(seq_bits) and k < len(dp_bits):
            (row_part,), col_part = rest_sums, last_sum
        elif k < len(dp_bits):
            col_part = last_sum
        else:
            row_part = last_sum
    layers = master.shape[0]
    fresh_row_moments, col_stats, local_sums = run_whole(
        square_kernel,
        [reduced_all, master, row_part, col_part, row_state, col_state],
        [(row_state.shape, F32), (col_state.shape, F32), ((8, 128), F32)],
        "squares",
    )
    state_sums = local_sums
    for step in seq_bits:
        (local_sums,) = together([(local_sums, step)])
    seq_sums = jnp.concatenate(
        [local_sums[: 2 * layers], state_sums[layers : 2 * layers], local_sums[3 * layers :]], axis=0
    )
    for step in dp_bits:
        (local_sums,) = together([(local_sums, step)])
    while small_steps:
        together([])
    small_grads, small_moments, small_new, scores = run_small(
        length, small, examples, small_state, small_params, sequences
    )
    example_norms, influence = scores[:, 0], scores[:, 1]
    new_master, new_low = run_whole(
        update_kernel,
        [reduced_all, master, fresh_row_moments, col_stats, local_sums, seq_sums],
        [(master.shape, F32), (master.shape, BF16)],
        "update",
    )
    return (
        block_out,
        grad_stream,
        example_norms,
        influence,
        reduced_all,
        fresh_row_moments,
        col_stats,
        new_master,
        new_low,
        small_grads,
        small_moments,
        small_new,
    )


def solution(mesh):
    placed = (
        P("dp", "seq", None),
        P("dp", "seq", None),
        P("dp"),
        P(None, "dp", "seq"),
        P(),
        P(None, None, "dp"),
        P(None, "seq"),
        P(),
    )
    return jax.shard_map(
        on_device,
        mesh=mesh,
        in_specs=placed,
        out_specs=(
            P("dp", "seq", None),
            P("dp", "seq", None),
            P("dp"),
            P("dp"),
            P(None, "dp", "seq"),
            P(None, None, "dp"),
            P(None, "seq"),
            P(None, "dp", "seq"),
            P(None, "dp", "seq"),
            P(),
            P(),
            P(),
        ),
        check_vma=False,
    )
```
